32 devices in a mesh: dp: 4 (over y, x), vocab: 8 (over z, core).
Axes of the slice: x: 2, y: 2, z: 4, core: 2. Of those that a mesh axis runs over, the one named last changes fastest.
Arguments:
- hidden: bfloat16 [4096, 5120], P('dp', 'vocab'), may hold values from -6 to 6
- logit_grad: bfloat16 [4096, 384], P('dp', 'vocab'), may hold values from -0.3984375 to 0.3984375
- predict_mask: int32 [4096], P('dp'), may hold values 0 or 1
- slot_grads: bfloat16 [32, 8, 6, 5120], P(('dp', 'vocab')), may hold values from -6 to 6
- slot_rows: int32 [32, 8, 6], P(('dp', 'vocab')), may hold values from 0 to 47
- slot_counts: int32 [32, 8], P(('dp', 'vocab')), may hold values from 0 to 6, as said below
- master: float32 [384, 5120], P(('vocab', 'dp')), may hold values from -0.1 to 0.1
- first_moment: float32 [384, 5120], P(('vocab', 'dp')), may hold values from -2 to 2
- second_moment: float32 [384, 5120], P(('vocab', 'dp')), may hold values from 0.5 to 8
Outputs:
- master_new: float32 [384, 5120], P(('vocab', 'dp'))
- first_new: float32 [384, 5120], P(('vocab', 'dp'))
- second_new: float32 [384, 5120], P(('vocab', 'dp'))
- table_new: bfloat16 [384, 5120], P('vocab')
The draws below stay inside these ranges and needn't reach their ends.
Inputs may be any that keep to these rules, and one draw needn't show every extreme that they name: `slot_counts`: some owner receives 6 live slots from every sender, in every draw.
All inputs are finite; a program needn't handle non-finite values. No bound on the sum of `predict_mask` on one device may be relied on, other than what follows from the above.
Results may differ from the reference program's by a relative error of at most 0.0004.
Values may be sent and summed in bfloat16 or wider, within the bound.
No kernel may reach another device: no remote copies, remote signals or barrier semaphores. Data moves between devices by JAX's collectives and lax.ppermute only.
A program may use at most 64 MiB of HBM per device.

```python
import math
import jax
import jax.numpy as jnp
import numpy as np
from jax import lax

D = 5120
CAP = 6
STEP = 8
ROWS_V = 48
W_ROWS = 384
TOKENS_H = 4096
SENDERS = 32
OWNERS = 8


def draw_slot_counts(key, part):
    first_key, second_key = jax.random.split(jax.random.fold_in(key, 11))
    counts = jax.random.randint(first_key, (SENDERS, OWNERS), 0, CAP + 1)
    chosen = jax.random.randint(second_key, (), 0, OWNERS)
    owner_index = jnp.arange(OWNERS)[None, :]
    return jnp.where(owner_index == chosen, CAP, counts).astype(jnp.int32)


def with_ends(result, key, low, largest):
    longest = result.shape.index(max(result.shape))
    spots = []
    for shift in (0, 1):
        where = [jax.random.randint(jax.random.fold_in(key, axis), (), 0, length) for axis, length in enumerate(result.shape)]
        where[longest] = (where[longest] + shift) % result.shape[longest]
        spots.append(tuple(where))
    return result.at[spots[0]].set(low).at[spots[1]].set(largest)


def raised(drawn, own_key, source, target, shards_of, factor):
    def block_of(dim):
        return (jnp.arange(drawn.shape[dim]) // (drawn.shape[dim] // shards_of)).reshape((-1,) + (1,) * (drawn.ndim - 1 - dim))

    one_side = jax.random.permutation(own_key, shards_of)[block_of(target)]
    second = (block_of(target) + shards_of // 2) % shards_of
    return jnp.where((block_of(source) == one_side) | (block_of(source) == second), factor * drawn, drawn)


def steps_of(stream_key, dims, cuts, low, largest):
    loudness = 1.0
    for axis_at, shards_of in cuts:
        draws = jax.random.uniform(jax.random.fold_in(jax.random.fold_in(stream_key, 6), axis_at), (shards_of,), jnp.float32, low / len(cuts), largest / len(cuts))
        loudness = loudness * jnp.repeat(jnp.exp(draws), dims[axis_at] // shards_of).reshape((-1,) + (1,) * (len(dims) - 1 - axis_at))
    return loudness


def rank_bounds(number_of, skew):
    loads = [(1 << 20) // math.isqrt(rank ** skew) + 1 for rank in range(1, number_of + 1)]
    scale = 1 + sum(loads) // (1 << 30)
    return np.cumsum(np.array([max(1, weight // scale) for weight in loads]))


def ranked_ids(key, extent, number_of, skew):
    listing = rank_bounds(number_of, skew)
    lot = jax.random.randint(jax.random.fold_in(key, 1), extent, 0, int(listing[number_of - 1]))
    grade = jnp.searchsorted(jnp.asarray(listing, jnp.int32), lot, side="right")
    return jax.random.permutation(jax.random.fold_in(key, 2), number_of)[grade].astype(jnp.int32)


def noise(rng, shape, deviation, bound, pieces=(), kind=jnp.bfloat16):
    loudness = steps_of(rng, shape, pieces, -0.22, 0.18) if pieces else 1.0
    array = jax.random.normal(rng, shape, jnp.float32) * deviation * loudness
    return jnp.minimum(jnp.maximum(array, -bound), bound).astype(kind)


def bell_draw_with(stream_key, shape, width, limit, pieces, heavy, kind=jnp.bfloat16):
    result = width * jax.random.normal(stream_key, shape, jnp.float32)
    if pieces:
        result = result * steps_of(stream_key, shape, pieces, -0.22, 0.18)
    return jnp.clip(raised(result, jax.random.fold_in(stream_key, 3), *heavy), -limit, limit).astype(kind)


def setup_inputs(seed: int = 0) -> dict:
    arg_keys = jax.random.split(jax.random.key(seed), 10)
    return {
        "hidden": noise(arg_keys[0], (TOKENS_H, D), 1.0, 6.0, ((0, 4), (1, 8))),
        "logit_grad": bell_draw_with(arg_keys[1], (TOKENS_H, W_ROWS), 0.05, 0.3984375, ((0, 4), (1, 8)), (0, 1, 8, 2.0)),
        "predict_mask": with_ends((jax.random.randint(arg_keys[2], (TOKENS_H,), 0, 4) < 3).astype(jnp.int32), jax.random.fold_in(arg_keys[2], 1), 0, 1),
        "slot_grads": noise(arg_keys[3], (SENDERS, OWNERS, CAP, D), 1.0, 6.0, ((0, 32),)),
        "slot_rows": with_ends(ranked_ids(arg_keys[4], (SENDERS, OWNERS, CAP), ROWS_V, 2), jax.random.fold_in(arg_keys[4], 3), 0, ROWS_V - 1).astype(jnp.int32),
        "slot_counts": draw_slot_counts(jax.random.fold_in(arg_keys[9], 71), 0),
        "master": noise(arg_keys[6], (W_ROWS, D), 0.02, 0.1, ((0, 32),), jnp.float32),
        "first_moment": noise(arg_keys[7], (W_ROWS, D), 0.3, 2.0, ((0, 32),), jnp.float32),
        "second_moment": jnp.clip(jnp.exp(math.log(8.0) - 2.7725887 * jax.random.uniform(arg_keys[8], (W_ROWS, D), jnp.float32) ** steps_of(arg_keys[8], (W_ROWS, D), ((0, 32),), -0.2, 0.2)), 0.5, 8.0),
    }


def reference(hidden, logit_grad, predict_mask, slot_grads, slot_rows, slot_counts, master, first_moment, second_moment):
    masked = logit_grad * predict_mask.astype(jnp.bfloat16)[:, None]
    head_grad = lax.dot_general(masked, hidden, (((0,), (0,)), ((), ())), preferred_element_type=jnp.float32)
    owner_base = (jnp.arange(OWNERS, dtype=jnp.int32) * ROWS_V)[:, None]
    slot_index = jnp.arange(CAP, dtype=jnp.int32)[None, :]

    def add_sender(carried, inputs):
        grads, rows_local, counts = inputs
        alive_slot = (slot_index < counts[:, None]).astype(jnp.float32)
        values = grads.astype(jnp.float32) * alive_slot[:, :, None]
        targets = (rows_local + owner_base).astype(jnp.int32).reshape(-1)
        carried = carried.at[targets].add(values.reshape(-1, values.shape[-1]))
        return (carried, None)
    start_grad = jnp.zeros((W_ROWS, hidden.shape[1]), jnp.float32)
    embed_grad, unused = lax.scan(add_sender, start_grad, (slot_grads, slot_rows, slot_counts))
    gradient = head_grad + embed_grad
    first_new = 0.9 * first_moment + 0.1 * gradient
    second_new = 0.95 * second_moment + 0.05 * gradient * gradient
    first_hat = first_new / (1.0 - 0.9 ** STEP)
    second_hat = second_new / (1.0 - 0.95 ** STEP)
    master_new = master - 0.05 * (first_hat / (jnp.sqrt(second_hat) + 1e-08) + 0.1 * master)
    table_new = master_new.astype(jnp.bfloat16)
    return (master_new, first_new, second_new, table_new)
```

```python
import jax
import jax.numpy as jnp
from jax import lax
from jax.sharding import PartitionSpec as P

STEP = 8


def local(
    hidden,
    logit_grad,
    predict_mask,
    slot_grads,
    slot_rows,
    slot_counts,
    master,
    first_moment,
    second_moment,
):
    vocab = lax.axis_size("vocab")
    dp = lax.axis_size("dp")
    rows = logit_grad.shape[1]
    shard = master.shape[0]
    cols = hidden.shape[1]
    owners, cap, width = slot_grads.shape[1:]
    masked = (logit_grad * predict_mask.astype(jnp.bfloat16)[:, None]).T
    masked_all = lax.all_gather(masked, "vocab", axis=0, tiled=True)
    slot_index = jnp.arange(cap, dtype=jnp.int32)[None, :]
    ids = jnp.where(slot_index < slot_counts[0][:, None], slot_rows[0], -1)
    ids_all = lax.all_gather(ids, "vocab", axis=0, tiled=False)
    outgoing = slot_grads.reshape(owners * cap, vocab, cols).transpose(1, 0, 2)
    arrived = lax.all_to_all(outgoing, "vocab", split_axis=0, concat_axis=0, tiled=True)
    arrived = arrived.reshape(vocab, owners, cap, cols).transpose(1, 0, 2, 3).reshape(owners, vocab * cap, cols)
    ids_all = ids_all.transpose(1, 0, 2).reshape(owners, 1, vocab * cap)
    picked = (jnp.arange(rows, dtype=jnp.int32)[None, :, None] == ids_all).astype(jnp.bfloat16)
    head = jnp.dot(masked_all, hidden, preferred_element_type=jnp.float32)
    embed = lax.dot_general(picked, arrived, (((2,), (1,)), ((0,), (0,))), preferred_element_type=jnp.float32)
    part = head.reshape(vocab, dp, shard, cols) + embed.reshape(vocab, dp, shard, cols)
    part = part.transpose(1, 0, 2, 3).reshape(dp, vocab * shard, cols)
    part = lax.all_to_all(part, "dp", split_axis=0, concat_axis=0, tiled=True)
    total = part.sum(axis=0).reshape(vocab, shard, cols)
    total = lax.all_to_all(total, "vocab", split_axis=0, concat_axis=0, tiled=True)
    gradient = total.transpose(1, 0, 2).reshape(shard, width)
    first_new = 0.9 * first_moment + 0.1 * gradient
    second_new = 0.95 * second_moment + 0.05 * gradient * gradient
    first_hat = first_new / (1.0 - 0.9**STEP)
    second_hat = second_new / (1.0 - 0.95**STEP)
    master_new = master - 0.05 * (first_hat / (jnp.sqrt(second_hat) + 1e-08) + 0.1 * master)
    table_new = lax.all_gather(master_new.astype(jnp.bfloat16), "dp", axis=0, tiled=True)
    return (master_new, first_new, second_new, table_new)


def solution(mesh):
    in_specs = (
        P("dp", "vocab"),
        P("dp", "vocab"),
        P("dp"),
        P(("dp", "vocab"), None, None, None),
        P(("dp", "vocab"), None, None),
        P(("dp", "vocab"), None),
        P(("vocab", "dp"), None),
        P(("vocab", "dp"), None),
        P(("vocab", "dp"), None),
    )
    out_specs = (
        P(("vocab", "dp"), None),
        P(("vocab", "dp"), None),
        P(("vocab", "dp"), None),
        P("vocab", None),
    )
    return jax.shard_map(local, mesh=mesh, in_specs=in_specs, out_specs=out_specs, check_vma=False)
```

```python
import jax
import jax.numpy as jnp
from jax import lax
from jax.sharding import PartitionSpec as P

STEP = 8
CORES = 2
LANES = 128


def local(
    hidden,
    logit_grad,
    predict_mask,
    slot_grads,
    slot_rows,
    slot_counts,
    master,
    first_moment,
    second_moment,
):
    vocab = lax.axis_size("vocab")
    dp = lax.axis_size("dp")
    chips = vocab // CORES
    rows = logit_grad.shape[1]
    shard = master.shape[0]
    cols = hidden.shape[1] * CORES
    owners, cap, width = slot_grads.shape[1:]
    here = lax.axis_index("vocab")
    core = here % CORES
    z = here // CORES
    d = lax.axis_index("dp")

    def to_core(x):
        return lax.ppermute(x, "vocab", [(v, v ^ 1) for v in range(vocab)])

    def to_chip(x, s):
        return lax.ppermute(x, "vocab", [(v, v ^ (s * CORES)) for v in range(vocab)])

    def to_dp(x, t):
        return lax.ppermute(x, "dp", [(i, i ^ t) for i in range(dp)])

    label = jnp.arange(rows, dtype=jnp.int32)
    source = ((label // shard) ^ d) * shard + label % shard
    reorder = (source[:, None] == label[None, :]).astype(jnp.bfloat16)
    masked = logit_grad * predict_mask.astype(jnp.bfloat16)[:, None]
    masked = lax.dot_general(reorder, masked, (((1,), (1,)), ((), ())), preferred_element_type=jnp.bfloat16)

    slot_index = jnp.arange(cap, dtype=jnp.int32)[None, :]
    ids = ((slot_rows[0] // shard) ^ d) * shard + slot_rows[0] % shard
    ids = jnp.where(slot_index < slot_counts[0][:, None], ids, -1).astype(jnp.bfloat16)
    ids = jnp.broadcast_to(ids[:, :, None, None], (owners, cap, chips, LANES))
    slots = slot_grads[0].reshape(owners, cap, chips, cols)
    slots = jnp.concatenate([slots, ids], axis=3).reshape(chips, CORES, cap, chips, cols + LANES)
    mine = lax.dynamic_index_in_dim(slots, core, 1, keepdims=False)
    other = lax.dynamic_index_in_dim(slots, 1 - core, 1, keepdims=False)
    hidden_other = to_core(hidden)
    other = to_core(other)
    masked = [masked] + [to_chip(masked, s) for s in range(1, chips)]
    both = jnp.stack([mine, other]).reshape(CORES * chips * cap, chips, cols + LANES)
    slots = [lax.dynamic_index_in_dim(both, z ^ s, 1, keepdims=False) for s in range(chips)]
    slots = [slots[0]] + [to_chip(slots[s], s) for s in range(1, chips)]

    swap = core == 1
    low = jnp.where(swap, hidden_other, hidden)
    high = jnp.where(swap, hidden, hidden_other)
    wide = jnp.concatenate([low, high], axis=1)
    slots = jnp.concatenate(slots, axis=0)
    owner = (jnp.arange(slots.shape[0], dtype=jnp.int32) // cap) % chips
    ids = slots[:, cols].astype(jnp.int32)
    ids = jnp.where(ids < 0, -1, (owner ^ z) * rows + ids)
    picked = (jnp.arange(chips * rows, dtype=jnp.int32)[:, None] == ids[None, :]).astype(jnp.bfloat16)
    part = jnp.dot(jnp.concatenate(masked, axis=0), wide, preferred_element_type=jnp.float32)
    part = part + jnp.dot(picked, slots[:, :cols], preferred_element_type=jnp.float32)
    part = part.reshape(chips, dp, shard, cols)
    part = [part[:, t].reshape(chips * shard, cols) for t in range(dp)]
    total = part[0]
    for t in range(1, dp):
        total = total + to_dp(part[t], t)
    total = total.reshape(chips, shard, CORES, cols // CORES).transpose(0, 2, 1, 3)
    total = total.reshape(chips, CORES * shard, cols // CORES)
    pieces = [total[0]] + [to_chip(total[s], s) for s in range(1, chips)]
    pieces = jnp.stack(pieces).reshape(chips, CORES, shard, cols // CORES).transpose(0, 2, 1, 3)
    pieces = pieces.reshape(chips, shard, cols)
    gradient = jnp.concatenate([lax.dynamic_index_in_dim(pieces, z ^ s, 0, keepdims=False) for s in range(chips)], axis=1)
    first_new = 0.9 * first_moment + 0.1 * gradient
    second_new = 0.95 * second_moment + 0.05 * gradient * gradient
    first_hat = first_new / (1.0 - 0.9**STEP)
    second_hat = second_new / (1.0 - 0.95**STEP)
    master_new = master - 0.05 * (first_hat / (jnp.sqrt(second_hat) + 1e-08) + 0.1 * master)
    table = master_new.astype(jnp.bfloat16)
    table = table.reshape(shard, chips, cols).transpose(1, 0, 2).reshape(chips * shard, cols)
    table = jnp.stack([table] + [to_dp(table, t) for t in range(1, dp)])
    table = jnp.stack([lax.dynamic_index_in_dim(table, d ^ t, 0, keepdims=False) for t in range(dp)])
    table = table.reshape(dp, chips, shard, cols).transpose(0, 2, 1, 3).reshape(rows, width)
    return (master_new, first_new, second_new, table)


def solution(mesh):
    in_specs = (
        P("dp", "vocab"),
        P("dp", "vocab"),
        P("dp"),
        P(("dp", "vocab"), None, None, None),
        P(("dp", "vocab"), None, None),
        P(("dp", "vocab"), None),
        P(("vocab", "dp"), None),
        P(("vocab", "dp"), None),
        P(("vocab", "dp"), None),
    )
    out_specs = (
        P(("vocab", "dp"), None),
        P(("vocab", "dp"), None),
        P(("vocab", "dp"), None),
        P("vocab", None),
    )
    return jax.shard_map(local, mesh=mesh, in_specs=in_specs, out_specs=out_specs, check_vma=False)
```

```python
import functools

import jax
import jax.numpy as jnp
from jax import lax
from jax.experimental import pallas as pl
from jax.experimental.pallas import tpu as pltpu
from jax.sharding import PartitionSpec as P

STEP = 8
CORES = 2
LANES = 128
VMEM_LIMIT = 24 * 1024 * 1024


def place():
    here = lax.axis_index("vocab")
    return lax.axis_index("dp"), lax.shift_right_logical(here, 1), here & 1


def iota(shape, axis):
    return lax.broadcasted_iota(jnp.int32, shape, axis)


def over(x, n):
    return ((x.astype(jnp.float32) + 0.5) * (1.0 / n)).astype(jnp.int32)


def one_hot(flag):
    return jnp.where(flag, 1.0, 0.0).astype(jnp.bfloat16)


def exact(left, right):
    return jnp.dot(left, right, preferred_element_type=jnp.float32)


def slots_kernel(chips, dp, shard, slots_ref, rows_ref, counts_ref, *out_refs):
    d, z, core = place()
    cap, owners = rows_ref.shape[0], rows_ref.shape[2]
    count = cap * owners
    group = cap * chips
    width = slots_ref.shape[1] // chips
    own_lane = iota((count, owners), 1) == iota((count, owners), 0) % owners
    rows = jnp.broadcast_to(rows_ref[...], (cap, owners, owners)).reshape(count, owners)
    rows = jnp.sum(jnp.where(own_lane, rows, 0), axis=1, keepdims=True)
    live = jnp.broadcast_to(counts_ref[...], (count, owners))
    live = jnp.sum(jnp.where(own_lane, live, 0), axis=1, keepdims=True)
    block = over(rows, shard)
    ids = (block ^ d) * shard + rows - block * shard
    ids = jnp.where(over(iota((count, 1), 0), owners) < live, ids, -1)
    ids = jnp.broadcast_to(ids, (count, LANES)).astype(jnp.bfloat16)
    for away in range(CORES):
        q = iota((group, count), 0)
        slot = over(q, chips)
        wanted = slot * owners + (q - slot * chips) * CORES + (core ^ away)
        pick = one_hot(iota((group, count), 1) == wanted)
        picked_ids = exact(pick, ids).astype(jnp.bfloat16)
        for s in range(chips):
            start = pl.multiple_of((z ^ s) * width, LANES)
            out_ref = out_refs[away * chips + s]
            out_ref[:, :width] = exact(pick, slots_ref[:, pl.ds(start, width)]).astype(jnp.bfloat16)
            out_ref[:, width:] = picked_ids


def head_kernel(chips, dp, shard, mask_ref, own_ref, other_ref, *refs):
    d, z, core = place()
    parts, out_ref = refs[:-1], refs[-1]
    rows = dp * shard
    total = chips * rows
    cols = own_ref.shape[1]
    mask = mask_ref[...].astype(jnp.float32).astype(jnp.bfloat16)
    columns = jnp.concatenate([part[...] for part in parts], axis=0) * mask
    r = iota((total, total), 0)
    t = over(r, chips * shard)
    s = over(r - t * (chips * shard), shard)
    i = r - t * (chips * shard) - s * shard
    order = one_hot(iota((total, total), 1) == s * rows + (t ^ d) * shard + i)
    columns = exact(order, columns).astype(jnp.bfloat16)
    out_ref[:, pl.ds(pl.multiple_of(core * cols, LANES), cols)] = exact(columns, own_ref[...])
    out_ref[:, pl.ds(pl.multiple_of((1 - core) * cols, LANES), cols)] = exact(columns, other_ref[...])


def embed_kernel(chips, dp, shard, head_ref, *refs):
    d, z, core = place()
    slot_refs, out_refs = refs[:-dp], refs[-dp:]
    total, cols = head_ref.shape
    count = len(slot_refs) * slot_refs[0].shape[0]
    ids = jnp.concatenate([ref[:, cols:].astype(jnp.float32) for ref in slot_refs], axis=0)
    ids = ids[:, :1].astype(jnp.int32)
    values = jnp.concatenate([ref[:, :cols].astype(jnp.float32) for ref in slot_refs], axis=0)
    values = values.astype(jnp.bfloat16)
    block = over(jnp.maximum(ids, 0), shard)
    owner = (iota((count, 1), 0) % chips) ^ z
    target = (block * chips + owner) * shard + ids - block * shard
    target = jnp.where(ids < 0, -1, target)
    picked = one_hot(iota((count, total), 1) == target)
    embed = lax.dot_general(picked, values, (((0,), (0,)), ((), ())), preferred_element_type=jnp.float32)
    part = head_ref[...] + embed
    size = chips * shard
    for t, out_ref in enumerate(out_refs):
        out_ref[...] = part[t * size : (t + 1) * size]


def sum_kernel(chips, shard, *refs):
    dp = len(refs) - chips
    total = refs[0][...]
    for t in range(1, dp):
        total = total + refs[t][...]
    half = total.shape[1] // CORES
    for s, out_ref in enumerate(refs[dp:]):
        rows = total[s * shard : (s + 1) * shard]
        out_ref[...] = jnp.concatenate([rows[:, :half], rows[:, half:]], axis=0)


def adam_kernel(chips, shard, master_ref, first_ref, second_ref, *refs):
    d, z, core = place()
    pieces, (master_out, first_out, second_out, table_ref) = refs[:chips], refs[chips:]
    half = pieces[0].shape[1]
    table = []
    for s, piece in enumerate(pieces):
        piece = piece[...]
        gradient = jnp.concatenate([piece[:shard], piece[shard:]], axis=1)
        spot = pl.ds(pl.multiple_of((z ^ s) * (CORES * half), LANES), CORES * half)
        master = master_ref[:, spot]
        first_new = 0.9 * first_ref[:, spot] + 0.1 * gradient
        second_new = 0.95 * second_ref[:, spot] + 0.05 * gradient * gradient
        first_hat = first_new / (1.0 - 0.9**STEP)
        second_hat = second_new / (1.0 - 0.95**STEP)
        master_new = master - 0.05 * (first_hat / (jnp.sqrt(second_hat) + 1e-08) + 0.1 * master)
        master_out[:, spot] = master_new
        first_out[:, spot] = first_new
        second_out[:, spot] = second_new
        table.append(master_new)
    table_ref[...] = jnp.concatenate(table, axis=0).astype(jnp.bfloat16)


def table_kernel(chips, shard, *refs):
    d, z, core = place()
    parts, out_ref = refs[:-1], refs[-1]
    dp = len(parts)
    cols = parts[0].shape[1]
    rows = dp * shard
    total = chips * rows
    values = jnp.concatenate([part[...] for part in parts], axis=0)
    r = iota((total, total), 0)
    s = over(r, rows)
    e = over(r - s * rows, shard)
    i = r - s * rows - e * shard
    order = one_hot(iota((total, total), 1) == ((e ^ d) * chips + s) * shard + i)
    values = exact(order, values).astype(jnp.bfloat16)
    for s in range(chips):
        spot = pl.ds(pl.multiple_of((z ^ s) * cols, LANES), cols)
        out_ref[:, spot] = values[s * rows : (s + 1) * rows]


def shaped(shape, kind):
    return jax.ShapeDtypeStruct(shape, kind)


def run(kernel, outs, *args, flops=0):
    moved = sum(x.size * x.dtype.itemsize for x in (*args, *jax.tree.leaves(outs)))
    return pl.pallas_call(
        kernel,
        out_shape=outs,
        cost_estimate=pl.CostEstimate(flops=flops, bytes_accessed=moved, transcendentals=0),
        compiler_params=pltpu.CompilerParams(vmem_limit_bytes=VMEM_LIMIT),
    )(*args)


def aligned(
    hidden,
    logit_grad,
    predict_mask,
    slot_grads,
    slot_rows,
    slot_counts,
    master,
    first_moment,
    second_moment,
):
    vocab = lax.axis_size("vocab")
    dp = lax.axis_size("dp")
    chips = vocab // CORES
    rows = logit_grad.shape[1]
    shard = master.shape[0]
    cols = hidden.shape[1] * CORES
    depth = hidden.shape[0]
    owners, cap, width = slot_grads.shape[1:]
    sizes = (chips, dp, shard)
    bf16, f32 = jnp.bfloat16, jnp.float32

    def send(x, s, away=0):
        move = s * CORES + away
        return lax.ppermute(x, "vocab", [(v, v ^ move) for v in range(vocab)]) if move else x

    def send_dp(x, t):
        return lax.ppermute(x, "dp", [(i, i ^ t) for i in range(dp)]) if t else x

    columns = logit_grad.T
    columns = [send(columns, s) for s in range(chips)]
    hidden_other = send(hidden, 0, 1)
    messages = run(
        functools.partial(slots_kernel, *sizes),
        [shaped((cap * chips, cols + LANES), bf16)] * (CORES * chips),
        slot_grads[0].transpose(1, 0, 2).reshape(cap * owners, width),
        slot_rows.transpose(2, 0, 1),
        slot_counts,
    )
    arrived = [send(messages[away * chips + s], s, away) for s in range(chips) for away in range(CORES)]
    head = run(
        functools.partial(head_kernel, *sizes),
        shaped((chips * rows, cols), f32),
        predict_mask[None, :],
        hidden,
        hidden_other,
        *columns,
        flops=2 * chips * rows * depth * cols,
    )
    parts = run(
        functools.partial(embed_kernel, *sizes),
        [shaped((chips * shard, cols), f32)] * dp,
        head,
        *arrived,
    )
    parts = [send_dp(parts[t], t) for t in range(dp)]
    pieces = run(
        functools.partial(sum_kernel, chips, shard),
        [shaped((CORES * shard, cols // CORES), f32)] * chips,
        *parts,
    )
    pieces = [send(pieces[s], s) for s in range(chips)]
    master_new, first_new, second_new, table = run(
        functools.partial(adam_kernel, chips, shard),
        [shaped(master.shape, f32)] * 3 + [shaped((chips * shard, cols), bf16)],
        master,
        first_moment,
        second_moment,
        *pieces,
    )
    table = run(
        functools.partial(table_kernel, chips, shard),
        shaped((rows, width), bf16),
        *[send_dp(table, t) for t in range(dp)],
    )
    return (master_new, first_new, second_new, table)


def plain(
    hidden,
    logit_grad,
    predict_mask,
    slot_grads,
    slot_rows,
    slot_counts,
    master,
    first_moment,
    second_moment,
):
    vocab = lax.axis_size("vocab")
    dp = lax.axis_size("dp")
    chips = vocab // CORES
    rows = logit_grad.shape[1]
    shard = master.shape[0]
    cols = hidden.shape[1] * CORES
    owners, cap, width = slot_grads.shape[1:]
    here = lax.axis_index("vocab")
    core = here % CORES
    z = here // CORES
    d = lax.axis_index("dp")

    def to_core(x):
        return lax.ppermute(x, "vocab", [(v, v ^ 1) for v in range(vocab)])

    def to_chip(x, s):
        return lax.ppermute(x, "vocab", [(v, v ^ (s * CORES)) for v in range(vocab)])

    def to_dp(x, t):
        return lax.ppermute(x, "dp", [(i, i ^ t) for i in range(dp)])

    label = jnp.arange(rows, dtype=jnp.int32)
    source = ((label // shard) ^ d) * shard + label % shard
    reorder = (source[:, None] == label[None, :]).astype(jnp.bfloat16)
    masked = logit_grad * predict_mask.astype(jnp.bfloat16)[:, None]
    masked = lax.dot_general(reorder, masked, (((1,), (1,)), ((), ())), preferred_element_type=jnp.bfloat16)

    slot_index = jnp.arange(cap, dtype=jnp.int32)[None, :]
    ids = ((slot_rows[0] // shard) ^ d) * shard + slot_rows[0] % shard
    ids = jnp.where(slot_index < slot_counts[0][:, None], ids, -1).astype(jnp.bfloat16)
    ids = jnp.broadcast_to(ids[:, :, None, None], (owners, cap, chips, LANES))
    slots = slot_grads[0].reshape(owners, cap, chips, cols)
    slots = jnp.concatenate([slots, ids], axis=3).reshape(chips, CORES, cap, chips, cols + LANES)
    mine = lax.dynamic_index_in_dim(slots, core, 1, keepdims=False)
    other = lax.dynamic_index_in_dim(slots, 1 - core, 1, keepdims=False)
    hidden_other = to_core(hidden)
    other = to_core(other)
    masked = [masked] + [to_chip(masked, s) for s in range(1, chips)]
    both = jnp.stack([mine, other]).reshape(CORES * chips * cap, chips, cols + LANES)
    slots = [lax.dynamic_index_in_dim(both, z ^ s, 1, keepdims=False) for s in range(chips)]
    slots = [slots[0]] + [to_chip(slots[s], s) for s in range(1, chips)]

    swap = core == 1
    low = jnp.where(swap, hidden_other, hidden)
    high = jnp.where(swap, hidden, hidden_other)
    wide = jnp.concatenate([low, high], axis=1)
    slots = jnp.concatenate(slots, axis=0)
    owner = (jnp.arange(slots.shape[0], dtype=jnp.int32) // cap) % chips
    ids = slots[:, cols].astype(jnp.int32)
    ids = jnp.where(ids < 0, -1, (owner ^ z) * rows + ids)
    picked = (jnp.arange(chips * rows, dtype=jnp.int32)[:, None] == ids[None, :]).astype(jnp.bfloat16)
    part = jnp.dot(jnp.concatenate(masked, axis=0), wide, preferred_element_type=jnp.float32)
    part = part + jnp.dot(picked, slots[:, :cols], preferred_element_type=jnp.float32)
    part = part.reshape(chips, dp, shard, cols)
    part = [part[:, t].reshape(chips * shard, cols) for t in range(dp)]
    total = part[0]
    for t in range(1, dp):
        total = total + to_dp(part[t], t)
    total = total.reshape(chips, shard, CORES, cols // CORES).transpose(0, 2, 1, 3)
    total = total.reshape(chips, CORES * shard, cols // CORES)
    pieces = [total[0]] + [to_chip(total[s], s) for s in range(1, chips)]
    pieces = jnp.stack(pieces).reshape(chips, CORES, shard, cols // CORES).transpose(0, 2, 1, 3)
    pieces = pieces.reshape(chips, shard, cols)
    gradient = jnp.concatenate([lax.dynamic_index_in_dim(pieces, z ^ s, 0, keepdims=False) for s in range(chips)], axis=1)
    first_new = 0.9 * first_moment + 0.1 * gradient
    second_new = 0.95 * second_moment + 0.05 * gradient * gradient
    first_hat = first_new / (1.0 - 0.9**STEP)
    second_hat = second_new / (1.0 - 0.95**STEP)
    master_new = master - 0.05 * (first_hat / (jnp.sqrt(second_hat) + 1e-08) + 0.1 * master)
    table = master_new.astype(jnp.bfloat16)
    table = table.reshape(shard, chips, cols).transpose(1, 0, 2).reshape(chips * shard, cols)
    table = jnp.stack([table] + [to_dp(table, t) for t in range(1, dp)])
    table = jnp.stack([lax.dynamic_index_in_dim(table, d ^ t, 0, keepdims=False) for t in range(dp)])
    table = table.reshape(dp, chips, shard, cols).transpose(0, 2, 1, 3).reshape(rows, width)
    return (master_new, first_new, second_new, table)


def local(hidden, logit_grad, predict_mask, slot_grads, *rest):
    vocab = lax.axis_size("vocab")
    fits = hidden.shape[1] % LANES == 0 and logit_grad.shape[1] % 16 == 0
    fits = fits and (vocab // CORES * slot_grads.shape[2]) % 8 == 0
    step = aligned if fits else plain
    return step(hidden, logit_grad, predict_mask, slot_grads, *rest)


def solution(mesh):
    in_specs = (
        P("dp", "vocab"),
        P("dp", "vocab"),
        P("dp"),
        P(("dp", "vocab"), None, None, None),
        P(("dp", "vocab"), None, None),
        P(("dp", "vocab"), None),
        P(("vocab", "dp"), None),
        P(("vocab", "dp"), None),
        P(("vocab", "dp"), None),
    )
    out_specs = (
        P(("vocab", "dp"), None),
        P(("vocab", "dp"), None),
        P(("vocab", "dp"), None),
        P("vocab", None),
    )
    return jax.shard_map(local, mesh=mesh, in_specs=in_specs, out_specs=out_specs, check_vma=False)
```

```python
import functools

import jax
import jax.numpy as jnp
from jax import lax
from jax.experimental import pallas as pl
from jax.experimental.pallas import tpu as pltpu
from jax.sharding import PartitionSpec as P

STEP = 8
CORES = 2
LANES = 128
VMEM_LIMIT = 24 * 1024 * 1024


def place():
    here = lax.axis_index("vocab")
    return lax.axis_index("dp"), lax.shift_right_logical(here, 1), here & 1


def iota(shape, axis):
    return lax.broadcasted_iota(jnp.int32, shape, axis)


def over(x, n):
    return ((x.astype(jnp.float32) + 0.5) * (1.0 / n)).astype(jnp.int32)


def one_hot(flag):
    return jnp.where(flag, 1.0, 0.0).astype(jnp.bfloat16)


def exact(left, right):
    return jnp.dot(left, right, preferred_element_type=jnp.float32)


def slots_kernel(chips, dp, shard, slots_hbm, rows_hbm, counts_hbm, own_out, other_out, slots_ref, rows_ref, counts_ref, sems):
    d, z, core = place()
    copies = [
        pltpu.make_async_copy(rows_hbm, rows_ref, sems.at[0]),
        pltpu.make_async_copy(counts_hbm, counts_ref, sems.at[1]),
        pltpu.make_async_copy(slots_hbm, slots_ref, sems.at[2]),
    ]
    for copy in copies:
        copy.start()
    for copy in copies:
        copy.wait()
    cap, owners = rows_ref.shape[0], rows_ref.shape[2]
    count = cap * owners
    group = cap * chips
    width = slots_ref.shape[1] // chips
    half = chips // 2
    own_lane = iota((count, owners), 1) == iota((count, owners), 0) % owners
    rows = jnp.broadcast_to(rows_ref[...], (cap, owners, owners)).reshape(count, owners)
    rows = jnp.sum(jnp.where(own_lane, rows, 0), axis=1, keepdims=True)
    live = jnp.broadcast_to(counts_ref[...], (count, owners))
    live = jnp.sum(jnp.where(own_lane, live, 0), axis=1, keepdims=True)
    block = over(rows, shard)
    ids = (block ^ d) * shard + rows - block * shard
    ids = jnp.where(over(iota((count, 1), 0), owners) < live, ids, -1)
    ids = jnp.broadcast_to(ids, (count, LANES)).astype(jnp.bfloat16)
    q = iota((CORES * group, count), 0)
    away = jnp.where(q >= group, 1, 0)
    q = q - away * group
    near = jnp.where(q >= group // 2, 1, 0)
    q = q - near * (group // 2)
    slot = over(q, half)
    owner = q - slot * half + (1 - near) * half
    for s in range(chips):
        wanted = slot * owners + (owner ^ z ^ s) * CORES + (away ^ core)
        pick = one_hot(iota((CORES * group, count), 1) == wanted)
        start = pl.multiple_of((z ^ s) * width, LANES)
        values = exact(pick, slots_ref[:, pl.ds(start, width)]).astype(jnp.bfloat16)
        picked_ids = exact(pick, ids).astype(jnp.bfloat16)
        first = s * (width + LANES)
        for out_ref, spot in ((own_out, slice(0, group)), (other_out, slice(group, CORES * group))):
            out_ref[:, first : first + width] = values[spot]
            out_ref[:, first + width : first + width + LANES] = picked_ids[spot]


def merge_kernel(chips, own_ref, other_ref, *out_refs):
    size = own_ref.shape[1] // chips
    part = own_ref.shape[0] // 2
    for s in range(chips):
        own = own_ref[:, s * size : (s + 1) * size].astype(jnp.float32)
        other = other_ref[:, s * size : (s + 1) * size].astype(jnp.float32)
        for h in range(2):
            spot = slice(h * part, (h + 1) * part)
            both = jnp.concatenate([own[spot], other[spot]], axis=0)
            out_refs[h * chips + s][...] = both.astype(jnp.bfloat16)


def head_kernel(chips, dp, shard, mask_hbm, hidden_hbm, columns_hbm, other_ref, *refs):
    d, z, core = place()
    parts, outs = refs[: chips - 1], refs[chips - 1 : chips + 1]
    mask_ref, own_ref, columns_ref, sems = refs[chips + 1 :]
    copies = [
        pltpu.make_async_copy(mask_hbm, mask_ref, sems.at[0]),
        pltpu.make_async_copy(columns_hbm, columns_ref, sems.at[1]),
        pltpu.make_async_copy(hidden_hbm, own_ref, sems.at[2]),
    ]
    for copy in copies:
        copy.start()
    for copy in copies:
        copy.wait()
    rows = dp * shard
    total = chips * rows
    cols = own_ref.shape[1]
    half = chips // 2
    mask = mask_ref[...].astype(jnp.float32).astype(jnp.bfloat16)
    columns = jnp.concatenate([part[...] for part in (columns_ref, *parts)], axis=0) * mask
    r = iota((total, total), 0)
    near = jnp.where(r >= total // 2, 1, 0)
    r = r - near * (total // 2)
    t = over(r, half * shard)
    j = over(r - t * (half * shard), shard)
    i = r - t * (half * shard) - j * shard
    order = one_hot(iota((total, total), 1) == (j + (1 - near) * half) * rows + (t ^ d) * shard + i)
    columns = exact(order, columns).astype(jnp.bfloat16)
    for at, ref in ((core, own_ref), (1 - core, other_ref)):
        head = exact(columns, ref[...])
        spot = pl.ds(pl.multiple_of(at * cols, LANES), cols)
        for h in range(2):
            outs[h][:, spot] = head[h * (total // 2) : (h + 1) * (total // 2)]


def embed_kernel(chips, dp, shard, head_ref, *refs):
    slot_refs, out_refs = refs[:-dp], refs[-dp:]
    half = chips // 2
    total, cols = head_ref.shape
    count = len(slot_refs) * slot_refs[0].shape[0]
    ids = jnp.concatenate([ref[:, cols:].astype(jnp.float32) for ref in slot_refs], axis=0)
    ids = ids[:, :1].astype(jnp.int32)
    values = jnp.concatenate([ref[:, :cols].astype(jnp.float32) for ref in slot_refs], axis=0)
    values = values.astype(jnp.bfloat16)
    block = over(jnp.maximum(ids, 0), shard)
    target = (block * half + iota((count, 1), 0) % half) * shard + ids - block * shard
    target = jnp.where(ids < 0, -1, target)
    picked = one_hot(iota((count, total), 1) == target)
    embed = lax.dot_general(picked, values, (((0,), (0,)), ((), ())), preferred_element_type=jnp.float32)
    part = head_ref[...] + embed
    size = half * shard
    for t, out_ref in enumerate(out_refs):
        out_ref[...] = part[t * size : (t + 1) * size]


def sum_kernel(half, shard, *refs):
    dp = len(refs) - half
    total = refs[0][...]
    for t in range(1, dp):
        total = total + refs[t][...]
    cut = total.shape[1] // CORES
    for j, out_ref in enumerate(refs[dp:]):
        rows = total[j * shard : (j + 1) * shard]
        out_ref[...] = jnp.concatenate([rows[:, :cut], rows[:, cut:]], axis=0)


def step(shard, spot, piece_ref, master_ref, first_ref, second_ref):
    piece = piece_ref[...]
    gradient = jnp.concatenate([piece[:shard], piece[shard:]], axis=1)
    master = master_ref[:, spot]
    first_new = 0.9 * first_ref[:, spot] + 0.1 * gradient
    second_new = 0.95 * second_ref[:, spot] + 0.05 * gradient * gradient
    first_hat = first_new / (1.0 - 0.9**STEP)
    second_hat = second_new / (1.0 - 0.95**STEP)
    master_new = master - 0.05 * (first_hat / (jnp.sqrt(second_hat) + 1e-08) + 0.1 * master)
    return master_new, first_new, second_new


def chip_spot(z, s, piece_ref):
    cols = piece_ref.shape[1] * CORES
    return pl.ds(pl.multiple_of((z ^ s) * cols, LANES), cols)


def rows_kernel(members, shard, *refs):
    d, z, core = place()
    state, pieces, out_ref = refs[:3], refs[3:-1], refs[-1]
    table = [step(shard, chip_spot(z, s, piece), piece, *state)[0] for s, piece in zip(members, pieces)]
    out_ref[...] = jnp.concatenate(table, axis=0).astype(jnp.bfloat16)


def adam_kernel(shard, *refs):
    d, z, core = place()
    state, pieces, outs = refs[:3], refs[3:-3], refs[-3:]
    for s, piece in enumerate(pieces):
        spot = chip_spot(z, s, piece)
        for out_ref, value in zip(outs, step(shard, spot, piece, *state)):
            out_ref[:, spot] = value


def table_kernel(chips, dp, shard, *refs):
    d, z, core = place()
    parts, out_ref = refs[:-1], refs[-1]
    cols = parts[0].shape[1]
    rows = dp * shard
    total = chips * rows
    half = chips // 2
    values = jnp.concatenate([part[...].astype(jnp.float32) for part in parts], axis=0).astype(jnp.bfloat16)
    r = iota((total, total), 0)
    s = over(r, rows)
    e = over(r - s * rows, shard)
    i = r - s * rows - e * shard
    far = jnp.where(s >= half, 1, 0)
    j = s - far * half
    order = one_hot(iota((total, total), 1) == ((far * dp + (e ^ d)) * half + j) * shard + i)
    values = exact(order, values).astype(jnp.bfloat16)
    for s in range(chips):
        spot = pl.ds(pl.multiple_of((z ^ s) * cols, LANES), cols)
        out_ref[:, spot] = values[s * rows : (s + 1) * rows]


def shaped(shape, kind):
    return jax.ShapeDtypeStruct(shape, kind)


def run(kernel, outs, *args, flops=0, hbm=0, scratch=()):
    moved = sum(x.size * x.dtype.itemsize for x in (*args, *jax.tree.leaves(outs)))
    vmem = pl.BlockSpec(memory_space=pltpu.VMEM)
    args = [pltpu.with_memory_space_constraint(x, pltpu.HBM) if n < hbm else x for n, x in enumerate(args)]
    return pl.pallas_call(
        kernel,
        out_shape=outs,
        in_specs=[pl.BlockSpec(memory_space=pltpu.HBM)] * hbm + [vmem] * (len(args) - hbm),
        out_specs=jax.tree.map(lambda _: vmem, outs),
        scratch_shapes=list(scratch),
        cost_estimate=pl.CostEstimate(flops=flops, bytes_accessed=moved, transcendentals=0),
        compiler_params=pltpu.CompilerParams(vmem_limit_bytes=VMEM_LIMIT),
    )(*args)


def local_copies(*args):
    return [pltpu.VMEM(x.shape, x.dtype) for x in args] + [pltpu.SemaphoreType.DMA((len(args),))]


def aligned(
    hidden,
    logit_grad,
    predict_mask,
    slot_grads,
    slot_rows,
    slot_counts,
    master,
    first_moment,
    second_moment,
):
    vocab = lax.axis_size("vocab")
    dp = lax.axis_size("dp")
    chips = vocab // CORES
    half = chips // 2
    rows = logit_grad.shape[1]
    shard = master.shape[0]
    cols = hidden.shape[1] * CORES
    depth = hidden.shape[0]
    owners, cap, width = slot_grads.shape[1:]
    sizes = (chips, dp, shard)
    bf16, f32 = jnp.bfloat16, jnp.float32
    far, near = range(half, chips), range(half)

    def send(x, s, away=0):
        move = s * CORES + away
        return lax.ppermute(x, "vocab", [(v, v ^ move) for v in range(vocab)]) if move else x

    def send_dp(x, t):
        return lax.ppermute(x, "dp", [(i, i ^ t) for i in range(dp)]) if t else x

    columns = [logit_grad.T]
    for s in range(1, chips):
        columns.append(send(columns[s - 1], 1) if s % 2 else send(columns[0], s))
    hidden_other = send(hidden, 0, 1)
    slots_in = (
        slot_grads[0].transpose(1, 0, 2).reshape(cap * owners, width),
        slot_rows.transpose(2, 0, 1),
        slot_counts,
    )
    slots_own, slots_other = run(
        functools.partial(slots_kernel, *sizes),
        [shaped((cap * chips, chips * (cols + LANES)), bf16)] * CORES,
        *slots_in,
        hbm=3,
        scratch=local_copies(*slots_in),
    )
    messages = run(
        functools.partial(merge_kernel, chips),
        [shaped((cap * half * CORES, cols + LANES), bf16)] * (2 * chips),
        slots_own,
        send(slots_other, 0, 1),
    )
    head_in = (predict_mask[None, :], hidden, columns[0])
    head = run(
        functools.partial(head_kernel, *sizes),
        [shaped((half * rows, cols), f32)] * 2,
        *head_in,
        hidden_other,
        *columns[1:],
        flops=2 * chips * rows * depth * cols,
        hbm=3,
        scratch=local_copies(*head_in),
    )
    state = (master, first_moment, second_moment)
    messages = [messages[:chips], messages[chips:]]
    pieces, table = {}, []
    for h, members in enumerate((far, near)):
        start = head[h]
        if h:
            messages[h], _ = lax.optimization_barrier((messages[h], arrived[1]))
            start, _ = lax.optimization_barrier((start, parts[0]))
        arrived = [send(messages[h][s], s) for s in range(chips)]
        parts = run(
            functools.partial(embed_kernel, *sizes),
            [shaped((half * shard, cols), f32)] * dp,
            start,
            *arrived,
        )
        sums = run(
            functools.partial(sum_kernel, half, shard),
            [shaped((CORES * shard, cols // CORES), f32)] * half,
            *[send_dp(part, t) for t, part in enumerate(parts)],
        )
        for s, total in zip(members, sums):
            pieces[s] = send(total, s)
        table_rows = run(
            functools.partial(rows_kernel, tuple(members), shard),
            shaped((half * shard, cols), bf16),
            *state,
            *[pieces[s] for s in members],
        )
        table = [send_dp(table_rows, t) for t in range(dp)] + table
    master_new, first_new, second_new = run(
        functools.partial(adam_kernel, shard),
        [shaped(master.shape, f32)] * 3,
        *state,
        *[pieces[s] for s in range(chips)],
    )
    table = run(functools.partial(table_kernel, *sizes), shaped((rows, width), bf16), *table)
    return (master_new, first_new, second_new, table)


def plain(
    hidden,
    logit_grad,
    predict_mask,
    slot_grads,
    slot_rows,
    slot_counts,
    master,
    first_moment,
    second_moment,
):
    vocab = lax.axis_size("vocab")
    dp = lax.axis_size("dp")
    chips = vocab // CORES
    rows = logit_grad.shape[1]
    shard = master.shape[0]
    cols = hidden.shape[1] * CORES
    owners, cap, width = slot_grads.shape[1:]
    here = lax.axis_index("vocab")
    core = here % CORES
    z = here // CORES
    d = lax.axis_index("dp")

    def to_core(x):
        return lax.ppermute(x, "vocab", [(v, v ^ 1) for v in range(vocab)])

    def to_chip(x, s):
        return lax.ppermute(x, "vocab", [(v, v ^ (s * CORES)) for v in range(vocab)])

    def to_dp(x, t):
        return lax.ppermute(x, "dp", [(i, i ^ t) for i in range(dp)])

    label = jnp.arange(rows, dtype=jnp.int32)
    source = ((label // shard) ^ d) * shard + label % shard
    reorder = (source[:, None] == label[None, :]).astype(jnp.bfloat16)
    masked = logit_grad * predict_mask.astype(jnp.bfloat16)[:, None]
    masked = lax.dot_general(reorder, masked, (((1,), (1,)), ((), ())), preferred_element_type=jnp.bfloat16)

    slot_index = jnp.arange(cap, dtype=jnp.int32)[None, :]
    ids = ((slot_rows[0] // shard) ^ d) * shard + slot_rows[0] % shard
    ids = jnp.where(slot_index < slot_counts[0][:, None], ids, -1).astype(jnp.bfloat16)
    ids = jnp.broadcast_to(ids[:, :, None, None], (owners, cap, chips, LANES))
    slots = slot_grads[0].reshape(owners, cap, chips, cols)
    slots = jnp.concatenate([slots, ids], axis=3).reshape(chips, CORES, cap, chips, cols + LANES)
    mine = lax.dynamic_index_in_dim(slots, core, 1, keepdims=False)
    other = lax.dynamic_index_in_dim(slots, 1 - core, 1, keepdims=False)
    hidden_other = to_core(hidden)
    other = to_core(other)
    masked = [masked] + [to_chip(masked, s) for s in range(1, chips)]
    both = jnp.stack([mine, other]).reshape(CORES * chips * cap, chips, cols + LANES)
    slots = [lax.dynamic_index_in_dim(both, z ^ s, 1, keepdims=False) for s in range(chips)]
    slots = [slots[0]] + [to_chip(slots[s], s) for s in range(1, chips)]

    swap = core == 1
    low = jnp.where(swap, hidden_other, hidden)
    high = jnp.where(swap, hidden, hidden_other)
    wide = jnp.concatenate([low, high], axis=1)
    slots = jnp.concatenate(slots, axis=0)
    owner = (jnp.arange(slots.shape[0], dtype=jnp.int32) // cap) % chips
    ids = slots[:, cols].astype(jnp.int32)
    ids = jnp.where(ids < 0, -1, (owner ^ z) * rows + ids)
    picked = (jnp.arange(chips * rows, dtype=jnp.int32)[:, None] == ids[None, :]).astype(jnp.bfloat16)
    part = jnp.dot(jnp.concatenate(masked, axis=0), wide, preferred_element_type=jnp.float32)
    part = part + jnp.dot(picked, slots[:, :cols], preferred_element_type=jnp.float32)
    part = part.reshape(chips, dp, shard, cols)
    part = [part[:, t].reshape(chips * shard, cols) for t in range(dp)]
    total = part[0]
    for t in range(1, dp):
        total = total + to_dp(part[t], t)
    total = total.reshape(chips, shard, CORES, cols // CORES).transpose(0, 2, 1, 3)
    total = total.reshape(chips, CORES * shard, cols // CORES)
    pieces = [total[0]] + [to_chip(total[s], s) for s in range(1, chips)]
    pieces = jnp.stack(pieces).reshape(chips, CORES, shard, cols // CORES).transpose(0, 2, 1, 3)
    pieces = pieces.reshape(chips, shard, cols)
    gradient = jnp.concatenate([lax.dynamic_index_in_dim(pieces, z ^ s, 0, keepdims=False) for s in range(chips)], axis=1)
    first_new = 0.9 * first_moment + 0.1 * gradient
    second_new = 0.95 * second_moment + 0.05 * gradient * gradient
    first_hat = first_new / (1.0 - 0.9**STEP)
    second_hat = second_new / (1.0 - 0.95**STEP)
    master_new = master - 0.05 * (first_hat / (jnp.sqrt(second_hat) + 1e-08) + 0.1 * master)
    table = master_new.astype(jnp.bfloat16)
    table = table.reshape(shard, chips, cols).transpose(1, 0, 2).reshape(chips * shard, cols)
    table = jnp.stack([table] + [to_dp(table, t) for t in range(1, dp)])
    table = jnp.stack([lax.dynamic_index_in_dim(table, d ^ t, 0, keepdims=False) for t in range(dp)])
    table = table.reshape(dp, chips, shard, cols).transpose(0, 2, 1, 3).reshape(rows, width)
    return (master_new, first_new, second_new, table)


def local(hidden, logit_grad, predict_mask, slot_grads, *rest):
    vocab = lax.axis_size("vocab")
    fits = hidden.shape[1] % LANES == 0 and logit_grad.shape[1] % 16 == 0
    fits = fits and (vocab // CORES * slot_grads.shape[2]) % 8 == 0
    step = aligned if fits else plain
    return step(hidden, logit_grad, predict_mask, slot_grads, *rest)


def solution(mesh):
    in_specs = (
        P("dp", "vocab"),
        P("dp", "vocab"),
        P("dp"),
        P(("dp", "vocab"), None, None, None),
        P(("dp", "vocab"), None, None),
        P(("dp", "vocab"), None),
        P(("vocab", "dp"), None),
        P(("vocab", "dp"), None),
        P(("vocab", "dp"), None),
    )
    out_specs = (
        P(("vocab", "dp"), None),
        P(("vocab", "dp"), None),
        P(("vocab", "dp"), None),
        P("vocab", None),
    )
    return jax.shard_map(local, mesh=mesh, in_specs=in_specs, out_specs=out_specs, check_vma=False)
```

```python
import functools

import jax
import jax.numpy as jnp
from jax import lax
from jax.experimental import pallas as pl
from jax.experimental.pallas import tpu as pltpu
from jax.sharding import PartitionSpec as P

STEP = 8
CORES = 2
LANES = 128
VMEM_LIMIT = 24 * 1024 * 1024


def place():
    here = lax.axis_index("vocab")
    return lax.axis_index("dp"), lax.shift_right_logical(here, 1), here & 1


def iota(shape, axis):
    return lax.broadcasted_iota(jnp.int32, shape, axis)


def over(x, n):
    return ((x.astype(jnp.float32) + 0.5) * (1.0 / n)).astype(jnp.int32)


def one_hot(flag):
    return jnp.where(flag, 1.0, 0.0).astype(jnp.bfloat16)


def exact(left, right):
    return jnp.dot(left, right, preferred_element_type=jnp.float32)


def slots_kernel(chips, dp, shard, slots_hbm, rows_hbm, counts_hbm, own_out, other_out, slots_ref, rows_ref, counts_ref, sems):
    d, z, core = place()
    copies = [
        pltpu.make_async_copy(rows_hbm, rows_ref, sems.at[0]),
        pltpu.make_async_copy(counts_hbm, counts_ref, sems.at[1]),
        pltpu.make_async_copy(slots_hbm, slots_ref, sems.at[2]),
    ]
    for copy in copies:
        copy.start()
    for copy in copies:
        copy.wait()
    cap, owners = rows_ref.shape[0], rows_ref.shape[2]
    count = cap * owners
    group = cap * chips
    width = slots_ref.shape[1] // chips
    half = chips // 2
    own_lane = iota((count, owners), 1) == iota((count, owners), 0) % owners
    rows = jnp.broadcast_to(rows_ref[...], (cap, owners, owners)).reshape(count, owners)
    rows = jnp.sum(jnp.where(own_lane, rows, 0), axis=1, keepdims=True)
    live = jnp.broadcast_to(counts_ref[...], (count, owners))
    live = jnp.sum(jnp.where(own_lane, live, 0), axis=1, keepdims=True)
    block = over(rows, shard)
    ids = (block ^ d) * shard + rows - block * shard
    ids = jnp.where(over(iota((count, 1), 0), owners) < live, ids, -1)
    ids = jnp.broadcast_to(ids, (count, LANES)).astype(jnp.bfloat16)
    q = iota((CORES * group, count), 0)
    away = jnp.where(q >= group, 1, 0)
    q = q - away * group
    near = jnp.where(q >= group // 2, 1, 0)
    q = q - near * (group // 2)
    slot = over(q, half)
    owner = q - slot * half + (1 - near) * half
    for s in range(chips):
        wanted = slot * owners + (owner ^ z ^ s) * CORES + (away ^ core)
        pick = one_hot(iota((CORES * group, count), 1) == wanted)
        start = pl.multiple_of((z ^ s) * width, LANES)
        values = exact(pick, slots_ref[:, pl.ds(start, width)])
        picked_ids = exact(pick, ids)
        first = s * (width + LANES)
        for out_ref, spot in ((own_out, slice(0, group)), (other_out, slice(group, CORES * group))):
            out_ref[:, first : first + width] = values[spot].astype(jnp.bfloat16)
            out_ref[:, first + width : first + width + LANES] = picked_ids[spot].astype(jnp.bfloat16)


def merge_kernel(chips, own_ref, other_ref, *out_refs):
    size = own_ref.shape[1] // chips
    for s, out_ref in enumerate(out_refs):
        parts = [ref[:, s * size : (s + 1) * size].astype(jnp.float32) for ref in (own_ref, other_ref)]
        out_ref[...] = jnp.concatenate(parts, axis=0).astype(jnp.bfloat16)


def head_kernel(chips, dp, shard, mask_hbm, hidden_hbm, columns_hbm, other_ref, *refs):
    d, z, core = place()
    parts, out_ref = refs[: chips - 1], refs[chips - 1]
    mask_ref, own_ref, columns_ref, sems = refs[chips:]
    copies = [
        pltpu.make_async_copy(mask_hbm, mask_ref, sems.at[0]),
        pltpu.make_async_copy(columns_hbm, columns_ref, sems.at[1]),
        pltpu.make_async_copy(hidden_hbm, own_ref, sems.at[2]),
    ]
    for copy in copies:
        copy.start()
    for copy in copies:
        copy.wait()
    rows = dp * shard
    total = chips * rows
    cols = own_ref.shape[1]
    half = chips // 2
    mask = mask_ref[...].astype(jnp.float32).astype(jnp.bfloat16)
    columns = jnp.concatenate([part[...] for part in (columns_ref, *parts)], axis=0) * mask
    r = iota((total, total), 0)
    near = jnp.where(r >= total // 2, 1, 0)
    r = r - near * (total // 2)
    t = over(r, half * shard)
    j = over(r - t * (half * shard), shard)
    i = r - t * (half * shard) - j * shard
    order = one_hot(iota((total, total), 1) == (j + (1 - near) * half) * rows + (t ^ d) * shard + i)
    columns = exact(order, columns).astype(jnp.bfloat16)
    for at, ref in ((core, own_ref), (1 - core, other_ref)):
        out_ref[:, pl.ds(pl.multiple_of(at * cols, LANES), cols)] = exact(columns, ref[...])


def embed_kernel(chips, dp, shard, head_ref, *refs):
    slot_refs, out_refs = refs[: -2 * dp], refs[-2 * dp :]
    half = chips // 2
    total, cols = head_ref.shape
    size = half * shard
    count = sum(ref.shape[0] for ref in slot_refs)
    ids = jnp.concatenate([ref[:, cols:] for ref in slot_refs], axis=0)
    ids = ids.astype(jnp.float32)[:, :1].astype(jnp.int32)
    values = jnp.concatenate([ref[:, :cols] for ref in slot_refs], axis=0)
    block = over(jnp.maximum(ids, 0), shard)
    group = slot_refs[0].shape[0] // CORES
    place_in = iota((count, 1), 0) % group
    near = jnp.where(place_in >= group // 2, 1, 0)
    target = near * (total // 2) + (block * half + place_in % half) * shard + ids - block * shard
    target = jnp.where(ids < 0, -1, target)
    picked = one_hot(iota((count, total), 1) == target)
    embed = lax.dot_general(picked, values, (((0,), (0,)), ((), ())), preferred_element_type=jnp.float32)
    for n, out_ref in enumerate(out_refs):
        spot = slice(n * size, (n + 1) * size)
        out_ref[...] = head_ref[spot] + embed[spot]


def sum_kernel(half, shard, *refs):
    dp = len(refs) - half
    total = refs[0][...]
    for t in range(1, dp):
        total = total + refs[t][...]
    cut = total.shape[1] // CORES
    for j, out_ref in enumerate(refs[dp:]):
        rows = total[j * shard : (j + 1) * shard]
        out_ref[...] = jnp.concatenate([rows[:, :cut], rows[:, cut:]], axis=0)


def step(shard, spot, piece_ref, master_ref, first_ref, second_ref):
    piece = piece_ref[...]
    gradient = jnp.concatenate([piece[:shard], piece[shard:]], axis=1)
    master = master_ref[:, spot]
    first_new = 0.9 * first_ref[:, spot] + 0.1 * gradient
    second_new = 0.95 * second_ref[:, spot] + 0.05 * gradient * gradient
    first_hat = first_new / (1.0 - 0.9**STEP)
    second_hat = second_new / (1.0 - 0.95**STEP)
    master_new = master - 0.05 * (first_hat / (jnp.sqrt(second_hat) + 1e-08) + 0.1 * master)
    return master_new, first_new, second_new


def chip_spot(z, s, piece_ref):
    cols = piece_ref.shape[1] * CORES
    return pl.ds(pl.multiple_of((z ^ s) * cols, LANES), cols)


def rows_kernel(shard, *refs):
    d, z, core = place()
    state, pieces, out_ref = refs[:3], refs[3:-1], refs[-1]
    table = [step(shard, chip_spot(z, s, piece), piece, *state)[0] for s, piece in enumerate(pieces)]
    out_ref[...] = jnp.concatenate(table, axis=0).astype(jnp.bfloat16)


def adam_kernel(shard, *refs):
    d, z, core = place()
    state, pieces, outs = refs[:3], refs[3:-3], refs[-3:]
    for s, piece in enumerate(pieces):
        spot = chip_spot(z, s, piece)
        for out_ref, value in zip(outs, step(shard, spot, piece, *state)):
            out_ref[:, spot] = value


def table_kernel(chips, dp, shard, *refs):
    d, z, core = place()
    parts, out_ref = refs[:-1], refs[-1]
    cols = parts[0].shape[1]
    rows = dp * shard
    total = chips * rows
    values = jnp.concatenate([part[...] for part in parts], axis=0)
    r = iota((total, total), 0)
    s = over(r, rows)
    e = over(r - s * rows, shard)
    i = r - s * rows - e * shard
    order = one_hot(iota((total, total), 1) == ((e ^ d) * chips + s) * shard + i)
    values = exact(order, values).astype(jnp.bfloat16)
    for s in range(chips):
        spot = pl.ds(pl.multiple_of((z ^ s) * cols, LANES), cols)
        out_ref[:, spot] = values[s * rows : (s + 1) * rows]


def shaped(shape, kind):
    return jax.ShapeDtypeStruct(shape, kind)


def run(kernel, outs, *args, flops=0, hbm=0, scratch=()):
    moved = sum(x.size * x.dtype.itemsize for x in (*args, *jax.tree.leaves(outs)))
    vmem = pl.BlockSpec(memory_space=pltpu.VMEM)
    args = [pltpu.with_memory_space_constraint(x, pltpu.HBM) if n < hbm else x for n, x in enumerate(args)]
    return pl.pallas_call(
        kernel,
        out_shape=outs,
        in_specs=[pl.BlockSpec(memory_space=pltpu.HBM)] * hbm + [vmem] * (len(args) - hbm),
        out_specs=jax.tree.map(lambda _: vmem, outs),
        scratch_shapes=list(scratch),
        cost_estimate=pl.CostEstimate(flops=flops, bytes_accessed=moved, transcendentals=0),
        compiler_params=pltpu.CompilerParams(vmem_limit_bytes=VMEM_LIMIT),
    )(*args)


def local_copies(*args):
    return [pltpu.VMEM(x.shape, x.dtype) for x in args] + [pltpu.SemaphoreType.DMA((len(args),))]


def aligned(
    hidden,
    logit_grad,
    predict_mask,
    slot_grads,
    slot_rows,
    slot_counts,
    master,
    first_moment,
    second_moment,
):
    vocab = lax.axis_size("vocab")
    dp = lax.axis_size("dp")
    chips = vocab // CORES
    half = chips // 2
    rows = logit_grad.shape[1]
    shard = master.shape[0]
    cols = hidden.shape[1] * CORES
    depth = hidden.shape[0]
    owners, cap, width = slot_grads.shape[1:]
    sizes = (chips, dp, shard)
    bf16, f32 = jnp.bfloat16, jnp.float32
    far, near = range(half, chips), range(half)

    def send(x, s, away=0):
        move = s * CORES + away
        return lax.ppermute(x, "vocab", [(v, v ^ move) for v in range(vocab)]) if move else x

    def send_dp(x, t):
        return lax.ppermute(x, "dp", [(i, i ^ t) for i in range(dp)]) if t else x

    columns = [logit_grad.T]
    for s in range(1, chips):
        columns.append(send(columns[s - 1], 1) if s % 2 else send(columns[0], s))
    hidden_other = send(hidden, 0, 1)
    slots_in = (
        slot_grads[0].transpose(1, 0, 2).reshape(cap * owners, width),
        slot_rows.transpose(2, 0, 1),
        slot_counts,
    )
    slots_own, slots_other = run(
        functools.partial(slots_kernel, *sizes),
        [shaped((cap * chips, chips * (cols + LANES)), bf16)] * CORES,
        *slots_in,
        hbm=3,
        scratch=local_copies(*slots_in),
    )
    messages = run(
        functools.partial(merge_kernel, chips),
        [shaped((cap * chips * CORES, cols + LANES), bf16)] * chips,
        slots_own,
        send(slots_other, 0, 1),
    )
    head_in = (predict_mask[None, :], hidden, columns[0])
    head = run(
        functools.partial(head_kernel, *sizes),
        shaped((chips * rows, cols), f32),
        *head_in,
        hidden_other,
        *columns[1:],
        flops=2 * chips * rows * depth * cols,
        hbm=3,
        scratch=local_copies(*head_in),
    )
    state = (master, first_moment, second_moment)
    parts = run(
        functools.partial(embed_kernel, *sizes),
        [shaped((half * shard, cols), f32)] * (2 * dp),
        head,
        *[send(message, s) for s, message in enumerate(messages)],
    )
    pieces = {}
    for h, members in enumerate((far, near)):
        sums = run(
            functools.partial(sum_kernel, half, shard),
            [shaped((CORES * shard, cols // CORES), f32)] * half,
            *[send_dp(parts[h * dp + t], t) for t in range(dp)],
        )
        for s, total in zip(members, sums):
            pieces[s] = send(total, s)
    pieces = [pieces[s] for s in range(chips)]
    table = run(
        functools.partial(rows_kernel, shard),
        shaped((chips * shard, cols), bf16),
        *state,
        *pieces,
    )
    master_new, first_new, second_new = run(
        functools.partial(adam_kernel, shard),
        [shaped(master.shape, f32)] * 3,
        *state,
        *pieces,
    )
    table = run(
        functools.partial(table_kernel, *sizes),
        shaped((rows, width), bf16),
        *[send_dp(table, t) for t in range(dp)],
    )
    return (master_new, first_new, second_new, table)


def plain(
    hidden,
    logit_grad,
    predict_mask,
    slot_grads,
    slot_rows,
    slot_counts,
    master,
    first_moment,
    second_moment,
):
    vocab = lax.axis_size("vocab")
    dp = lax.axis_size("dp")
    chips = vocab // CORES
    rows = logit_grad.shape[1]
    shard = master.shape[0]
    cols = hidden.shape[1] * CORES
    owners, cap, width = slot_grads.shape[1:]
    here = lax.axis_index("vocab")
    core = here % CORES
    z = here // CORES
    d = lax.axis_index("dp")

    def to_core(x):
        return lax.ppermute(x, "vocab", [(v, v ^ 1) for v in range(vocab)])

    def to_chip(x, s):
        return lax.ppermute(x, "vocab", [(v, v ^ (s * CORES)) for v in range(vocab)])

    def to_dp(x, t):
        return lax.ppermute(x, "dp", [(i, i ^ t) for i in range(dp)])

    label = jnp.arange(rows, dtype=jnp.int32)
    source = ((label // shard) ^ d) * shard + label % shard
    reorder = (source[:, None] == label[None, :]).astype(jnp.bfloat16)
    masked = logit_grad * predict_mask.astype(jnp.bfloat16)[:, None]
    masked = lax.dot_general(reorder, masked, (((1,), (1,)), ((), ())), preferred_element_type=jnp.bfloat16)

    slot_index = jnp.arange(cap, dtype=jnp.int32)[None, :]
    ids = ((slot_rows[0] // shard) ^ d) * shard + slot_rows[0] % shard
    ids = jnp.where(slot_index < slot_counts[0][:, None], ids, -1).astype(jnp.bfloat16)
    ids = jnp.broadcast_to(ids[:, :, None, None], (owners, cap, chips, LANES))
    slots = slot_grads[0].reshape(owners, cap, chips, cols)
    slots = jnp.concatenate([slots, ids], axis=3).reshape(chips, CORES, cap, chips, cols + LANES)
    mine = lax.dynamic_index_in_dim(slots, core, 1, keepdims=False)
    other = lax.dynamic_index_in_dim(slots, 1 - core, 1, keepdims=False)
    hidden_other = to_core(hidden)
    other = to_core(other)
    masked = [masked] + [to_chip(masked, s) for s in range(1, chips)]
    both = jnp.stack([mine, other]).reshape(CORES * chips * cap, chips, cols + LANES)
    slots = [lax.dynamic_index_in_dim(both, z ^ s, 1, keepdims=False) for s in range(chips)]
    slots = [slots[0]] + [to_chip(slots[s], s) for s in range(1, chips)]

    swap = core == 1
    low = jnp.where(swap, hidden_other, hidden)
    high = jnp.where(swap, hidden, hidden_other)
    wide = jnp.concatenate([low, high], axis=1)
    slots = jnp.concatenate(slots, axis=0)
    owner = (jnp.arange(slots.shape[0], dtype=jnp.int32) // cap) % chips
    ids = slots[:, cols].astype(jnp.int32)
    ids = jnp.where(ids < 0, -1, (owner ^ z) * rows + ids)
    picked = (jnp.arange(chips * rows, dtype=jnp.int32)[:, None] == ids[None, :]).astype(jnp.bfloat16)
    part = jnp.dot(jnp.concatenate(masked, axis=0), wide, preferred_element_type=jnp.float32)
    part = part + jnp.dot(picked, slots[:, :cols], preferred_element_type=jnp.float32)
    part = part.reshape(chips, dp, shard, cols)
    part = [part[:, t].reshape(chips * shard, cols) for t in range(dp)]
    total = part[0]
    for t in range(1, dp):
        total = total + to_dp(part[t], t)
    total = total.reshape(chips, shard, CORES, cols // CORES).transpose(0, 2, 1, 3)
    total = total.reshape(chips, CORES * shard, cols // CORES)
    pieces = [total[0]] + [to_chip(total[s], s) for s in range(1, chips)]
    pieces = jnp.stack(pieces).reshape(chips, CORES, shard, cols // CORES).transpose(0, 2, 1, 3)
    pieces = pieces.reshape(chips, shard, cols)
    gradient = jnp.concatenate([lax.dynamic_index_in_dim(pieces, z ^ s, 0, keepdims=False) for s in range(chips)], axis=1)
    first_new = 0.9 * first_moment + 0.1 * gradient
    second_new = 0.95 * second_moment + 0.05 * gradient * gradient
    first_hat = first_new / (1.0 - 0.9**STEP)
    second_hat = second_new / (1.0 - 0.95**STEP)
    master_new = master - 0.05 * (first_hat / (jnp.sqrt(second_hat) + 1e-08) + 0.1 * master)
    table = master_new.astype(jnp.bfloat16)
    table = table.reshape(shard, chips, cols).transpose(1, 0, 2).reshape(chips * shard, cols)
    table = jnp.stack([table] + [to_dp(table, t) for t in range(1, dp)])
    table = jnp.stack([lax.dynamic_index_in_dim(table, d ^ t, 0, keepdims=False) for t in range(dp)])
    table = table.reshape(dp, chips, shard, cols).transpose(0, 2, 1, 3).reshape(rows, width)
    return (master_new, first_new, second_new, table)


def local(hidden, logit_grad, predict_mask, slot_grads, *rest):
    vocab = lax.axis_size("vocab")
    fits = hidden.shape[1] % LANES == 0 and logit_grad.shape[1] % 16 == 0
    fits = fits and (vocab // CORES * slot_grads.shape[2]) % 8 == 0
    step = aligned if fits else plain
    return step(hidden, logit_grad, predict_mask, slot_grads, *rest)


def solution(mesh):
    in_specs = (
        P("dp", "vocab"),
        P("dp", "vocab"),
        P("dp"),
        P(("dp", "vocab"), None, None, None),
        P(("dp", "vocab"), None, None),
        P(("dp", "vocab"), None),
        P(("vocab", "dp"), None),
        P(("vocab", "dp"), None),
        P(("vocab", "dp"), None),
    )
    out_specs = (
        P(("vocab", "dp"), None),
        P(("vocab", "dp"), None),
        P(("vocab", "dp"), None),
        P("vocab", None),
    )
    return jax.shard_map(local, mesh=mesh, in_specs=in_specs, out_specs=out_specs, check_vma=False)
```

```python
import functools

import jax
import jax.numpy as jnp
from jax import lax
from jax.experimental import pallas as pl
from jax.experimental.pallas import tpu as pltpu
from jax.sharding import PartitionSpec as P

STEP = 8
CORES = 2
LANES = 128
VMEM_LIMIT = 24 * 1024 * 1024


def place():
    here = lax.axis_index("vocab")
    return lax.axis_index("dp"), lax.shift_right_logical(here, 1), here & 1


def iota(shape, axis):
    return lax.broadcasted_iota(jnp.int32, shape, axis)


def over(x, n):
    return ((x.astype(jnp.float32) + 0.5) * (1.0 / n)).astype(jnp.int32)


def one_hot(flag):
    return jnp.where(flag, 1.0, 0.0).astype(jnp.bfloat16)


def exact(left, right):
    return jnp.dot(left, right, preferred_element_type=jnp.float32)


def slots_kernel(chips, dp, shard, slots_hbm, rows_hbm, counts_hbm, own_out, other_out, slots_ref, rows_ref, counts_ref, sems):
    d, z, core = place()
    copies = [
        pltpu.make_async_copy(rows_hbm, rows_ref, sems.at[0]),
        pltpu.make_async_copy(counts_hbm, counts_ref, sems.at[1]),
        pltpu.make_async_copy(slots_hbm, slots_ref, sems.at[2]),
    ]
    for copy in copies:
        copy.start()
    for copy in copies:
        copy.wait()
    cap, owners = rows_ref.shape[0], rows_ref.shape[2]
    count = cap * owners
    group = cap * chips
    width = slots_ref.shape[1] // chips
    half = chips // 2
    own_lane = iota((count, owners), 1) == iota((count, owners), 0) % owners
    rows = jnp.broadcast_to(rows_ref[...], (cap, owners, owners)).reshape(count, owners)
    rows = jnp.sum(jnp.where(own_lane, rows, 0), axis=1, keepdims=True)
    live = jnp.broadcast_to(counts_ref[...], (count, owners))
    live = jnp.sum(jnp.where(own_lane, live, 0), axis=1, keepdims=True)
    block = over(rows, shard)
    ids = (block ^ d) * shard + rows - block * shard
    ids = jnp.where(over(iota((count, 1), 0), owners) < live, ids, -1)
    ids = jnp.broadcast_to(ids, (count, LANES)).astype(jnp.bfloat16)
    q = iota((CORES * group, count), 0)
    away = jnp.where(q >= group, 1, 0)
    q = q - away * group
    near = jnp.where(q >= group // 2, 1, 0)
    q = q - near * (group // 2)
    slot = over(q, half)
    owner = q - slot * half + (1 - near) * half
    for s in range(chips):
        wanted = slot * owners + (owner ^ z ^ s) * CORES + (away ^ core)
        pick = one_hot(iota((CORES * group, count), 1) == wanted)
        start = pl.multiple_of((z ^ s) * width, LANES)
        values = exact(pick, slots_ref[:, pl.ds(start, width)])
        picked_ids = exact(pick, ids)
        first = s * (width + LANES)
        for out_ref, spot in ((own_out, slice(0, group)), (other_out, slice(group, CORES * group))):
            out_ref[:, first : first + width] = values[spot].astype(jnp.bfloat16)
            out_ref[:, first + width : first + width + LANES] = picked_ids[spot].astype(jnp.bfloat16)


def merge_kernel(chips, own_ref, other_ref, *out_refs):
    size = own_ref.shape[1] // chips
    for s, out_ref in enumerate(out_refs):
        parts = [ref[:, s * size : (s + 1) * size].astype(jnp.float32) for ref in (own_ref, other_ref)]
        out_ref[...] = jnp.concatenate(parts, axis=0).astype(jnp.bfloat16)


def head_kernel(chips, dp, shard, mask_hbm, columns_hbm, hidden_hbm, other_ref, *refs):
    d, z, core = place()
    parts, out_ref = refs[: chips - 1], refs[chips - 1]
    mask_ref, columns_ref, own_ref, sems = refs[chips:]
    copies = [
        pltpu.make_async_copy(mask_hbm, mask_ref, sems.at[0]),
        pltpu.make_async_copy(columns_hbm, columns_ref, sems.at[1]),
        pltpu.make_async_copy(hidden_hbm, own_ref, sems.at[2]),
    ]
    for copy in copies:
        copy.start()
    rows = dp * shard
    total = chips * rows
    cols = other_ref.shape[1]
    half = chips // 2
    r = iota((total, total), 0)
    near = jnp.where(r >= total // 2, 1, 0)
    r = r - near * (total // 2)
    t = over(r, half * shard)
    j = over(r - t * (half * shard), shard)
    i = r - t * (half * shard) - j * shard
    order = one_hot(iota((total, total), 1) == (j + (1 - near) * half) * rows + (t ^ d) * shard + i)
    for copy in copies[:2]:
        copy.wait()
    mask = mask_ref[...].astype(jnp.float32).astype(jnp.bfloat16)
    columns = jnp.concatenate([part[...] for part in (columns_ref, *parts)], axis=0) * mask
    columns = exact(order, columns).astype(jnp.bfloat16)
    out_ref[:, pl.ds(pl.multiple_of((1 - core) * cols, LANES), cols)] = exact(columns, other_ref[...])
    copies[2].wait()
    out_ref[:, pl.ds(pl.multiple_of(core * cols, LANES), cols)] = exact(columns, own_ref[...])


def embed_kernel(chips, dp, shard, head_ref, *refs):
    slot_refs, out_refs = refs[: -2 * dp], refs[-2 * dp :]
    half = chips // 2
    total, cols = head_ref.shape
    size = half * shard
    count = sum(ref.shape[0] for ref in slot_refs)
    ids = jnp.concatenate([ref[:, cols:] for ref in slot_refs], axis=0)
    ids = ids.astype(jnp.float32)[:, :1].astype(jnp.int32)
    values = jnp.concatenate([ref[:, :cols] for ref in slot_refs], axis=0)
    block = over(jnp.maximum(ids, 0), shard)
    group = slot_refs[0].shape[0] // CORES
    place_in = iota((count, 1), 0) % group
    near = jnp.where(place_in >= group // 2, 1, 0)
    target = near * (total // 2) + (block * half + place_in % half) * shard + ids - block * shard
    target = jnp.where(ids < 0, -1, target)
    picked = one_hot(iota((count, total), 1) == target)
    embed = lax.dot_general(picked, values, (((0,), (0,)), ((), ())), preferred_element_type=jnp.float32)
    for n, out_ref in enumerate(out_refs):
        spot = slice(n * size, (n + 1) * size)
        out_ref[...] = head_ref[spot] + embed[spot]


def sum_kernel(half, shard, *refs):
    dp = len(refs) - half
    total = refs[0][...]
    for t in range(1, dp):
        total = total + refs[t][...]
    cut = total.shape[1] // CORES
    for j, out_ref in enumerate(refs[dp:]):
        rows = total[j * shard : (j + 1) * shard]
        out_ref[...] = jnp.concatenate([rows[:, :cut], rows[:, cut:]], axis=0)


def step(shard, spot, piece_ref, master_ref, first_ref, second_ref):
    piece = piece_ref[...]
    gradient = jnp.concatenate([piece[:shard], piece[shard:]], axis=1)
    master = master_ref[:, spot]
    first_new = 0.9 * first_ref[:, spot] + 0.1 * gradient
    second_new = 0.95 * second_ref[:, spot] + 0.05 * gradient * gradient
    first_hat = first_new / (1.0 - 0.9**STEP)
    second_hat = second_new / (1.0 - 0.95**STEP)
    master_new = master - 0.05 * (first_hat / (jnp.sqrt(second_hat) + 1e-08) + 0.1 * master)
    return master_new, first_new, second_new


def chip_spot(z, s, piece_ref):
    cols = piece_ref.shape[1] * CORES
    return pl.ds(pl.multiple_of((z ^ s) * cols, LANES), cols)


def rows_kernel(shard, *refs):
    d, z, core = place()
    state, pieces, out_ref = refs[:3], refs[3:-1], refs[-1]
    table = [step(shard, chip_spot(z, s, piece), piece, *state)[0] for s, piece in enumerate(pieces)]
    out_ref[...] = jnp.concatenate(table, axis=0).astype(jnp.bfloat16)


def adam_kernel(shard, *refs):
    d, z, core = place()
    state, pieces, outs = refs[:3], refs[3:-3], refs[-3:]
    for s, piece in enumerate(pieces):
        spot = chip_spot(z, s, piece)
        for out_ref, value in zip(outs, step(shard, spot, piece, *state)):
            out_ref[:, spot] = value


def table_kernel(chips, dp, shard, *refs):
    d, z, core = place()
    parts, out_ref = refs[:-1], refs[-1]
    cols = parts[0].shape[1]
    rows = dp * shard
    total = chips * rows
    values = jnp.concatenate([part[...] for part in parts], axis=0)
    r = iota((total, total), 0)
    s = over(r, rows)
    e = over(r - s * rows, shard)
    i = r - s * rows - e * shard
    order = one_hot(iota((total, total), 1) == ((e ^ d) * chips + s) * shard + i)
    values = exact(order, values).astype(jnp.bfloat16)
    for s in range(chips):
        spot = pl.ds(pl.multiple_of((z ^ s) * cols, LANES), cols)
        out_ref[:, spot] = values[s * rows : (s + 1) * rows]


def shaped(shape, kind):
    return jax.ShapeDtypeStruct(shape, kind)


def run(kernel, outs, *args, cost=1, hbm=0, scratch=()):
    moved = sum(x.size * x.dtype.itemsize for x in (*args, *jax.tree.leaves(outs)))
    vmem = pl.BlockSpec(memory_space=pltpu.VMEM)
    args = [pltpu.with_memory_space_constraint(x, pltpu.HBM) if n < hbm else x for n, x in enumerate(args)]
    return pl.pallas_call(
        kernel,
        out_shape=outs,
        in_specs=[pl.BlockSpec(memory_space=pltpu.HBM)] * hbm + [vmem] * (len(args) - hbm),
        out_specs=jax.tree.map(lambda _: vmem, outs),
        scratch_shapes=list(scratch),
        cost_estimate=pl.CostEstimate(flops=0, bytes_accessed=moved * cost, transcendentals=0),
        compiler_params=pltpu.CompilerParams(vmem_limit_bytes=VMEM_LIMIT),
    )(*args)


def local_copies(*args):
    return [pltpu.VMEM(x.shape, x.dtype) for x in args] + [pltpu.SemaphoreType.DMA((len(args),))]


def aligned(
    hidden,
    logit_grad,
    predict_mask,
    slot_grads,
    slot_rows,
    slot_counts,
    master,
    first_moment,
    second_moment,
):
    vocab = lax.axis_size("vocab")
    dp = lax.axis_size("dp")
    chips = vocab // CORES
    half = chips // 2
    rows = logit_grad.shape[1]
    shard = master.shape[0]
    cols = hidden.shape[1] * CORES
    owners, cap, width = slot_grads.shape[1:]
    sizes = (chips, dp, shard)
    bf16, f32 = jnp.bfloat16, jnp.float32
    far, near = range(half, chips), range(half)

    def send(x, s, away=0):
        move = s * CORES + away
        return lax.ppermute(x, "vocab", [(v, v ^ move) for v in range(vocab)]) if move else x

    def send_dp(x, t):
        return lax.ppermute(x, "dp", [(i, i ^ t) for i in range(dp)]) if t else x

    hidden_other = send(hidden, 0, 1)
    slots_in = (
        slot_grads[0].transpose(1, 0, 2).reshape(cap * owners, width),
        slot_rows.transpose(2, 0, 1),
        slot_counts,
    )
    slots_own, slots_other = run(
        functools.partial(slots_kernel, *sizes),
        [shaped((cap * chips, chips * (cols + LANES)), bf16)] * CORES,
        *slots_in,
        hbm=3,
        scratch=local_copies(*slots_in),
    )
    slots_other = send(slots_other, 0, 1)
    slots_other, hidden_other = lax.optimization_barrier((slots_other, hidden_other))
    messages = run(
        functools.partial(merge_kernel, chips),
        [shaped((cap * chips * CORES, cols + LANES), bf16)] * chips,
        slots_own,
        slots_other,
    )
    columns = [logit_grad.T]
    for s in range(1, chips):
        if s % 2 and s > 1:
            late = columns[s - 1]
            late, _ = lax.optimization_barrier((late, messages[0]))
            columns.append(send(late, 1))
        else:
            columns.append(send(columns[0], s))
    head_in = (predict_mask[None, :], columns[0], hidden)
    head = run(
        functools.partial(head_kernel, *sizes),
        shaped((chips * rows, cols), f32),
        *head_in,
        hidden_other,
        *columns[1:],
        cost=0,
        hbm=3,
        scratch=local_copies(*head_in),
    )
    state = (master, first_moment, second_moment)
    parts = run(
        functools.partial(embed_kernel, *sizes),
        [shaped((half * shard, cols), f32)] * (2 * dp),
        head,
        *[send(messages[s], s) for s in reversed(range(chips))],
    )
    pieces = {}
    for h, members in enumerate((far, near)):
        heard = [send_dp(parts[h * dp + t], t) for t in range(dp)]
        if h:
            heard[0], _ = lax.optimization_barrier((heard[0], sums[0]))
        sums = run(
            functools.partial(sum_kernel, half, shard),
            [shaped((CORES * shard, cols // CORES), f32)] * half,
            *heard,
        )
        for s, total in zip(members, sums):
            pieces[s] = send(total, s)
    pieces = [pieces[s] for s in range(chips)]
    table = run(
        functools.partial(rows_kernel, shard),
        shaped((chips * shard, cols), bf16),
        *state,
        *pieces,
    )
    master_new, first_new, second_new = run(
        functools.partial(adam_kernel, shard),
        [shaped(master.shape, f32)] * 3,
        *state,
        *pieces,
    )
    table = run(
        functools.partial(table_kernel, *sizes),
        shaped((rows, width), bf16),
        *[send_dp(table, t) for t in range(dp)],
    )
    return (master_new, first_new, second_new, table)


def plain(
    hidden,
    logit_grad,
    predict_mask,
    slot_grads,
    slot_rows,
    slot_counts,
    master,
    first_moment,
    second_moment,
):
    vocab = lax.axis_size("vocab")
    dp = lax.axis_size("dp")
    chips = vocab // CORES
    rows = logit_grad.shape[1]
    shard = master.shape[0]
    cols = hidden.shape[1] * CORES
    owners, cap, width = slot_grads.shape[1:]
    here = lax.axis_index("vocab")
    core = here % CORES
    z = here // CORES
    d = lax.axis_index("dp")

    def to_core(x):
        return lax.ppermute(x, "vocab", [(v, v ^ 1) for v in range(vocab)])

    def to_chip(x, s):
        return lax.ppermute(x, "vocab", [(v, v ^ (s * CORES)) for v in range(vocab)])

    def to_dp(x, t):
        return lax.ppermute(x, "dp", [(i, i ^ t) for i in range(dp)])

    label = jnp.arange(rows, dtype=jnp.int32)
    source = ((label // shard) ^ d) * shard + label % shard
    reorder = (source[:, None] == label[None, :]).astype(jnp.bfloat16)
    masked = logit_grad * predict_mask.astype(jnp.bfloat16)[:, None]
    masked = lax.dot_general(reorder, masked, (((1,), (1,)), ((), ())), preferred_element_type=jnp.bfloat16)

    slot_index = jnp.arange(cap, dtype=jnp.int32)[None, :]
    ids = ((slot_rows[0] // shard) ^ d) * shard + slot_rows[0] % shard
    ids = jnp.where(slot_index < slot_counts[0][:, None], ids, -1).astype(jnp.bfloat16)
    ids = jnp.broadcast_to(ids[:, :, None, None], (owners, cap, chips, LANES))
    slots = slot_grads[0].reshape(owners, cap, chips, cols)
    slots = jnp.concatenate([slots, ids], axis=3).reshape(chips, CORES, cap, chips, cols + LANES)
    mine = lax.dynamic_index_in_dim(slots, core, 1, keepdims=False)
    other = lax.dynamic_index_in_dim(slots, 1 - core, 1, keepdims=False)
    hidden_other = to_core(hidden)
    other = to_core(other)
    masked = [masked] + [to_chip(masked, s) for s in range(1, chips)]
    both = jnp.stack([mine, other]).reshape(CORES * chips * cap, chips, cols + LANES)
    slots = [lax.dynamic_index_in_dim(both, z ^ s, 1, keepdims=False) for s in range(chips)]
    slots = [slots[0]] + [to_chip(slots[s], s) for s in range(1, chips)]

    swap = core == 1
    low = jnp.where(swap, hidden_other, hidden)
    high = jnp.where(swap, hidden, hidden_other)
    wide = jnp.concatenate([low, high], axis=1)
    slots = jnp.concatenate(slots, axis=0)
    owner = (jnp.arange(slots.shape[0], dtype=jnp.int32) // cap) % chips
    ids = slots[:, cols].astype(jnp.int32)
    ids = jnp.where(ids < 0, -1, (owner ^ z) * rows + ids)
    picked = (jnp.arange(chips * rows, dtype=jnp.int32)[:, None] == ids[None, :]).astype(jnp.bfloat16)
    part = jnp.dot(jnp.concatenate(masked, axis=0), wide, preferred_element_type=jnp.float32)
    part = part + jnp.dot(picked, slots[:, :cols], preferred_element_type=jnp.float32)
    part = part.reshape(chips, dp, shard, cols)
    part = [part[:, t].reshape(chips * shard, cols) for t in range(dp)]
    total = part[0]
    for t in range(1, dp):
        total = total + to_dp(part[t], t)
    total = total.reshape(chips, shard, CORES, cols // CORES).transpose(0, 2, 1, 3)
    total = total.reshape(chips, CORES * shard, cols // CORES)
    pieces = [total[0]] + [to_chip(total[s], s) for s in range(1, chips)]
    pieces = jnp.stack(pieces).reshape(chips, CORES, shard, cols // CORES).transpose(0, 2, 1, 3)
    pieces = pieces.reshape(chips, shard, cols)
    gradient = jnp.concatenate([lax.dynamic_index_in_dim(pieces, z ^ s, 0, keepdims=False) for s in range(chips)], axis=1)
    first_new = 0.9 * first_moment + 0.1 * gradient
    second_new = 0.95 * second_moment + 0.05 * gradient * gradient
    first_hat = first_new / (1.0 - 0.9**STEP)
    second_hat = second_new / (1.0 - 0.95**STEP)
    master_new = master - 0.05 * (first_hat / (jnp.sqrt(second_hat) + 1e-08) + 0.1 * master)
    table = master_new.astype(jnp.bfloat16)
    table = table.reshape(shard, chips, cols).transpose(1, 0, 2).reshape(chips * shard, cols)
    table = jnp.stack([table] + [to_dp(table, t) for t in range(1, dp)])
    table = jnp.stack([lax.dynamic_index_in_dim(table, d ^ t, 0, keepdims=False) for t in range(dp)])
    table = table.reshape(dp, chips, shard, cols).transpose(0, 2, 1, 3).reshape(rows, width)
    return (master_new, first_new, second_new, table)


def local(hidden, logit_grad, predict_mask, slot_grads, *rest):
    vocab = lax.axis_size("vocab")
    fits = hidden.shape[1] % LANES == 0 and logit_grad.shape[1] % 16 == 0
    fits = fits and (vocab // CORES * slot_grads.shape[2]) % 8 == 0
    step = aligned if fits else plain
    return step(hidden, logit_grad, predict_mask, slot_grads, *rest)


def solution(mesh):
    in_specs = (
        P("dp", "vocab"),
        P("dp", "vocab"),
        P("dp"),
        P(("dp", "vocab"), None, None, None),
        P(("dp", "vocab"), None, None),
        P(("dp", "vocab"), None),
        P(("vocab", "dp"), None),
        P(("vocab", "dp"), None),
        P(("vocab", "dp"), None),
    )
    out_specs = (
        P(("vocab", "dp"), None),
        P(("vocab", "dp"), None),
        P(("vocab", "dp"), None),
        P("vocab", None),
    )
    return jax.shard_map(local, mesh=mesh, in_specs=in_specs, out_specs=out_specs, check_vma=False)
```

```python
import functools

import jax
import jax.numpy as jnp
from jax import lax
from jax.experimental import pallas as pl
from jax.experimental.pallas import tpu as pltpu
from jax.sharding import PartitionSpec as P

STEP = 8
CORES = 2
LANES = 128
VMEM_LIMIT = 24 * 1024 * 1024


def place():
    here = lax.axis_index("vocab")
    return lax.axis_index("dp"), lax.shift_right_logical(here, 1), here & 1


def iota(shape, axis):
    return lax.broadcasted_iota(jnp.int32, shape, axis)


def over(x, n):
    return ((x.astype(jnp.float32) + 0.5) * (1.0 / n)).astype(jnp.int32)


def one_hot(flag):
    return jnp.where(flag, 1.0, 0.0).astype(jnp.bfloat16)


def exact(left, right):
    return jnp.dot(left, right, preferred_element_type=jnp.float32)


def slots_kernel(chips, slots_hbm, rows_hbm, counts_hbm, own_out, other_out, slots_ref, rows_ref, counts_ref, sems):
    d, z, core = place()
    copies = [
        pltpu.make_async_copy(rows_hbm, rows_ref, sems.at[0]),
        pltpu.make_async_copy(counts_hbm, counts_ref, sems.at[1]),
        pltpu.make_async_copy(slots_hbm, slots_ref, sems.at[2]),
    ]
    for copy in copies:
        copy.start()
    cap, owners = rows_ref.shape[0], rows_ref.shape[2]
    count = cap * owners
    group = cap * chips
    part = slots_ref.shape[1] // 2
    q = iota((count, count), 0)
    away = jnp.where(q >= group, 1, 0)
    q = q - away * group
    s = over(q, cap)
    wanted = (q - s * cap) * owners + (s ^ z) * CORES + (away ^ core)
    pick = one_hot(iota((count, count), 1) == wanted)
    own_lane = iota((count, owners), 1) == iota((count, owners), 0) % owners
    for copy in copies[:2]:
        copy.wait()
    rows = jnp.broadcast_to(rows_ref[...], (cap, owners, owners)).reshape(count, owners)
    rows = jnp.sum(jnp.where(own_lane, rows, 0), axis=1, keepdims=True)
    live = jnp.broadcast_to(counts_ref[...], (count, owners))
    live = jnp.sum(jnp.where(own_lane, live, 0), axis=1, keepdims=True)
    ids = jnp.where(over(iota((count, 1), 0), owners) < live, rows, -1)
    ids = jnp.broadcast_to(ids, (count, LANES)).astype(jnp.bfloat16)
    ids = exact(pick, ids)
    copies[2].wait()
    outs = ((own_out, slice(0, group)), (other_out, slice(group, count)))
    for away in range(2):
        start = pl.multiple_of(((d & 1) ^ away) * part, LANES)
        values = exact(pick, slots_ref[:, pl.ds(start, part)])
        for out_ref, spot in outs:
            out_ref[:, away * part : (away + 1) * part] = values[spot].astype(jnp.bfloat16)
    for out_ref, spot in outs:
        out_ref[:, 2 * part :] = ids[spot].astype(jnp.bfloat16)


def pair_kernel(own_ref, other_ref, out_ref):
    part = out_ref.shape[1] - LANES
    both = [ref[:, part:].astype(jnp.float32) for ref in (own_ref, other_ref)]
    out_ref[...] = jnp.concatenate(both, axis=0).astype(jnp.bfloat16)


def owners_kernel(cap, own_ref, other_ref, pair_ref, *out_refs):
    part = pair_ref.shape[1] - LANES
    group = own_ref.shape[0]
    pair = pair_ref[...].astype(jnp.float32)
    held = [pair[:group], pair[group:]]
    for ref in (own_ref, other_ref):
        values = [ref[:, :part].astype(jnp.float32), ref[:, 2 * part :].astype(jnp.float32)]
        held.append(jnp.concatenate(values, axis=1))
    for s, out_ref in enumerate(out_refs):
        rows = [block[s * cap : (s + 1) * cap] for block in held]
        out_ref[...] = jnp.concatenate(rows, axis=0).astype(jnp.bfloat16)


def head_kernel(chips, dp, shard, mask_hbm, columns_hbm, hidden_hbm, other_ref, *refs):
    d, z, core = place()
    parts, outs = refs[: chips - 1], refs[chips - 1 : chips - 1 + dp]
    mask_ref, columns_ref, own_ref, sems = refs[chips - 1 + dp :]
    copies = [
        pltpu.make_async_copy(mask_hbm, mask_ref, sems.at[0]),
        pltpu.make_async_copy(columns_hbm, columns_ref, sems.at[1]),
        pltpu.make_async_copy(hidden_hbm, own_ref, sems.at[2]),
    ]
    for copy in copies:
        copy.start()
    rows = dp * shard
    total = chips * rows
    cols = other_ref.shape[1]
    size = chips * shard
    r = iota((total, total), 0)
    t = over(r, size)
    s = over(r - t * size, shard)
    i = r - t * size - s * shard
    order = one_hot(iota((total, total), 1) == s * rows + (t ^ d) * shard + i)
    for copy in copies[:2]:
        copy.wait()
    mask = mask_ref[...].astype(jnp.float32).astype(jnp.bfloat16)
    columns = jnp.concatenate([part[...] for part in (columns_ref, *parts)], axis=0) * mask
    columns = exact(order, columns).astype(jnp.bfloat16)
    for at, ref in ((1 - core, other_ref), (core, own_ref)):
        if ref is own_ref:
            copies[2].wait()
        head = exact(columns, ref[...])
        spot = pl.ds(pl.multiple_of(at * cols, LANES), cols)
        for t, out_ref in enumerate(outs):
            out_ref[:, spot] = head[t * size : (t + 1) * size]


def stacked(rows):
    cut = rows.shape[1] // 2
    return jnp.concatenate([rows[:, :cut], rows[:, cut:]], axis=0)


def unstacked(rows):
    cut = rows.shape[0] // 2
    return jnp.concatenate([rows[:cut], rows[cut:]], axis=1)


def embed_kernel(dp, shard, *refs):
    d, z, core = place()
    slot_refs, out_refs = refs[:-dp], refs[-dp:]
    part = slot_refs[0].shape[1] - LANES
    count = sum(ref.shape[0] for ref in slot_refs)
    both = jnp.concatenate([ref[...].astype(jnp.float32) for ref in slot_refs], axis=0)
    ids = both[:, part : part + 1].astype(jnp.int32)
    values = both[:, :part].astype(jnp.bfloat16)
    block = over(jnp.maximum(ids, 0), shard)
    target = jnp.where(ids < 0, -1, (block ^ d) * shard + ids - block * shard)
    picked = one_hot(iota((count, dp * shard), 1) == target)
    embed = lax.dot_general(picked, values, (((0,), (0,)), ((), ())), preferred_element_type=jnp.float32)
    for t, out_ref in enumerate(out_refs):
        out_ref[...] = stacked(embed[t * shard : (t + 1) * shard])


def gather_kernel(*refs):
    d, z, core = place()
    parts, out_ref = refs[:-1], refs[-1]
    part = out_ref.shape[1] // 2
    for side in range(2):
        total = parts[side][...]
        for t in range(side + 2, len(parts), 2):
            total = total + parts[t][...]
        out_ref[:, pl.ds(pl.multiple_of(((d & 1) ^ side) * part, LANES), part)] = unstacked(total)


def sum_kernel(chips, shard, *refs):
    dp = len(refs) - chips
    total = refs[0][...]
    for t in range(1, dp):
        total = total + refs[t][...]
    for s, out_ref in enumerate(refs[dp:]):
        out_ref[...] = stacked(total[s * shard : (s + 1) * shard])


def step(spot, piece_ref, embed_ref, master_ref, first_ref, second_ref):
    gradient = unstacked(piece_ref[...]) + embed_ref[:, spot]
    master = master_ref[:, spot]
    first_new = 0.9 * first_ref[:, spot] + 0.1 * gradient
    second_new = 0.95 * second_ref[:, spot] + 0.05 * gradient * gradient
    first_hat = first_new / (1.0 - 0.9**STEP)
    second_hat = second_new / (1.0 - 0.95**STEP)
    master_new = master - 0.05 * (first_hat / (jnp.sqrt(second_hat) + 1e-08) + 0.1 * master)
    return master_new, first_new, second_new


def chip_spot(z, s, piece_ref):
    cols = piece_ref.shape[1] * 2
    return pl.ds(pl.multiple_of((z ^ s) * cols, LANES), cols)


def rows_kernel(*refs):
    d, z, core = place()
    state, pieces, out_ref = refs[:4], refs[4:-1], refs[-1]
    table = [step(chip_spot(z, s, piece), piece, *state)[0] for s, piece in enumerate(pieces)]
    out_ref[...] = jnp.concatenate(table, axis=0).astype(jnp.bfloat16)


def adam_kernel(*refs):
    d, z, core = place()
    state, pieces, outs = refs[:4], refs[4:-3], refs[-3:]
    for s, piece in enumerate(pieces):
        spot = chip_spot(z, s, piece)
        for out_ref, value in zip(outs, step(spot, piece, *state)):
            out_ref[:, spot] = value


def table_kernel(chips, dp, shard, *refs):
    d, z, core = place()
    parts, out_ref = refs[:-1], refs[-1]
    cols = parts[0].shape[1]
    rows = dp * shard
    total = chips * rows
    values = jnp.concatenate([part[...] for part in parts], axis=0)
    r = iota((total, total), 0)
    s = over(r, rows)
    e = over(r - s * rows, shard)
    i = r - s * rows - e * shard
    order = one_hot(iota((total, total), 1) == ((e ^ d) * chips + s) * shard + i)
    values = exact(order, values).astype(jnp.bfloat16)
    for s in range(chips):
        spot = pl.ds(pl.multiple_of((z ^ s) * cols, LANES), cols)
        out_ref[:, spot] = values[s * rows : (s + 1) * rows]


def shaped(shape, kind):
    return jax.ShapeDtypeStruct(shape, kind)


def run(kernel, outs, *args, cost=1, hbm=0, scratch=()):
    moved = sum(x.size * x.dtype.itemsize for x in (*args, *jax.tree.leaves(outs)))
    vmem = pl.BlockSpec(memory_space=pltpu.VMEM)
    args = [pltpu.with_memory_space_constraint(x, pltpu.HBM) if n < hbm else x for n, x in enumerate(args)]
    return pl.pallas_call(
        kernel,
        out_shape=outs,
        in_specs=[pl.BlockSpec(memory_space=pltpu.HBM)] * hbm + [vmem] * (len(args) - hbm),
        out_specs=jax.tree.map(lambda _: vmem, outs),
        scratch_shapes=list(scratch),
        cost_estimate=pl.CostEstimate(flops=0, bytes_accessed=moved * cost, transcendentals=0),
        compiler_params=pltpu.CompilerParams(vmem_limit_bytes=VMEM_LIMIT),
    )(*args)


def local_copies(*args):
    return [pltpu.VMEM(x.shape, x.dtype) for x in args] + [pltpu.SemaphoreType.DMA((len(args),))]


def aligned(
    hidden,
    logit_grad,
    predict_mask,
    slot_grads,
    slot_rows,
    slot_counts,
    master,
    first_moment,
    second_moment,
):
    vocab = lax.axis_size("vocab")
    dp = lax.axis_size("dp")
    chips = vocab // CORES
    rows = logit_grad.shape[1]
    shard = master.shape[0]
    cols = hidden.shape[1] * CORES
    owners, cap, width = slot_grads.shape[1:]
    group = cap * chips
    bf16, f32 = jnp.bfloat16, jnp.float32

    def send(x, s, away=0):
        move = s * CORES + away
        return lax.ppermute(x, "vocab", [(v, v ^ move) for v in range(vocab)]) if move else x

    def send_dp(x, t):
        return lax.ppermute(x, "dp", [(i, i ^ t) for i in range(dp)]) if t else x

    hidden_other = send(hidden, 0, 1)
    slots_in = (
        slot_grads[0].transpose(1, 0, 2).reshape(cap * owners, width),
        slot_rows.transpose(2, 0, 1),
        slot_counts,
    )
    slots_own, slots_other = run(
        functools.partial(slots_kernel, chips),
        [shaped((group, width + LANES), bf16)] * CORES,
        *slots_in,
        hbm=3,
        scratch=local_copies(*slots_in),
    )
    slots_other = send(slots_other, 0, 1)
    slots_pair = send_dp(run(pair_kernel, shaped((CORES * group, width // 2 + LANES), bf16), slots_own, slots_other), 1)
    messages = run(
        functools.partial(owners_kernel, cap),
        [shaped((2 * CORES * cap, width // 2 + LANES), bf16)] * chips,
        slots_own,
        slots_other,
        slots_pair,
    )
    columns = [logit_grad.T]
    for s in range(1, chips):
        columns.append(send(columns[s - 1], 1) if s % 2 else send(columns[0], s))
    head_in = (predict_mask[None, :], columns[0], hidden)
    head = run(
        functools.partial(head_kernel, chips, dp, shard),
        [shaped((chips * shard, cols), f32)] * dp,
        *head_in,
        hidden_other,
        *columns[1:],
        hbm=3,
        scratch=local_copies(*head_in),
    )
    embed = run(
        functools.partial(embed_kernel, dp, shard),
        [shaped((2 * shard, width // 4), f32)] * dp,
        *[send(messages[s], s) for s in reversed(range(chips))],
    )
    sums = run(
        functools.partial(sum_kernel, chips, shard),
        [shaped((2 * shard, cols // 2), f32)] * chips,
        *[send_dp(head[t], t) for t in range(dp)],
    )
    pieces = [send(sums[s], s) for s in range(chips)]
    embed = run(gather_kernel, shaped((shard, width), f32), *[send_dp(embed[t], t) for t in range(dp)])
    state = (embed, master, first_moment, second_moment)
    table = run(rows_kernel, shaped((chips * shard, cols), bf16), *state, *pieces)
    master_new, first_new, second_new = run(adam_kernel, [shaped(master.shape, f32)] * 3, *state, *pieces)
    table = run(
        functools.partial(table_kernel, chips, dp, shard),
        shaped((rows, width), bf16),
        *[send_dp(table, t) for t in range(dp)],
    )
    return (master_new, first_new, second_new, table)


def plain(
    hidden,
    logit_grad,
    predict_mask,
    slot_grads,
    slot_rows,
    slot_counts,
    master,
    first_moment,
    second_moment,
):
    vocab = lax.axis_size("vocab")
    dp = lax.axis_size("dp")
    chips = vocab // CORES
    rows = logit_grad.shape[1]
    shard = master.shape[0]
    cols = hidden.shape[1] * CORES
    owners, cap, width = slot_grads.shape[1:]
    here = lax.axis_index("vocab")
    core = here % CORES
    z = here // CORES
    d = lax.axis_index("dp")

    def to_core(x):
        return lax.ppermute(x, "vocab", [(v, v ^ 1) for v in range(vocab)])

    def to_chip(x, s):
        return lax.ppermute(x, "vocab", [(v, v ^ (s * CORES)) for v in range(vocab)])

    def to_dp(x, t):
        return lax.ppermute(x, "dp", [(i, i ^ t) for i in range(dp)])

    label = jnp.arange(rows, dtype=jnp.int32)
    source = ((label // shard) ^ d) * shard + label % shard
    reorder = (source[:, None] == label[None, :]).astype(jnp.bfloat16)
    masked = logit_grad * predict_mask.astype(jnp.bfloat16)[:, None]
    masked = lax.dot_general(reorder, masked, (((1,), (1,)), ((), ())), preferred_element_type=jnp.bfloat16)

    slot_index = jnp.arange(cap, dtype=jnp.int32)[None, :]
    ids = ((slot_rows[0] // shard) ^ d) * shard + slot_rows[0] % shard
    ids = jnp.where(slot_index < slot_counts[0][:, None], ids, -1).astype(jnp.bfloat16)
    ids = jnp.broadcast_to(ids[:, :, None, None], (owners, cap, chips, LANES))
    slots = slot_grads[0].reshape(owners, cap, chips, cols)
    slots = jnp.concatenate([slots, ids], axis=3).reshape(chips, CORES, cap, chips, cols + LANES)
    mine = lax.dynamic_index_in_dim(slots, core, 1, keepdims=False)
    other = lax.dynamic_index_in_dim(slots, 1 - core, 1, keepdims=False)
    hidden_other = to_core(hidden)
    other = to_core(other)
    masked = [masked] + [to_chip(masked, s) for s in range(1, chips)]
    both = jnp.stack([mine, other]).reshape(CORES * chips * cap, chips, cols + LANES)
    slots = [lax.dynamic_index_in_dim(both, z ^ s, 1, keepdims=False) for s in range(chips)]
    slots = [slots[0]] + [to_chip(slots[s], s) for s in range(1, chips)]

    swap = core == 1
    low = jnp.where(swap, hidden_other, hidden)
    high = jnp.where(swap, hidden, hidden_other)
    wide = jnp.concatenate([low, high], axis=1)
    slots = jnp.concatenate(slots, axis=0)
    owner = (jnp.arange(slots.shape[0], dtype=jnp.int32) // cap) % chips
    ids = slots[:, cols].astype(jnp.int32)
    ids = jnp.where(ids < 0, -1, (owner ^ z) * rows + ids)
    picked = (jnp.arange(chips * rows, dtype=jnp.int32)[:, None] == ids[None, :]).astype(jnp.bfloat16)
    part = jnp.dot(jnp.concatenate(masked, axis=0), wide, preferred_element_type=jnp.float32)
    part = part + jnp.dot(picked, slots[:, :cols], preferred_element_type=jnp.float32)
    part = part.reshape(chips, dp, shard, cols)
    part = [part[:, t].reshape(chips * shard, cols) for t in range(dp)]
    total = part[0]
    for t in range(1, dp):
        total = total + to_dp(part[t], t)
    total = total.reshape(chips, shard, CORES, cols // CORES).transpose(0, 2, 1, 3)
    total = total.reshape(chips, CORES * shard, cols // CORES)
    pieces = [total[0]] + [to_chip(total[s], s) for s in range(1, chips)]
    pieces = jnp.stack(pieces).reshape(chips, CORES, shard, cols // CORES).transpose(0, 2, 1, 3)
    pieces = pieces.reshape(chips, shard, cols)
    gradient = jnp.concatenate([lax.dynamic_index_in_dim(pieces, z ^ s, 0, keepdims=False) for s in range(chips)], axis=1)
    first_new = 0.9 * first_moment + 0.1 * gradient
    second_new = 0.95 * second_moment + 0.05 * gradient * gradient
    first_hat = first_new / (1.0 - 0.9**STEP)
    second_hat = second_new / (1.0 - 0.95**STEP)
    master_new = master - 0.05 * (first_hat / (jnp.sqrt(second_hat) + 1e-08) + 0.1 * master)
    table = master_new.astype(jnp.bfloat16)
    table = table.reshape(shard, chips, cols).transpose(1, 0, 2).reshape(chips * shard, cols)
    table = jnp.stack([table] + [to_dp(table, t) for t in range(1, dp)])
    table = jnp.stack([lax.dynamic_index_in_dim(table, d ^ t, 0, keepdims=False) for t in range(dp)])
    table = table.reshape(dp, chips, shard, cols).transpose(0, 2, 1, 3).reshape(rows, width)
    return (master_new, first_new, second_new, table)


def local(hidden, logit_grad, predict_mask, slot_grads, *rest):
    vocab = lax.axis_size("vocab")
    fits = hidden.shape[1] % LANES == 0 and logit_grad.shape[1] % 16 == 0
    fits = fits and (vocab // CORES * slot_grads.shape[2]) % 8 == 0 and lax.axis_size("dp") % 2 == 0
    step = aligned if fits else plain
    return step(hidden, logit_grad, predict_mask, slot_grads, *rest)


def solution(mesh):
    in_specs = (
        P("dp", "vocab"),
        P("dp", "vocab"),
        P("dp"),
        P(("dp", "vocab"), None, None, None),
        P(("dp", "vocab"), None, None),
        P(("dp", "vocab"), None),
        P(("vocab", "dp"), None),
        P(("vocab", "dp"), None),
        P(("vocab", "dp"), None),
    )
    out_specs = (
        P(("vocab", "dp"), None),
        P(("vocab", "dp"), None),
        P(("vocab", "dp"), None),
        P("vocab", None),
    )
    return jax.shard_map(local, mesh=mesh, in_specs=in_specs, out_specs=out_specs, check_vma=False)
```

```python
import functools

import jax
import jax.numpy as jnp
from jax import lax
from jax.experimental import pallas as pl
from jax.experimental.pallas import tpu as pltpu
from jax.sharding import PartitionSpec as P

STEP = 8
CORES = 2
LANES = 128
ID_ROWS = 16
VMEM_LIMIT = 24 * 1024 * 1024


def place():
    here = lax.axis_index("vocab")
    return lax.axis_index("dp"), lax.shift_right_logical(here, 1), here & 1


def iota(shape, axis):
    return lax.broadcasted_iota(jnp.int32, shape, axis)


def over(x, n):
    return ((x.astype(jnp.float32) + 0.5) * (1.0 / n)).astype(jnp.int32)


def one_hot(flag):
    return jnp.where(flag, 1.0, 0.0).astype(jnp.bfloat16)


def exact(left, right):
    return jnp.dot(left, right, preferred_element_type=jnp.float32)


def slots_kernel(chips, dp, shard, slots_hbm, rows_hbm, counts_hbm, own_out, other_out, slots_ref, rows_ref, counts_ref, sems):
    d, z, core = place()
    copies = [
        pltpu.make_async_copy(rows_hbm, rows_ref, sems.at[0]),
        pltpu.make_async_copy(counts_hbm, counts_ref, sems.at[1]),
        pltpu.make_async_copy(slots_hbm, slots_ref, sems.at[2]),
    ]
    for copy in copies:
        copy.start()
    cap, owners = rows_ref.shape[0], rows_ref.shape[2]
    count = cap * owners
    group = cap * chips
    width = slots_ref.shape[1] // chips
    half = chips // 2
    q = iota((count, count), 0)
    away = jnp.where(q >= group, 1, 0)
    q = q - away * group
    near = jnp.where(q >= group // 2, 1, 0)
    q = q - near * (group // 2)
    slot = over(q, half)
    owner = q - slot * half + (1 - near) * half
    picks = [
        one_hot(iota((count, count), 1) == slot * owners + (owner ^ z ^ s) * CORES + (away ^ core))
        for s in range(chips)
    ]
    own_lane = iota((count, owners), 1) == iota((count, owners), 0) % owners
    for copy in copies[:2]:
        copy.wait()
    rows = jnp.broadcast_to(rows_ref[...], (cap, owners, owners)).reshape(count, owners)
    rows = jnp.sum(jnp.where(own_lane, rows, 0), axis=1, keepdims=True)
    live = jnp.broadcast_to(counts_ref[...], (count, owners))
    live = jnp.sum(jnp.where(own_lane, live, 0), axis=1, keepdims=True)
    block = over(rows, shard)
    ids = (block ^ d) * shard + rows - block * shard
    ids = jnp.where(over(iota((count, 1), 0), owners) < live, ids, -1)
    ids = jnp.broadcast_to(ids, (count, LANES)).astype(jnp.bfloat16)
    copies[2].wait()
    for s, pick in enumerate(picks):
        start = pl.multiple_of((z ^ s) * width, LANES)
        values = exact(pick, slots_ref[:, pl.ds(start, width)])
        picked_ids = exact(pick, ids)
        first = s * (width + LANES)
        for out_ref, spot in ((own_out, slice(0, group)), (other_out, slice(group, count))):
            out_ref[:, first : first + width] = values[spot].astype(jnp.bfloat16)
            out_ref[:, first + width : first + width + LANES] = picked_ids[spot].astype(jnp.bfloat16)


def diagonal(values, axis):
    return jnp.sum(jnp.where(iota(values.shape, 0) == iota(values.shape, 1), values, 0.0), axis=axis, keepdims=True)


def merge_kernel(chips, hidden_hbm, own_ref, other_ref, *refs):
    out_refs, hidden_ref, sems = refs[:chips], refs[chips], refs[-1]
    copy = pltpu.make_async_copy(hidden_hbm, hidden_ref, sems.at[0])
    copy.start()
    size = own_ref.shape[1] // chips
    width = size - LANES
    for s, out_ref in enumerate(out_refs):
        parts = [ref[:, s * size : (s + 1) * size].astype(jnp.float32) for ref in (own_ref, other_ref)]
        both = jnp.concatenate(parts, axis=0)
        ids = jnp.broadcast_to(diagonal(both[:, width:], 0), (ID_ROWS, LANES))
        blocks = [both[:, c : c + LANES] for c in range(0, width, LANES)]
        out_ref[...] = jnp.concatenate([*blocks, ids], axis=0).astype(jnp.bfloat16)
    copy.wait()


def head_kernel(chips, dp, shard, mask_ref, own_ref, other_ref, *refs):
    d, z, core = place()
    parts, out_ref = refs[:-1], refs[-1]
    rows = dp * shard
    total = chips * rows
    cols = own_ref.shape[1]
    half = chips // 2
    mask = mask_ref[...].astype(jnp.float32).astype(jnp.bfloat16)
    columns = jnp.concatenate([part[...] for part in parts], axis=0) * mask
    r = iota((total, total), 0)
    near = jnp.where(r >= total // 2, 1, 0)
    r = r - near * (total // 2)
    t = over(r, half * shard)
    j = over(r - t * (half * shard), shard)
    i = r - t * (half * shard) - j * shard
    order = one_hot(iota((total, total), 1) == (j + (1 - near) * half) * rows + (t ^ d) * shard + i)
    columns = exact(order, columns).astype(jnp.bfloat16)
    for at, ref in ((core, own_ref), (1 - core, other_ref)):
        out_ref[:, pl.ds(pl.multiple_of(at * cols, LANES), cols)] = exact(columns, ref[...])


def embed_kernel(chips, dp, shard, head_ref, *refs):
    slot_refs, out_refs = refs[: -2 * dp], refs[-2 * dp :]
    half = chips // 2
    total, cols = head_ref.shape
    size = half * shard
    group = (slot_refs[0].shape[0] - ID_ROWS) // (cols // LANES)
    count = len(slot_refs) * group
    ids, values = [], []
    for ref in slot_refs:
        row = ref[cols // LANES * group :, :].astype(jnp.float32)[:1]
        ids.append(diagonal(jnp.broadcast_to(row, (group, LANES)), 1))
        blocks = [ref[c * group : (c + 1) * group, :] for c in range(cols // LANES)]
        values.append(jnp.concatenate(blocks, axis=1))
    ids = jnp.concatenate(ids, axis=0).astype(jnp.int32)
    values = jnp.concatenate(values, axis=0)
    block = over(jnp.maximum(ids, 0), shard)
    place_in = iota((count, 1), 0) % (group // CORES)
    near = jnp.where(place_in >= group // (2 * CORES), 1, 0)
    target = near * (total // 2) + (block * half + place_in % half) * shard + ids - block * shard
    target = jnp.where(ids < 0, -1, target)
    picked = one_hot(iota((count, total), 1) == target)
    embed = lax.dot_general(picked, values, (((0,), (0,)), ((), ())), preferred_element_type=jnp.float32)
    for n, out_ref in enumerate(out_refs):
        spot = slice(n * size, (n + 1) * size)
        out_ref[...] = head_ref[spot] + embed[spot]


def sum_kernel(half, shard, *refs):
    dp = len(refs) - half
    total = refs[0][...]
    for t in range(1, dp):
        total = total + refs[t][...]
    cut = total.shape[1] // CORES
    for j, out_ref in enumerate(refs[dp:]):
        rows = total[j * shard : (j + 1) * shard]
        out_ref[...] = jnp.concatenate([rows[:, :cut], rows[:, cut:]], axis=0)


def step(shard, spot, piece_ref, master_ref, first_ref, second_ref):
    piece = piece_ref[...]
    gradient = jnp.concatenate([piece[:shard], piece[shard:]], axis=1)
    master = master_ref[:, spot]
    first_new = 0.9 * first_ref[:, spot] + 0.1 * gradient
    second_new = 0.95 * second_ref[:, spot] + 0.05 * gradient * gradient
    first_hat = first_new / (1.0 - 0.9**STEP)
    second_hat = second_new / (1.0 - 0.95**STEP)
    master_new = master - 0.05 * (first_hat / (jnp.sqrt(second_hat) + 1e-08) + 0.1 * master)
    return master_new, first_new, second_new


def chip_spot(z, s, piece_ref):
    cols = piece_ref.shape[1] * CORES
    return pl.ds(pl.multiple_of((z ^ s) * cols, LANES), cols)


def rows_kernel(shard, *refs):
    d, z, core = place()
    state, pieces, out_ref = refs[:3], refs[3:-1], refs[-1]
    table = [step(shard, chip_spot(z, s, piece), piece, *state)[0] for s, piece in enumerate(pieces)]
    out_ref[...] = jnp.concatenate(table, axis=0).astype(jnp.bfloat16)


def adam_kernel(shard, *refs):
    d, z, core = place()
    state, pieces, outs = refs[:3], refs[3:-3], refs[-3:]
    for s, piece in enumerate(pieces):
        spot = chip_spot(z, s, piece)
        for out_ref, value in zip(outs, step(shard, spot, piece, *state)):
            out_ref[:, spot] = value


def table_kernel(chips, dp, shard, *refs):
    d, z, core = place()
    parts, out_ref = refs[:-1], refs[-1]
    cols = parts[0].shape[1]
    rows = dp * shard
    total = chips * rows
    values = jnp.concatenate([part[...] for part in parts], axis=0)
    r = iota((total, total), 0)
    s = over(r, rows)
    e = over(r - s * rows, shard)
    i = r - s * rows - e * shard
    order = one_hot(iota((total, total), 1) == ((e ^ d) * chips + s) * shard + i)
    values = exact(order, values).astype(jnp.bfloat16)
    for s in range(chips):
        spot = pl.ds(pl.multiple_of((z ^ s) * cols, LANES), cols)
        out_ref[:, spot] = values[s * rows : (s + 1) * rows]


def shaped(shape, kind):
    return jax.ShapeDtypeStruct(shape, kind)


def run(kernel, outs, *args, cost=1, hbm=0, scratch=()):
    moved = sum(x.size * x.dtype.itemsize for x in (*args, *jax.tree.leaves(outs)))
    vmem = pl.BlockSpec(memory_space=pltpu.VMEM)
    args = [pltpu.with_memory_space_constraint(x, pltpu.HBM) if n < hbm else x for n, x in enumerate(args)]
    return pl.pallas_call(
        kernel,
        out_shape=outs,
        in_specs=[pl.BlockSpec(memory_space=pltpu.HBM)] * hbm + [vmem] * (len(args) - hbm),
        out_specs=jax.tree.map(lambda _: vmem, outs),
        scratch_shapes=list(scratch),
        cost_estimate=pl.CostEstimate(flops=0, bytes_accessed=moved * cost, transcendentals=0),
        compiler_params=pltpu.CompilerParams(vmem_limit_bytes=VMEM_LIMIT),
    )(*args)


def local_copies(*args):
    return [pltpu.VMEM(x.shape, x.dtype) for x in args] + [pltpu.SemaphoreType.DMA((len(args),))]


def aligned(
    hidden,
    logit_grad,
    predict_mask,
    slot_grads,
    slot_rows,
    slot_counts,
    master,
    first_moment,
    second_moment,
):
    vocab = lax.axis_size("vocab")
    dp = lax.axis_size("dp")
    chips = vocab // CORES
    half = chips // 2
    rows = logit_grad.shape[1]
    shard = master.shape[0]
    cols = hidden.shape[1] * CORES
    owners, cap, width = slot_grads.shape[1:]
    sizes = (chips, dp, shard)
    bf16, f32 = jnp.bfloat16, jnp.float32
    far, near = range(half, chips), range(half)

    def send(x, s, away=0):
        move = s * CORES + away
        return lax.ppermute(x, "vocab", [(v, v ^ move) for v in range(vocab)]) if move else x

    def send_dp(x, t):
        return lax.ppermute(x, "dp", [(i, i ^ t) for i in range(dp)]) if t else x

    hidden_other = send(hidden, 0, 1)
    slots_in = (
        slot_grads[0].transpose(1, 0, 2).reshape(cap * owners, width),
        slot_rows.transpose(2, 0, 1),
        slot_counts,
    )
    slots_own, slots_other = run(
        functools.partial(slots_kernel, *sizes),
        [shaped((cap * chips, chips * (cols + LANES)), bf16)] * CORES,
        *slots_in,
        hbm=3,
        scratch=local_copies(*slots_in),
    )
    slots_other = send(slots_other, 0, 1)
    slots_other, hidden_other = lax.optimization_barrier((slots_other, hidden_other))
    slots = cap * chips * CORES
    *messages, held = run(
        functools.partial(merge_kernel, chips),
        [shaped((slots * cols // LANES + ID_ROWS, LANES), bf16)] * chips + [shaped(hidden.shape, bf16)],
        hidden,
        slots_own,
        slots_other,
        hbm=1,
        scratch=[pltpu.SemaphoreType.DMA((1,))],
    )
    columns = [logit_grad.T]
    for s in range(1, chips):
        if s % 2 and s > 1:
            late = columns[s - 1]
            late, _ = lax.optimization_barrier((late, messages[0]))
            columns.append(send(late, 1))
        else:
            columns.append(send(columns[0], s))
    head = run(
        functools.partial(head_kernel, *sizes),
        shaped((chips * rows, cols), f32),
        predict_mask[None, :],
        held,
        hidden_other,
        *columns,
        cost=0,
    )
    state = (master, first_moment, second_moment)
    parts = run(
        functools.partial(embed_kernel, *sizes),
        [shaped((half * shard, cols), f32)] * (2 * dp),
        head,
        *[send(messages[s], s) for s in reversed(range(chips))],
    )
    pieces = {}
    for h, members in enumerate((far, near)):
        heard = [send_dp(parts[h * dp + t], t) for t in range(dp)]
        if h:
            heard[0], _ = lax.optimization_barrier((heard[0], sums[0]))
        sums = run(
            functools.partial(sum_kernel, half, shard),
            [shaped((CORES * shard, cols // CORES), f32)] * half,
            *heard,
        )
        for s, total in zip(members, sums):
            pieces[s] = send(total, s)
    pieces = [pieces[s] for s in range(chips)]
    table = run(
        functools.partial(rows_kernel, shard),
        shaped((chips * shard, cols), bf16),
        *state,
        *pieces,
    )
    master_new, first_new, second_new = run(
        functools.partial(adam_kernel, shard),
        [shaped(master.shape, f32)] * 3,
        *state,
        *pieces,
    )
    table = run(
        functools.partial(table_kernel, *sizes),
        shaped((rows, width), bf16),
        *[send_dp(table, t) for t in range(dp)],
    )
    return (master_new, first_new, second_new, table)


def plain(
    hidden,
    logit_grad,
    predict_mask,
    slot_grads,
    slot_rows,
    slot_counts,
    master,
    first_moment,
    second_moment,
):
    vocab = lax.axis_size("vocab")
    dp = lax.axis_size("dp")
    chips = vocab // CORES
    rows = logit_grad.shape[1]
    shard = master.shape[0]
    cols = hidden.shape[1] * CORES
    owners, cap, width = slot_grads.shape[1:]
    here = lax.axis_index("vocab")
    core = here % CORES
    z = here // CORES
    d = lax.axis_index("dp")

    def to_core(x):
        return lax.ppermute(x, "vocab", [(v, v ^ 1) for v in range(vocab)])

    def to_chip(x, s):
        return lax.ppermute(x, "vocab", [(v, v ^ (s * CORES)) for v in range(vocab)])

    def to_dp(x, t):
        return lax.ppermute(x, "dp", [(i, i ^ t) for i in range(dp)])

    label = jnp.arange(rows, dtype=jnp.int32)
    source = ((label // shard) ^ d) * shard + label % shard
    reorder = (source[:, None] == label[None, :]).astype(jnp.bfloat16)
    masked = logit_grad * predict_mask.astype(jnp.bfloat16)[:, None]
    masked = lax.dot_general(reorder, masked, (((1,), (1,)), ((), ())), preferred_element_type=jnp.bfloat16)

    slot_index = jnp.arange(cap, dtype=jnp.int32)[None, :]
    ids = ((slot_rows[0] // shard) ^ d) * shard + slot_rows[0] % shard
    ids = jnp.where(slot_index < slot_counts[0][:, None], ids, -1).astype(jnp.bfloat16)
    ids = jnp.broadcast_to(ids[:, :, None, None], (owners, cap, chips, LANES))
    slots = slot_grads[0].reshape(owners, cap, chips, cols)
    slots = jnp.concatenate([slots, ids], axis=3).reshape(chips, CORES, cap, chips, cols + LANES)
    mine = lax.dynamic_index_in_dim(slots, core, 1, keepdims=False)
    other = lax.dynamic_index_in_dim(slots, 1 - core, 1, keepdims=False)
    hidden_other = to_core(hidden)
    other = to_core(other)
    masked = [masked] + [to_chip(masked, s) for s in range(1, chips)]
    both = jnp.stack([mine, other]).reshape(CORES * chips * cap, chips, cols + LANES)
    slots = [lax.dynamic_index_in_dim(both, z ^ s, 1, keepdims=False) for s in range(chips)]
    slots = [slots[0]] + [to_chip(slots[s], s) for s in range(1, chips)]

    swap = core == 1
    low = jnp.where(swap, hidden_other, hidden)
    high = jnp.where(swap, hidden, hidden_other)
    wide = jnp.concatenate([low, high], axis=1)
    slots = jnp.concatenate(slots, axis=0)
    owner = (jnp.arange(slots.shape[0], dtype=jnp.int32) // cap) % chips
    ids = slots[:, cols].astype(jnp.int32)
    ids = jnp.where(ids < 0, -1, (owner ^ z) * rows + ids)
    picked = (jnp.arange(chips * rows, dtype=jnp.int32)[:, None] == ids[None, :]).astype(jnp.bfloat16)
    part = jnp.dot(jnp.concatenate(masked, axis=0), wide, preferred_element_type=jnp.float32)
    part = part + jnp.dot(picked, slots[:, :cols], preferred_element_type=jnp.float32)
    part = part.reshape(chips, dp, shard, cols)
    part = [part[:, t].reshape(chips * shard, cols) for t in range(dp)]
    total = part[0]
    for t in range(1, dp):
        total = total + to_dp(part[t], t)
    total = total.reshape(chips, shard, CORES, cols // CORES).transpose(0, 2, 1, 3)
    total = total.reshape(chips, CORES * shard, cols // CORES)
    pieces = [total[0]] + [to_chip(total[s], s) for s in range(1, chips)]
    pieces = jnp.stack(pieces).reshape(chips, CORES, shard, cols // CORES).transpose(0, 2, 1, 3)
    pieces = pieces.reshape(chips, shard, cols)
    gradient = jnp.concatenate([lax.dynamic_index_in_dim(pieces, z ^ s, 0, keepdims=False) for s in range(chips)], axis=1)
    first_new = 0.9 * first_moment + 0.1 * gradient
    second_new = 0.95 * second_moment + 0.05 * gradient * gradient
    first_hat = first_new / (1.0 - 0.9**STEP)
    second_hat = second_new / (1.0 - 0.95**STEP)
    master_new = master - 0.05 * (first_hat / (jnp.sqrt(second_hat) + 1e-08) + 0.1 * master)
    table = master_new.astype(jnp.bfloat16)
    table = table.reshape(shard, chips, cols).transpose(1, 0, 2).reshape(chips * shard, cols)
    table = jnp.stack([table] + [to_dp(table, t) for t in range(1, dp)])
    table = jnp.stack([lax.dynamic_index_in_dim(table, d ^ t, 0, keepdims=False) for t in range(dp)])
    table = table.reshape(dp, chips, shard, cols).transpose(0, 2, 1, 3).reshape(rows, width)
    return (master_new, first_new, second_new, table)


def local(hidden, logit_grad, predict_mask, slot_grads, *rest):
    vocab = lax.axis_size("vocab")
    fits = hidden.shape[1] % LANES == 0 and logit_grad.shape[1] % 16 == 0
    slots = vocab * slot_grads.shape[2]
    fits = fits and slots % 16 == 0 and slots <= LANES
    step = aligned if fits else plain
    return step(hidden, logit_grad, predict_mask, slot_grads, *rest)


def solution(mesh):
    in_specs = (
        P("dp", "vocab"),
        P("dp", "vocab"),
        P("dp"),
        P(("dp", "vocab"), None, None, None),
        P(("dp", "vocab"), None, None),
        P(("dp", "vocab"), None),
        P(("vocab", "dp"), None),
        P(("vocab", "dp"), None),
        P(("vocab", "dp"), None),
    )
    out_specs = (
        P(("vocab", "dp"), None),
        P(("vocab", "dp"), None),
        P(("vocab", "dp"), None),
        P("vocab", None),
    )
    return jax.shard_map(local, mesh=mesh, in_specs=in_specs, out_specs=out_specs, check_vma=False)
```

```python
import functools

import jax
import jax.numpy as jnp
from jax import lax
from jax.experimental import pallas as pl
from jax.experimental.pallas import tpu as pltpu
from jax.sharding import PartitionSpec as P

STEP = 8
CORES = 2
LANES = 128
ID_ROWS = 16
VMEM_LIMIT = 24 * 1024 * 1024


def place():
    here = lax.axis_index("vocab")
    return lax.axis_index("dp"), lax.shift_right_logical(here, 1), here & 1


def iota(shape, axis):
    return lax.broadcasted_iota(jnp.int32, shape, axis)


def over(x, n):
    return ((x.astype(jnp.float32) + 0.5) * (1.0 / n)).astype(jnp.int32)


def one_hot(flag):
    return jnp.where(flag, 1.0, 0.0).astype(jnp.bfloat16)


def exact(left, right):
    return jnp.dot(left, right, preferred_element_type=jnp.float32)


def slots_kernel(chips, dp, slots_hbm, rows_hbm, counts_hbm, own_out, other_out, slots_ref, rows_ref, counts_ref, sems):
    d, z, core = place()
    copies = [
        pltpu.make_async_copy(rows_hbm, rows_ref, sems.at[0]),
        pltpu.make_async_copy(counts_hbm, counts_ref, sems.at[1]),
        pltpu.make_async_copy(slots_hbm, slots_ref, sems.at[2]),
    ]
    for copy in copies:
        copy.start()
    cap, owners = rows_ref.shape[0], rows_ref.shape[2]
    count = cap * owners
    group = cap * chips
    part = slots_ref.shape[1] // dp
    q = iota((count, count), 0)
    away = jnp.where(q >= group, 1, 0)
    q = q - away * group
    s = over(q, cap)
    wanted = (q - s * cap) * owners + (s ^ z) * CORES + (away ^ core)
    pick = one_hot(iota((count, count), 1) == wanted)
    own_lane = iota((count, owners), 1) == iota((count, owners), 0) % owners
    for copy in copies[:2]:
        copy.wait()
    rows = jnp.broadcast_to(rows_ref[...], (cap, owners, owners)).reshape(count, owners)
    rows = jnp.sum(jnp.where(own_lane, rows, 0), axis=1, keepdims=True)
    live = jnp.broadcast_to(counts_ref[...], (count, owners))
    live = jnp.sum(jnp.where(own_lane, live, 0), axis=1, keepdims=True)
    ids = jnp.where(over(iota((count, 1), 0), owners) < live, rows, -1)
    ids = jnp.broadcast_to(ids, (count, LANES)).astype(jnp.bfloat16)
    ids = exact(pick, ids)
    copies[2].wait()
    outs = ((own_out, slice(0, group)), (other_out, slice(group, count)))
    for t in range(dp):
        values = exact(pick, slots_ref[:, pl.ds(pl.multiple_of((d ^ t) * part, LANES), part)])
        for out_ref, spot in outs:
            out_ref[:, t * part : (t + 1) * part] = values[spot].astype(jnp.bfloat16)
    for out_ref, spot in outs:
        out_ref[:, dp * part :] = ids[spot].astype(jnp.bfloat16)


def diagonal(values, axis):
    return jnp.sum(jnp.where(iota(values.shape, 0) == iota(values.shape, 1), values, 0.0), axis=axis, keepdims=True)


def packed(values, ids):
    ids = jnp.broadcast_to(ids, (ids.shape[0], LANES))
    ids = jnp.broadcast_to(diagonal(ids, 0), (ID_ROWS, LANES))
    blocks = [values[:, c : c + LANES] for c in range(0, values.shape[1], LANES)]
    return jnp.concatenate([*blocks, ids], axis=0).astype(jnp.bfloat16)


def unpacked(ref, cols):
    group = (ref.shape[0] - ID_ROWS) // (cols // LANES)
    row = ref[cols // LANES * group :, :].astype(jnp.float32)[:1]
    ids = diagonal(jnp.broadcast_to(row, (group, LANES)), 1)
    values = [ref[c * group : (c + 1) * group, :] for c in range(cols // LANES)]
    return jnp.concatenate(values, axis=1).astype(jnp.float32), ids


def peers_kernel(dp, own_ref, other_ref, *out_refs):
    part = (own_ref.shape[1] - LANES) // dp
    ids = [ref[:, dp * part :].astype(jnp.float32) for ref in (own_ref, other_ref)]
    ids = jnp.concatenate(ids, axis=0)[:, :1]
    for t, out_ref in enumerate(out_refs):
        values = [ref[:, t * part : (t + 1) * part].astype(jnp.float32) for ref in (own_ref, other_ref)]
        out_ref[...] = packed(jnp.concatenate(values, axis=0), ids)


def owners_kernel(chips, cap, cols, *refs):
    in_refs, out_refs = refs[:-chips], refs[-chips:]
    held = [unpacked(ref, cols) for ref in in_refs]
    group = cap * chips
    for s, out_ref in enumerate(out_refs):
        spots = [slice(core * group + s * cap, core * group + (s + 1) * cap) for core in range(CORES)]
        rows = [[block[spot] for block in both for spot in spots] for both in zip(*held)]
        values, ids = [jnp.concatenate(blocks, axis=0) for blocks in rows]
        out_ref[...] = packed(values, ids)


def fetch_kernel(hidden_hbm, hidden_ref, sem):
    copy = pltpu.make_async_copy(hidden_hbm, hidden_ref, sem)
    copy.start()
    copy.wait()


def head_kernel(chips, dp, shard, mask_ref, own_ref, other_ref, *refs):
    d, z, core = place()
    parts, outs = refs[:chips], refs[chips:]
    rows = dp * shard
    total = chips * rows
    cols = own_ref.shape[1]
    size = chips * shard
    r = iota((total, total), 0)
    t = over(r, size)
    s = over(r - t * size, shard)
    i = r - t * size - s * shard
    order = one_hot(iota((total, total), 1) == s * rows + (t ^ d) * shard + i)
    mask = mask_ref[...].astype(jnp.float32).astype(jnp.bfloat16)
    columns = jnp.concatenate([part[...] for part in parts], axis=0) * mask
    columns = exact(order, columns).astype(jnp.bfloat16)
    for at, ref in ((core, own_ref), (1 - core, other_ref)):
        head = exact(columns, ref[...])
        spot = pl.ds(pl.multiple_of(at * cols, LANES), cols)
        for t, out_ref in enumerate(outs):
            out_ref[:, spot] = head[t * size : (t + 1) * size]


def stacked(rows):
    cut = rows.shape[1] // 2
    return jnp.concatenate([rows[:, :cut], rows[:, cut:]], axis=0)


def unstacked(rows):
    cut = rows.shape[0] // 2
    return jnp.concatenate([rows[:cut], rows[cut:]], axis=1)


def embed_kernel(dp, shard, cols, *refs):
    d, z, core = place()
    slot_refs, out_refs = refs[:-dp], refs[-dp:]
    held = [unpacked(ref, cols) for ref in slot_refs]
    values, ids = [jnp.concatenate(blocks, axis=0) for blocks in zip(*held)]
    values, ids = values.astype(jnp.bfloat16), ids.astype(jnp.int32)
    count = values.shape[0]
    block = over(jnp.maximum(ids, 0), shard)
    target = jnp.where(ids < 0, -1, (block ^ d) * shard + ids - block * shard)
    picked = one_hot(iota((count, dp * shard), 1) == target)
    embed = lax.dot_general(picked, values, (((0,), (0,)), ((), ())), preferred_element_type=jnp.float32)
    for t, out_ref in enumerate(out_refs):
        out_ref[...] = stacked(embed[t * shard : (t + 1) * shard])


def gather_kernel(*refs):
    d, z, core = place()
    parts, out_ref = refs[:-1], refs[-1]
    cols = out_ref.shape[1] // len(parts)
    for t, part in enumerate(parts):
        out_ref[:, pl.ds(pl.multiple_of((d ^ t) * cols, LANES), cols)] = unstacked(part[...])


def sum_kernel(chips, shard, *refs):
    dp = len(refs) - chips
    total = refs[0][...]
    for t in range(1, dp):
        total = total + refs[t][...]
    for s, out_ref in enumerate(refs[dp:]):
        out_ref[...] = stacked(total[s * shard : (s + 1) * shard])


def step(spot, piece_ref, embed_ref, master_ref, first_ref, second_ref):
    gradient = unstacked(piece_ref[...]) + embed_ref[:, spot]
    master = master_ref[:, spot]
    first_new = 0.9 * first_ref[:, spot] + 0.1 * gradient
    second_new = 0.95 * second_ref[:, spot] + 0.05 * gradient * gradient
    first_hat = first_new / (1.0 - 0.9**STEP)
    second_hat = second_new / (1.0 - 0.95**STEP)
    master_new = master - 0.05 * (first_hat / (jnp.sqrt(second_hat) + 1e-08) + 0.1 * master)
    return master_new, first_new, second_new


def chip_spot(z, s, piece_ref):
    cols = piece_ref.shape[1] * 2
    return pl.ds(pl.multiple_of((z ^ s) * cols, LANES), cols)


def rows_kernel(*refs):
    d, z, core = place()
    state, pieces, out_ref = refs[:4], refs[4:-1], refs[-1]
    table = [step(chip_spot(z, s, piece), piece, *state)[0] for s, piece in enumerate(pieces)]
    out_ref[...] = jnp.concatenate(table, axis=0).astype(jnp.bfloat16)


def adam_kernel(*refs):
    d, z, core = place()
    state, pieces, outs = refs[:4], refs[4:-3], refs[-3:]
    for s, piece in enumerate(pieces):
        spot = chip_spot(z, s, piece)
        for out_ref, value in zip(outs, step(spot, piece, *state)):
            out_ref[:, spot] = value


def table_kernel(chips, dp, shard, *refs):
    d, z, core = place()
    parts, out_ref = refs[:-1], refs[-1]
    cols = parts[0].shape[1]
    rows = dp * shard
    total = chips * rows
    values = jnp.concatenate([part[...] for part in parts], axis=0)
    r = iota((total, total), 0)
    s = over(r, rows)
    e = over(r - s * rows, shard)
    i = r - s * rows - e * shard
    order = one_hot(iota((total, total), 1) == ((e ^ d) * chips + s) * shard + i)
    values = exact(order, values).astype(jnp.bfloat16)
    for s in range(chips):
        spot = pl.ds(pl.multiple_of((z ^ s) * cols, LANES), cols)
        out_ref[:, spot] = values[s * rows : (s + 1) * rows]


def shaped(shape, kind):
    return jax.ShapeDtypeStruct(shape, kind)


def run(kernel, outs, *args, cost=1, hbm=0, scratch=()):
    moved = sum(x.size * x.dtype.itemsize for x in (*args, *jax.tree.leaves(outs)))
    vmem = pl.BlockSpec(memory_space=pltpu.VMEM)
    args = [pltpu.with_memory_space_constraint(x, pltpu.HBM) if n < hbm else x for n, x in enumerate(args)]
    return pl.pallas_call(
        kernel,
        out_shape=outs,
        in_specs=[pl.BlockSpec(memory_space=pltpu.HBM)] * hbm + [vmem] * (len(args) - hbm),
        out_specs=jax.tree.map(lambda _: vmem, outs),
        scratch_shapes=list(scratch),
        cost_estimate=pl.CostEstimate(flops=0, bytes_accessed=moved * cost, transcendentals=0),
        compiler_params=pltpu.CompilerParams(vmem_limit_bytes=VMEM_LIMIT),
    )(*args)


def local_copies(*args):
    return [pltpu.VMEM(x.shape, x.dtype) for x in args] + [pltpu.SemaphoreType.DMA((len(args),))]


def aligned(
    hidden,
    logit_grad,
    predict_mask,
    slot_grads,
    slot_rows,
    slot_counts,
    master,
    first_moment,
    second_moment,
):
    vocab = lax.axis_size("vocab")
    dp = lax.axis_size("dp")
    chips = vocab // CORES
    rows = logit_grad.shape[1]
    shard = master.shape[0]
    cols = hidden.shape[1] * CORES
    owners, cap, width = slot_grads.shape[1:]
    group = cap * chips
    bf16, f32 = jnp.bfloat16, jnp.float32

    def send(x, s, away=0):
        move = s * CORES + away
        return lax.ppermute(x, "vocab", [(v, v ^ move) for v in range(vocab)]) if move else x

    def send_dp(x, t):
        return lax.ppermute(x, "dp", [(i, i ^ t) for i in range(dp)]) if t else x

    hidden_other = send(hidden, 0, 1)
    slots_in = (
        slot_grads[0].transpose(1, 0, 2).reshape(cap * owners, width),
        slot_rows.transpose(2, 0, 1),
        slot_counts,
    )
    slots_own, slots_other = run(
        functools.partial(slots_kernel, chips, dp),
        [shaped((group, width + LANES), bf16)] * CORES,
        *slots_in,
        hbm=3,
        scratch=local_copies(*slots_in),
    )
    slots_other = send(slots_other, 0, 1)
    slots_other, hidden_other = lax.optimization_barrier((slots_other, hidden_other))
    quarter = width // dp
    packets = [shaped((vocab * cap * quarter // LANES + ID_ROWS, LANES), bf16)]
    quarters = run(functools.partial(peers_kernel, dp), packets * dp, slots_own, slots_other)
    messages = run(
        functools.partial(owners_kernel, chips, cap, quarter),
        packets * chips,
        *[send_dp(quarters[t], t) for t in range(dp)],
    )
    columns = [logit_grad.T]
    for s in range(1, chips):
        columns.append(send(columns[s - 1], 1) if s % 2 else send(columns[0], s))
    held = run(fetch_kernel, shaped(hidden.shape, bf16), hidden, hbm=1, scratch=[pltpu.SemaphoreType.DMA])
    head = run(
        functools.partial(head_kernel, chips, dp, shard),
        [shaped((chips * shard, cols), f32)] * dp,
        predict_mask[None, :],
        held,
        hidden_other,
        *columns,
    )
    embed = run(
        functools.partial(embed_kernel, dp, shard, quarter),
        [shaped((2 * shard, quarter // 2), f32)] * dp,
        *[send(messages[s], s) for s in reversed(range(chips))],
    )
    sums = run(
        functools.partial(sum_kernel, chips, shard),
        [shaped((2 * shard, cols // 2), f32)] * chips,
        *[send_dp(head[t], t) for t in range(dp)],
    )
    pieces = [send(sums[s], s) for s in range(chips)]
    embed = run(gather_kernel, shaped((shard, width), f32), *[send_dp(embed[t], t) for t in range(dp)])
    state = (embed, master, first_moment, second_moment)
    table = run(rows_kernel, shaped((chips * shard, cols), bf16), *state, *pieces)
    master_new, first_new, second_new = run(adam_kernel, [shaped(master.shape, f32)] * 3, *state, *pieces)
    table = run(
        functools.partial(table_kernel, chips, dp, shard),
        shaped((rows, width), bf16),
        *[send_dp(table, t) for t in range(dp)],
    )
    return (master_new, first_new, second_new, table)


def plain(
    hidden,
    logit_grad,
    predict_mask,
    slot_grads,
    slot_rows,
    slot_counts,
    master,
    first_moment,
    second_moment,
):
    vocab = lax.axis_size("vocab")
    dp = lax.axis_size("dp")
    chips = vocab // CORES
    rows = logit_grad.shape[1]
    shard = master.shape[0]
    cols = hidden.shape[1] * CORES
    owners, cap, width = slot_grads.shape[1:]
    here = lax.axis_index("vocab")
    core = here % CORES
    z = here // CORES
    d = lax.axis_index("dp")

    def to_core(x):
        return lax.ppermute(x, "vocab", [(v, v ^ 1) for v in range(vocab)])

    def to_chip(x, s):
        return lax.ppermute(x, "vocab", [(v, v ^ (s * CORES)) for v in range(vocab)])

    def to_dp(x, t):
        return lax.ppermute(x, "dp", [(i, i ^ t) for i in range(dp)])

    label = jnp.arange(rows, dtype=jnp.int32)
    source = ((label // shard) ^ d) * shard + label % shard
    reorder = (source[:, None] == label[None, :]).astype(jnp.bfloat16)
    masked = logit_grad * predict_mask.astype(jnp.bfloat16)[:, None]
    masked = lax.dot_general(reorder, masked, (((1,), (1,)), ((), ())), preferred_element_type=jnp.bfloat16)

    slot_index = jnp.arange(cap, dtype=jnp.int32)[None, :]
    ids = ((slot_rows[0] // shard) ^ d) * shard + slot_rows[0] % shard
    ids = jnp.where(slot_index < slot_counts[0][:, None], ids, -1).astype(jnp.bfloat16)
    ids = jnp.broadcast_to(ids[:, :, None, None], (owners, cap, chips, LANES))
    slots = slot_grads[0].reshape(owners, cap, chips, cols)
    slots = jnp.concatenate([slots, ids], axis=3).reshape(chips, CORES, cap, chips, cols + LANES)
    mine = lax.dynamic_index_in_dim(slots, core, 1, keepdims=False)
    other = lax.dynamic_index_in_dim(slots, 1 - core, 1, keepdims=False)
    hidden_other = to_core(hidden)
    other = to_core(other)
    masked = [masked] + [to_chip(masked, s) for s in range(1, chips)]
    both = jnp.stack([mine, other]).reshape(CORES * chips * cap, chips, cols + LANES)
    slots = [lax.dynamic_index_in_dim(both, z ^ s, 1, keepdims=False) for s in range(chips)]
    slots = [slots[0]] + [to_chip(slots[s], s) for s in range(1, chips)]

    swap = core == 1
    low = jnp.where(swap, hidden_other, hidden)
    high = jnp.where(swap, hidden, hidden_other)
    wide = jnp.concatenate([low, high], axis=1)
    slots = jnp.concatenate(slots, axis=0)
    owner = (jnp.arange(slots.shape[0], dtype=jnp.int32) // cap) % chips
    ids = slots[:, cols].astype(jnp.int32)
    ids = jnp.where(ids < 0, -1, (owner ^ z) * rows + ids)
    picked = (jnp.arange(chips * rows, dtype=jnp.int32)[:, None] == ids[None, :]).astype(jnp.bfloat16)
    part = jnp.dot(jnp.concatenate(masked, axis=0), wide, preferred_element_type=jnp.float32)
    part = part + jnp.dot(picked, slots[:, :cols], preferred_element_type=jnp.float32)
    part = part.reshape(chips, dp, shard, cols)
    part = [part[:, t].reshape(chips * shard, cols) for t in range(dp)]
    total = part[0]
    for t in range(1, dp):
        total = total + to_dp(part[t], t)
    total = total.reshape(chips, shard, CORES, cols // CORES).transpose(0, 2, 1, 3)
    total = total.reshape(chips, CORES * shard, cols // CORES)
    pieces = [total[0]] + [to_chip(total[s], s) for s in range(1, chips)]
    pieces = jnp.stack(pieces).reshape(chips, CORES, shard, cols // CORES).transpose(0, 2, 1, 3)
    pieces = pieces.reshape(chips, shard, cols)
    gradient = jnp.concatenate([lax.dynamic_index_in_dim(pieces, z ^ s, 0, keepdims=False) for s in range(chips)], axis=1)
    first_new = 0.9 * first_moment + 0.1 * gradient
    second_new = 0.95 * second_moment + 0.05 * gradient * gradient
    first_hat = first_new / (1.0 - 0.9**STEP)
    second_hat = second_new / (1.0 - 0.95**STEP)
    master_new = master - 0.05 * (first_hat / (jnp.sqrt(second_hat) + 1e-08) + 0.1 * master)
    table = master_new.astype(jnp.bfloat16)
    table = table.reshape(shard, chips, cols).transpose(1, 0, 2).reshape(chips * shard, cols)
    table = jnp.stack([table] + [to_dp(table, t) for t in range(1, dp)])
    table = jnp.stack([lax.dynamic_index_in_dim(table, d ^ t, 0, keepdims=False) for t in range(dp)])
    table = table.reshape(dp, chips, shard, cols).transpose(0, 2, 1, 3).reshape(rows, width)
    return (master_new, first_new, second_new, table)


def local(hidden, logit_grad, predict_mask, slot_grads, *rest):
    vocab = lax.axis_size("vocab")
    fits = hidden.shape[1] % LANES == 0 and logit_grad.shape[1] % 16 == 0
    slots = vocab * slot_grads.shape[2]
    fits = fits and slots % 16 == 0 and slots <= LANES and lax.axis_size("dp") == vocab // CORES
    fits = fits and slot_grads.shape[3] // lax.axis_size("dp") % (2 * LANES) == 0
    step = aligned if fits else plain
    return step(hidden, logit_grad, predict_mask, slot_grads, *rest)


def solution(mesh):
    in_specs = (
        P("dp", "vocab"),
        P("dp", "vocab"),
        P("dp"),
        P(("dp", "vocab"), None, None, None),
        P(("dp", "vocab"), None, None),
        P(("dp", "vocab"), None),
        P(("vocab", "dp"), None),
        P(("vocab", "dp"), None),
        P(("vocab", "dp"), None),
    )
    out_specs = (
        P(("vocab", "dp"), None),
        P(("vocab", "dp"), None),
        P(("vocab", "dp"), None),
        P("vocab", None),
    )
    return jax.shard_map(local, mesh=mesh, in_specs=in_specs, out_specs=out_specs, check_vma=False)
```

```python
import functools

import jax
import jax.numpy as jnp
from jax import lax
from jax.experimental import pallas as pl
from jax.experimental.pallas import tpu as pltpu
from jax.sharding import PartitionSpec as P

STEP = 8
CORES = 2
LANES = 128
ID_ROWS = 16
VMEM_LIMIT = 24 * 1024 * 1024


def place():
    here = lax.axis_index("vocab")
    return lax.axis_index("dp"), lax.shift_right_logical(here, 1), here & 1


def iota(shape, axis):
    return lax.broadcasted_iota(jnp.int32, shape, axis)


def over(x, n):
    return ((x.astype(jnp.float32) + 0.5) * (1.0 / n)).astype(jnp.int32)


def one_hot(flag):
    return jnp.where(flag, 1.0, 0.0).astype(jnp.bfloat16)


def exact(left, right):
    return jnp.dot(left, right, preferred_element_type=jnp.float32)


def slots_kernel(chips, dp, slots_hbm, rows_hbm, counts_hbm, own_out, other_out, slots_ref, rows_ref, counts_ref, sems):
    d, z, core = place()
    copies = [
        pltpu.make_async_copy(rows_hbm, rows_ref, sems.at[0]),
        pltpu.make_async_copy(counts_hbm, counts_ref, sems.at[1]),
        pltpu.make_async_copy(slots_hbm, slots_ref, sems.at[2]),
    ]
    for copy in copies:
        copy.start()
    cap, owners = rows_ref.shape[0], rows_ref.shape[2]
    count = cap * owners
    group = cap * chips
    part = slots_ref.shape[1] // dp
    q = iota((count, count), 0)
    away = jnp.where(q >= group, 1, 0)
    q = q - away * group
    s = over(q, cap)
    wanted = (q - s * cap) * owners + (s ^ z) * CORES + (away ^ core)
    pick = one_hot(iota((count, count), 1) == wanted)
    own_lane = iota((count, owners), 1) == iota((count, owners), 0) % owners
    for copy in copies[:2]:
        copy.wait()
    rows = jnp.broadcast_to(rows_ref[...], (cap, owners, owners)).reshape(count, owners)
    rows = jnp.sum(jnp.where(own_lane, rows, 0), axis=1, keepdims=True)
    live = jnp.broadcast_to(counts_ref[...], (count, owners))
    live = jnp.sum(jnp.where(own_lane, live, 0), axis=1, keepdims=True)
    ids = jnp.where(over(iota((count, 1), 0), owners) < live, rows, -1)
    ids = jnp.broadcast_to(ids, (count, LANES)).astype(jnp.bfloat16)
    ids = exact(pick, ids)
    copies[2].wait()
    outs = ((own_out, slice(0, group)), (other_out, slice(group, count)))
    for t in range(dp):
        values = exact(pick, slots_ref[:, pl.ds(pl.multiple_of((d ^ t) * part, LANES), part)])
        for out_ref, spot in outs:
            out_ref[:, t * part : (t + 1) * part] = values[spot].astype(jnp.bfloat16)
    for out_ref, spot in outs:
        out_ref[:, dp * part :] = ids[spot].astype(jnp.bfloat16)


def diagonal(values, axis):
    return jnp.sum(jnp.where(iota(values.shape, 0) == iota(values.shape, 1), values, 0.0), axis=axis, keepdims=True)


def packed(values, ids):
    ids = jnp.broadcast_to(ids, (ids.shape[0], LANES))
    ids = jnp.broadcast_to(diagonal(ids, 0), (ID_ROWS, LANES))
    blocks = [values[:, c : c + LANES] for c in range(0, values.shape[1], LANES)]
    return jnp.concatenate([*blocks, ids], axis=0).astype(jnp.bfloat16)


def unpacked(ref, cols):
    group = (ref.shape[0] - ID_ROWS) // (cols // LANES)
    row = ref[cols // LANES * group :, :].astype(jnp.float32)[:1]
    ids = diagonal(jnp.broadcast_to(row, (group, LANES)), 1)
    values = [ref[c * group : (c + 1) * group, :] for c in range(cols // LANES)]
    return jnp.concatenate(values, axis=1).astype(jnp.float32), ids


def peers_kernel(dp, own_ref, other_ref, *out_refs):
    part = (own_ref.shape[1] - LANES) // dp
    ids = [ref[:, dp * part :].astype(jnp.float32) for ref in (own_ref, other_ref)]
    ids = jnp.concatenate(ids, axis=0)[:, :1]
    for t, out_ref in enumerate(out_refs):
        values = [ref[:, t * part : (t + 1) * part].astype(jnp.float32) for ref in (own_ref, other_ref)]
        out_ref[...] = packed(jnp.concatenate(values, axis=0), ids)


def owners_kernel(chips, cap, cols, *refs):
    in_refs, out_refs = refs[:-chips], refs[-chips:]
    held = [unpacked(ref, cols) for ref in in_refs]
    group = cap * chips
    for s, out_ref in enumerate(out_refs):
        spots = [slice(core * group + s * cap, core * group + (s + 1) * cap) for core in range(CORES)]
        rows = [[block[spot] for block in both for spot in spots] for both in zip(*held)]
        values, ids = [jnp.concatenate(blocks, axis=0) for blocks in rows]
        out_ref[...] = packed(values, ids)


def fetch_kernel(hidden_hbm, hidden_ref, sem):
    copy = pltpu.make_async_copy(hidden_hbm, hidden_ref, sem)
    copy.start()
    copy.wait()


def head_kernel(chips, dp, shard, mask_ref, own_ref, other_ref, *refs):
    d, z, core = place()
    parts, outs = refs[:chips], refs[chips:]
    rows = dp * shard
    total = chips * rows
    cols = own_ref.shape[1]
    size = chips * shard
    r = iota((total, total), 0)
    t = over(r, size)
    s = over(r - t * size, shard)
    i = r - t * size - s * shard
    order = one_hot(iota((total, total), 1) == s * rows + (t ^ d) * shard + i)
    mask = mask_ref[...].astype(jnp.float32).astype(jnp.bfloat16)
    columns = jnp.concatenate([part[...] for part in parts], axis=0) * mask
    columns = exact(order, columns).astype(jnp.bfloat16)
    for at, ref in ((core, own_ref), (1 - core, other_ref)):
        head = exact(columns, ref[...])
        spot = pl.ds(pl.multiple_of(at * cols, LANES), cols)
        for t, out_ref in enumerate(outs):
            out_ref[:, spot] = head[t * size : (t + 1) * size]


def stacked(rows):
    cut = rows.shape[1] // 2
    return jnp.concatenate([rows[:, :cut], rows[:, cut:]], axis=0)


def unstacked(rows):
    cut = rows.shape[0] // 2
    return jnp.concatenate([rows[:cut], rows[cut:]], axis=1)


def embed_kernel(dp, shard, cols, *refs):
    d, z, core = place()
    slot_refs, out_refs = refs[:-dp], refs[-dp:]
    held = [unpacked(ref, cols) for ref in slot_refs]
    values, ids = [jnp.concatenate(blocks, axis=0) for blocks in zip(*held)]
    values, ids = values.astype(jnp.bfloat16), ids.astype(jnp.int32)
    count = values.shape[0]
    block = over(jnp.maximum(ids, 0), shard)
    target = jnp.where(ids < 0, -1, (block ^ d) * shard + ids - block * shard)
    picked = one_hot(iota((count, dp * shard), 1) == target)
    embed = lax.dot_general(picked, values, (((0,), (0,)), ((), ())), preferred_element_type=jnp.float32)
    for t, out_ref in enumerate(out_refs):
        out_ref[...] = stacked(embed[t * shard : (t + 1) * shard])


def gather_kernel(*refs):
    d, z, core = place()
    parts, out_ref = refs[:-1], refs[-1]
    cols = out_ref.shape[1] // len(parts)
    for t, part in enumerate(parts):
        out_ref[:, pl.ds(pl.multiple_of((d ^ t) * cols, LANES), cols)] = unstacked(part[...])


def sum_kernel(chips, shard, *refs):
    dp = len(refs) - chips
    total = refs[0][...]
    for t in range(1, dp):
        total = total + refs[t][...]
    for s, out_ref in enumerate(refs[dp:]):
        out_ref[...] = stacked(total[s * shard : (s + 1) * shard])


def step(spot, piece_ref, embed_ref, master_ref, first_ref, second_ref):
    gradient = unstacked(piece_ref[...]) + embed_ref[:, spot]
    master = master_ref[:, spot]
    first_new = 0.9 * first_ref[:, spot] + 0.1 * gradient
    second_new = 0.95 * second_ref[:, spot] + 0.05 * gradient * gradient
    first_hat = first_new / (1.0 - 0.9**STEP)
    second_hat = second_new / (1.0 - 0.95**STEP)
    master_new = master - 0.05 * (first_hat / (jnp.sqrt(second_hat) + 1e-08) + 0.1 * master)
    return master_new, first_new, second_new


def chip_spot(z, s, piece_ref):
    cols = piece_ref.shape[1] * 2
    return pl.ds(pl.multiple_of((z ^ s) * cols, LANES), cols)


def rows_kernel(*refs):
    d, z, core = place()
    state, pieces, out_ref = refs[:4], refs[4:-1], refs[-1]
    table = [step(chip_spot(z, s, piece), piece, *state)[0] for s, piece in enumerate(reversed(pieces))]
    out_ref[...] = jnp.concatenate(table, axis=0).astype(jnp.bfloat16)


def adam_kernel(*refs):
    d, z, core = place()
    state, pieces, outs = refs[:4], refs[4:-3], refs[-3:]
    for s, piece in enumerate(reversed(pieces)):
        spot = chip_spot(z, s, piece)
        for out_ref, value in zip(outs, step(spot, piece, *state)):
            out_ref[:, spot] = value


def table_kernel(chips, dp, shard, *refs):
    d, z, core = place()
    parts, out_ref = refs[:-1], refs[-1]
    cols = parts[0].shape[1]
    rows = dp * shard
    total = chips * rows
    values = jnp.concatenate([part[...] for part in parts], axis=0)
    r = iota((total, total), 0)
    s = over(r, rows)
    e = over(r - s * rows, shard)
    i = r - s * rows - e * shard
    order = one_hot(iota((total, total), 1) == ((e ^ d) * chips + s) * shard + i)
    values = exact(order, values).astype(jnp.bfloat16)
    for s in range(chips):
        spot = pl.ds(pl.multiple_of((z ^ s) * cols, LANES), cols)
        out_ref[:, spot] = values[s * rows : (s + 1) * rows]


def shaped(shape, kind):
    return jax.ShapeDtypeStruct(shape, kind)


def run(kernel, outs, *args, cost=1, hbm=0, scratch=()):
    moved = sum(x.size * x.dtype.itemsize for x in (*args, *jax.tree.leaves(outs)))
    vmem = pl.BlockSpec(memory_space=pltpu.VMEM)
    args = [pltpu.with_memory_space_constraint(x, pltpu.HBM) if n < hbm else x for n, x in enumerate(args)]
    return pl.pallas_call(
        kernel,
        out_shape=outs,
        in_specs=[pl.BlockSpec(memory_space=pltpu.HBM)] * hbm + [vmem] * (len(args) - hbm),
        out_specs=jax.tree.map(lambda _: vmem, outs),
        scratch_shapes=list(scratch),
        cost_estimate=pl.CostEstimate(flops=0, bytes_accessed=moved * cost, transcendentals=0),
        compiler_params=pltpu.CompilerParams(vmem_limit_bytes=VMEM_LIMIT),
    )(*args)


def local_copies(*args):
    return [pltpu.VMEM(x.shape, x.dtype) for x in args] + [pltpu.SemaphoreType.DMA((len(args),))]


def aligned(
    hidden,
    logit_grad,
    predict_mask,
    slot_grads,
    slot_rows,
    slot_counts,
    master,
    first_moment,
    second_moment,
):
    vocab = lax.axis_size("vocab")
    dp = lax.axis_size("dp")
    chips = vocab // CORES
    rows = logit_grad.shape[1]
    shard = master.shape[0]
    cols = hidden.shape[1] * CORES
    owners, cap, width = slot_grads.shape[1:]
    group = cap * chips
    bf16, f32 = jnp.bfloat16, jnp.float32

    def send(x, s, away=0):
        move = s * CORES + away
        return lax.ppermute(x, "vocab", [(v, v ^ move) for v in range(vocab)]) if move else x

    def send_dp(x, t):
        return lax.ppermute(x, "dp", [(i, i ^ t) for i in range(dp)]) if t else x

    hidden_other = send(hidden, 0, 1)
    slots_in = (
        slot_grads[0].transpose(1, 0, 2).reshape(cap * owners, width),
        slot_rows.transpose(2, 0, 1),
        slot_counts,
    )
    slots_own, slots_other = run(
        functools.partial(slots_kernel, chips, dp),
        [shaped((group, width + LANES), bf16)] * CORES,
        *slots_in,
        hbm=3,
        scratch=local_copies(*slots_in),
    )
    slots_other = send(slots_other, 0, 1)
    slots_other, hidden_other = lax.optimization_barrier((slots_other, hidden_other))
    quarter = width // dp
    packets = [shaped((vocab * cap * quarter // LANES + ID_ROWS, LANES), bf16)]
    quarters = run(functools.partial(peers_kernel, dp), packets * dp, slots_own, slots_other)
    held = run(fetch_kernel, shaped(hidden.shape, bf16), hidden, hbm=1, scratch=[pltpu.SemaphoreType.DMA])
    quarters = [send_dp(quarters[t], t) for t in range(dp)]
    quarters[0], held = lax.optimization_barrier((quarters[0], held))
    messages = run(functools.partial(owners_kernel, chips, cap, quarter), packets * chips, *quarters)
    columns = [logit_grad.T]
    for s in range(1, chips):
        columns.append(send(columns[s - 1], 1) if s % 2 else send(columns[0], s))
    head = run(
        functools.partial(head_kernel, chips, dp, shard),
        [shaped((chips * shard, cols), f32)] * dp,
        predict_mask[None, :],
        held,
        hidden_other,
        *columns,
    )
    embed = run(
        functools.partial(embed_kernel, dp, shard, quarter),
        [shaped((2 * shard, quarter // 2), f32)] * dp,
        *[send(messages[s], s) for s in reversed(range(chips))],
    )
    sums = run(
        functools.partial(sum_kernel, chips, shard),
        [shaped((2 * shard, cols // 2), f32)] * chips,
        *[send_dp(head[t], t) for t in range(dp)],
    )
    pieces = [send(sums[s], s) for s in reversed(range(chips))]
    embed = run(gather_kernel, shaped((shard, width), f32), *[send_dp(embed[t], t) for t in range(dp)])
    state = (embed, master, first_moment, second_moment)
    table = run(rows_kernel, shaped((chips * shard, cols), bf16), *state, *pieces)
    master_new, first_new, second_new = run(adam_kernel, [shaped(master.shape, f32)] * 3, *state, *pieces)
    table = run(
        functools.partial(table_kernel, chips, dp, shard),
        shaped((rows, width), bf16),
        *[send_dp(table, t) for t in range(dp)],
    )
    return (master_new, first_new, second_new, table)


def plain(
    hidden,
    logit_grad,
    predict_mask,
    slot_grads,
    slot_rows,
    slot_counts,
    master,
    first_moment,
    second_moment,
):
    vocab = lax.axis_size("vocab")
    dp = lax.axis_size("dp")
    chips = vocab // CORES
    rows = logit_grad.shape[1]
    shard = master.shape[0]
    cols = hidden.shape[1] * CORES
    owners, cap, width = slot_grads.shape[1:]
    here = lax.axis_index("vocab")
    core = here % CORES
    z = here // CORES
    d = lax.axis_index("dp")

    def to_core(x):
        return lax.ppermute(x, "vocab", [(v, v ^ 1) for v in range(vocab)])

    def to_chip(x, s):
        return lax.ppermute(x, "vocab", [(v, v ^ (s * CORES)) for v in range(vocab)])

    def to_dp(x, t):
        return lax.ppermute(x, "dp", [(i, i ^ t) for i in range(dp)])

    label = jnp.arange(rows, dtype=jnp.int32)
    source = ((label // shard) ^ d) * shard + label % shard
    reorder = (source[:, None] == label[None, :]).astype(jnp.bfloat16)
    masked = logit_grad * predict_mask.astype(jnp.bfloat16)[:, None]
    masked = lax.dot_general(reorder, masked, (((1,), (1,)), ((), ())), preferred_element_type=jnp.bfloat16)

    slot_index = jnp.arange(cap, dtype=jnp.int32)[None, :]
    ids = ((slot_rows[0] // shard) ^ d) * shard + slot_rows[0] % shard
    ids = jnp.where(slot_index < slot_counts[0][:, None], ids, -1).astype(jnp.bfloat16)
    ids = jnp.broadcast_to(ids[:, :, None, None], (owners, cap, chips, LANES))
    slots = slot_grads[0].reshape(owners, cap, chips, cols)
    slots = jnp.concatenate([slots, ids], axis=3).reshape(chips, CORES, cap, chips, cols + LANES)
    mine = lax.dynamic_index_in_dim(slots, core, 1, keepdims=False)
    other = lax.dynamic_index_in_dim(slots, 1 - core, 1, keepdims=False)
    hidden_other = to_core(hidden)
    other = to_core(other)
    masked = [masked] + [to_chip(masked, s) for s in range(1, chips)]
    both = jnp.stack([mine, other]).reshape(CORES * chips * cap, chips, cols + LANES)
    slots = [lax.dynamic_index_in_dim(both, z ^ s, 1, keepdims=False) for s in range(chips)]
    slots = [slots[0]] + [to_chip(slots[s], s) for s in range(1, chips)]

    swap = core == 1
    low = jnp.where(swap, hidden_other, hidden)
    high = jnp.where(swap, hidden, hidden_other)
    wide = jnp.concatenate([low, high], axis=1)
    slots = jnp.concatenate(slots, axis=0)
    owner = (jnp.arange(slots.shape[0], dtype=jnp.int32) // cap) % chips
    ids = slots[:, cols].astype(jnp.int32)
    ids = jnp.where(ids < 0, -1, (owner ^ z) * rows + ids)
    picked = (jnp.arange(chips * rows, dtype=jnp.int32)[:, None] == ids[None, :]).astype(jnp.bfloat16)
    part = jnp.dot(jnp.concatenate(masked, axis=0), wide, preferred_element_type=jnp.float32)
    part = part + jnp.dot(picked, slots[:, :cols], preferred_element_type=jnp.float32)
    part = part.reshape(chips, dp, shard, cols)
    part = [part[:, t].reshape(chips * shard, cols) for t in range(dp)]
    total = part[0]
    for t in range(1, dp):
        total = total + to_dp(part[t], t)
    total = total.reshape(chips, shard, CORES, cols // CORES).transpose(0, 2, 1, 3)
    total = total.reshape(chips, CORES * shard, cols // CORES)
    pieces = [total[0]] + [to_chip(total[s], s) for s in range(1, chips)]
    pieces = jnp.stack(pieces).reshape(chips, CORES, shard, cols // CORES).transpose(0, 2, 1, 3)
    pieces = pieces.reshape(chips, shard, cols)
    gradient = jnp.concatenate([lax.dynamic_index_in_dim(pieces, z ^ s, 0, keepdims=False) for s in range(chips)], axis=1)
    first_new = 0.9 * first_moment + 0.1 * gradient
    second_new = 0.95 * second_moment + 0.05 * gradient * gradient
    first_hat = first_new / (1.0 - 0.9**STEP)
    second_hat = second_new / (1.0 - 0.95**STEP)
    master_new = master - 0.05 * (first_hat / (jnp.sqrt(second_hat) + 1e-08) + 0.1 * master)
    table = master_new.astype(jnp.bfloat16)
    table = table.reshape(shard, chips, cols).transpose(1, 0, 2).reshape(chips * shard, cols)
    table = jnp.stack([table] + [to_dp(table, t) for t in range(1, dp)])
    table = jnp.stack([lax.dynamic_index_in_dim(table, d ^ t, 0, keepdims=False) for t in range(dp)])
    table = table.reshape(dp, chips, shard, cols).transpose(0, 2, 1, 3).reshape(rows, width)
    return (master_new, first_new, second_new, table)


def local(hidden, logit_grad, predict_mask, slot_grads, *rest):
    vocab = lax.axis_size("vocab")
    fits = hidden.shape[1] % LANES == 0 and logit_grad.shape[1] % 16 == 0
    slots = vocab * slot_grads.shape[2]
    fits = fits and slots % 16 == 0 and slots <= LANES and lax.axis_size("dp") == vocab // CORES
    fits = fits and slot_grads.shape[3] // lax.axis_size("dp") % (2 * LANES) == 0
    step = aligned if fits else plain
    return step(hidden, logit_grad, predict_mask, slot_grads, *rest)


def solution(mesh):
    in_specs = (
        P("dp", "vocab"),
        P("dp", "vocab"),
        P("dp"),
        P(("dp", "vocab"), None, None, None),
        P(("dp", "vocab"), None, None),
        P(("dp", "vocab"), None),
        P(("vocab", "dp"), None),
        P(("vocab", "dp"), None),
        P(("vocab", "dp"), None),
    )
    out_specs = (
        P(("vocab", "dp"), None),
        P(("vocab", "dp"), None),
        P(("vocab", "dp"), None),
        P("vocab", None),
    )
    return jax.shard_map(local, mesh=mesh, in_specs=in_specs, out_specs=out_specs, check_vma=False)
```

```python
import functools

import jax
import jax.numpy as jnp
from jax import lax
from jax.experimental import pallas as pl
from jax.experimental.pallas import tpu as pltpu
from jax.sharding import PartitionSpec as P

STEP = 8
CORES = 2
LANES = 128
ID_ROWS = 16
VMEM_LIMIT = 24 * 1024 * 1024


def place():
    here = lax.axis_index("vocab")
    return lax.axis_index("dp"), lax.shift_right_logical(here, 1), here & 1


def iota(shape, axis):
    return lax.broadcasted_iota(jnp.int32, shape, axis)


def over(x, n):
    return ((x.astype(jnp.float32) + 0.5) * (1.0 / n)).astype(jnp.int32)


def one_hot(flag):
    return jnp.where(flag, 1.0, 0.0).astype(jnp.bfloat16)


def exact(left, right):
    return jnp.dot(left, right, preferred_element_type=jnp.float32)


def slots_kernel(chips, dp, slots_hbm, rows_hbm, counts_hbm, own_out, other_out, slots_ref, rows_ref, counts_ref, sems):
    d, z, core = place()
    copies = [
        pltpu.make_async_copy(rows_hbm, rows_ref, sems.at[0]),
        pltpu.make_async_copy(counts_hbm, counts_ref, sems.at[1]),
        pltpu.make_async_copy(slots_hbm, slots_ref, sems.at[2]),
    ]
    for copy in copies:
        copy.start()
    cap, owners = rows_ref.shape[0], rows_ref.shape[2]
    count = cap * owners
    group = cap * chips
    part = slots_ref.shape[1] // dp
    q = iota((count, count), 0)
    away = jnp.where(q >= group, 1, 0)
    q = q - away * group
    s = over(q, cap)
    wanted = (q - s * cap) * owners + (s ^ z) * CORES + (away ^ core)
    pick = one_hot(iota((count, count), 1) == wanted)
    own_lane = iota((count, owners), 1) == iota((count, owners), 0) % owners
    for copy in copies[:2]:
        copy.wait()
    rows = jnp.broadcast_to(rows_ref[...], (cap, owners, owners)).reshape(count, owners)
    rows = jnp.sum(jnp.where(own_lane, rows, 0), axis=1, keepdims=True)
    live = jnp.broadcast_to(counts_ref[...], (count, owners))
    live = jnp.sum(jnp.where(own_lane, live, 0), axis=1, keepdims=True)
    ids = jnp.where(over(iota((count, 1), 0), owners) < live, rows, -1)
    ids = jnp.broadcast_to(ids, (count, LANES)).astype(jnp.bfloat16)
    ids = exact(pick, ids)
    copies[2].wait()
    outs = ((own_out, slice(0, group)), (other_out, slice(group, count)))
    for t in range(dp):
        values = exact(pick, slots_ref[:, pl.ds(pl.multiple_of((d ^ t) * part, LANES), part)])
        for out_ref, spot in outs:
            out_ref[:, t * part : (t + 1) * part] = values[spot].astype(jnp.bfloat16)
    for out_ref, spot in outs:
        out_ref[:, dp * part :] = ids[spot].astype(jnp.bfloat16)


def diagonal(values, axis):
    return jnp.sum(jnp.where(iota(values.shape, 0) == iota(values.shape, 1), values, 0.0), axis=axis, keepdims=True)


def packed(values, ids):
    ids = jnp.broadcast_to(ids, (ids.shape[0], LANES))
    ids = jnp.broadcast_to(diagonal(ids, 0), (ID_ROWS, LANES))
    blocks = [values[:, c : c + LANES] for c in range(0, values.shape[1], LANES)]
    return jnp.concatenate([*blocks, ids], axis=0).astype(jnp.bfloat16)


def unpacked(ref, cols):
    group = (ref.shape[0] - ID_ROWS) // (cols // LANES)
    row = ref[cols // LANES * group :, :].astype(jnp.float32)[:1]
    ids = diagonal(jnp.broadcast_to(row, (group, LANES)), 1)
    values = [ref[c * group : (c + 1) * group, :] for c in range(cols // LANES)]
    return jnp.concatenate(values, axis=1).astype(jnp.float32), ids


def peers_kernel(dp, own_ref, other_ref, *out_refs):
    part = (own_ref.shape[1] - LANES) // dp
    ids = [ref[:, dp * part :].astype(jnp.float32) for ref in (own_ref, other_ref)]
    ids = jnp.concatenate(ids, axis=0)[:, :1]
    for t, out_ref in enumerate(out_refs):
        values = [ref[:, t * part : (t + 1) * part].astype(jnp.float32) for ref in (own_ref, other_ref)]
        out_ref[...] = packed(jnp.concatenate(values, axis=0), ids)


def owners_kernel(chips, cap, cols, *refs):
    in_refs, out_refs = refs[:-chips], refs[-chips:]
    held = [unpacked(ref, cols) for ref in in_refs]
    group = cap * chips
    for s, out_ref in enumerate(out_refs):
        spots = [slice(core * group + s * cap, core * group + (s + 1) * cap) for core in range(CORES)]
        rows = [[block[spot] for block in both for spot in spots] for both in zip(*held)]
        values, ids = [jnp.concatenate(blocks, axis=0) for blocks in rows]
        out_ref[...] = packed(values, ids)


def fetch_kernel(hidden_hbm, hidden_ref, sem):
    copy = pltpu.make_async_copy(hidden_hbm, hidden_ref, sem)
    copy.start()
    copy.wait()


def head_kernel(chips, dp, shard, mask_ref, own_ref, other_ref, *refs):
    d, z, core = place()
    parts, outs = refs[:chips], refs[chips:]
    rows = dp * shard
    total = chips * rows
    cols = own_ref.shape[1]
    size = chips * shard
    r = iota((total, total), 0)
    t = over(r, size)
    s = over(r - t * size, shard)
    i = r - t * size - s * shard
    order = one_hot(iota((total, total), 1) == s * rows + (t ^ d) * shard + i)
    mask = mask_ref[...].astype(jnp.float32).astype(jnp.bfloat16)
    columns = jnp.concatenate([part[...] for part in parts], axis=0) * mask
    columns = exact(order, columns).astype(jnp.bfloat16)
    for at, ref in ((core, own_ref), (1 - core, other_ref)):
        head = exact(columns, ref[...])
        spot = pl.ds(pl.multiple_of(at * cols, LANES), cols)
        for t, out_ref in enumerate(outs):
            out_ref[:, spot] = head[t * size : (t + 1) * size]


def stacked(rows):
    cut = rows.shape[1] // 2
    return jnp.concatenate([rows[:, :cut], rows[:, cut:]], axis=0)


def unstacked(rows):
    cut = rows.shape[0] // 2
    return jnp.concatenate([rows[:cut], rows[cut:]], axis=1)


def embed_kernel(dp, shard, cols, *refs):
    d, z, core = place()
    slot_refs, out_refs = refs[:-dp], refs[-dp:]
    held = [unpacked(ref, cols) for ref in slot_refs]
    values, ids = [jnp.concatenate(blocks, axis=0) for blocks in zip(*held)]
    values, ids = values.astype(jnp.bfloat16), ids.astype(jnp.int32)
    count = values.shape[0]
    block = over(jnp.maximum(ids, 0), shard)
    target = jnp.where(ids < 0, -1, (block ^ d) * shard + ids - block * shard)
    picked = one_hot(iota((count, dp * shard), 1) == target)
    embed = lax.dot_general(picked, values, (((0,), (0,)), ((), ())), preferred_element_type=jnp.float32)
    for t, out_ref in enumerate(out_refs):
        out_ref[...] = stacked(embed[t * shard : (t + 1) * shard])


def gather_kernel(*refs):
    d, z, core = place()
    parts, out_ref = refs[:-1], refs[-1]
    cols = out_ref.shape[1] // len(parts)
    for t, part in enumerate(parts):
        out_ref[:, pl.ds(pl.multiple_of((d ^ t) * cols, LANES), cols)] = unstacked(part[...])


def sum_kernel(chips, shard, *refs):
    dp = len(refs) - chips
    total = refs[0][...]
    for t in range(1, dp):
        total = total + refs[t][...]
    for s, out_ref in enumerate(refs[dp:]):
        out_ref[...] = stacked(total[s * shard : (s + 1) * shard])


def step(spot, piece_ref, embed_ref, master_ref, first_ref, second_ref):
    gradient = unstacked(piece_ref[...]) + embed_ref[:, spot]
    master = master_ref[:, spot]
    first_new = 0.9 * first_ref[:, spot] + 0.1 * gradient
    second_new = 0.95 * second_ref[:, spot] + 0.05 * gradient * gradient
    first_hat = first_new / (1.0 - 0.9**STEP)
    second_hat = second_new / (1.0 - 0.95**STEP)
    master_new = master - 0.05 * (first_hat / (jnp.sqrt(second_hat) + 1e-08) + 0.1 * master)
    return master_new, first_new, second_new


def chip_spot(z, s, piece_ref):
    cols = piece_ref.shape[1] * 2
    return pl.ds(pl.multiple_of((z ^ s) * cols, LANES), cols)


def rows_kernel(*refs):
    d, z, core = place()
    state, pieces, out_ref = refs[:4], refs[4:-1], refs[-1]
    table = [step(chip_spot(z, s, piece), piece, *state)[0] for s, piece in enumerate(reversed(pieces))]
    out_ref[...] = jnp.concatenate(table, axis=0).astype(jnp.bfloat16)


def adam_kernel(chips, dp, shard, *refs):
    d, z, core = place()
    state, pieces, outs, order_ref = refs[:4], refs[4:-4], refs[-4:-1], refs[-1]
    rows = dp * shard
    total = chips * rows
    r = iota((total, total), 0)
    s = over(r, rows)
    e = over(r - s * rows, shard)
    i = r - s * rows - e * shard
    order_ref[...] = one_hot(iota((total, total), 1) == ((e ^ d) * chips + s) * shard + i)
    for s, piece in enumerate(reversed(pieces)):
        spot = chip_spot(z, s, piece)
        for out_ref, value in zip(outs, step(spot, piece, *state)):
            out_ref[:, spot] = value


def table_kernel(chips, dp, shard, order_ref, *refs):
    d, z, core = place()
    parts, (out_hbm, out_ref, sems) = refs[-4::-1], refs[-3:]
    cols = parts[0].shape[1]
    rows = dp * shard
    values = jnp.concatenate([part[...] for part in parts], axis=0)
    values = exact(order_ref[...], values).astype(jnp.bfloat16)
    copies = []
    for s in range(chips):
        out_ref[s] = values[s * rows : (s + 1) * rows]
        spot = pl.ds(pl.multiple_of((z ^ s) * cols, LANES), cols)
        copies.append(pltpu.make_async_copy(out_ref.at[s], out_hbm.at[:, spot], sems.at[s]))
        copies[-1].start()
    for copy in copies:
        copy.wait()


def shaped(shape, kind):
    return jax.ShapeDtypeStruct(shape, kind)


def run(kernel, outs, *args, cost=1, hbm=0, out_hbm=False, scratch=()):
    moved = sum(x.size * x.dtype.itemsize for x in (*args, *jax.tree.leaves(outs)))
    vmem = pl.BlockSpec(memory_space=pltpu.VMEM)
    args = [pltpu.with_memory_space_constraint(x, pltpu.HBM) if n < hbm else x for n, x in enumerate(args)]
    return pl.pallas_call(
        kernel,
        out_shape=outs,
        in_specs=[pl.BlockSpec(memory_space=pltpu.HBM)] * hbm + [vmem] * (len(args) - hbm),
        out_specs=jax.tree.map(lambda _: pl.BlockSpec(memory_space=pltpu.HBM) if out_hbm else vmem, outs),
        scratch_shapes=list(scratch),
        cost_estimate=pl.CostEstimate(flops=0, bytes_accessed=moved * cost, transcendentals=0),
        compiler_params=pltpu.CompilerParams(vmem_limit_bytes=VMEM_LIMIT),
    )(*args)


def local_copies(*args):
    return [pltpu.VMEM(x.shape, x.dtype) for x in args] + [pltpu.SemaphoreType.DMA((len(args),))]


def aligned(
    hidden,
    logit_grad,
    predict_mask,
    slot_grads,
    slot_rows,
    slot_counts,
    master,
    first_moment,
    second_moment,
):
    vocab = lax.axis_size("vocab")
    dp = lax.axis_size("dp")
    chips = vocab // CORES
    rows = logit_grad.shape[1]
    shard = master.shape[0]
    cols = hidden.shape[1] * CORES
    owners, cap, width = slot_grads.shape[1:]
    group = cap * chips
    bf16, f32 = jnp.bfloat16, jnp.float32

    def send(x, s, away=0):
        move = s * CORES + away
        return lax.ppermute(x, "vocab", [(v, v ^ move) for v in range(vocab)]) if move else x

    def send_dp(x, t):
        return lax.ppermute(x, "dp", [(i, i ^ t) for i in range(dp)]) if t else x

    hidden_other = send(hidden, 0, 1)
    slots_in = (
        slot_grads[0].transpose(1, 0, 2).reshape(cap * owners, width),
        slot_rows.transpose(2, 0, 1),
        slot_counts,
    )
    slots_own, slots_other = run(
        functools.partial(slots_kernel, chips, dp),
        [shaped((group, width + LANES), bf16)] * CORES,
        *slots_in,
        hbm=3,
        scratch=local_copies(*slots_in),
    )
    slots_other = send(slots_other, 0, 1)
    slots_other, hidden_other = lax.optimization_barrier((slots_other, hidden_other))
    quarter = width // dp
    packets = [shaped((vocab * cap * quarter // LANES + ID_ROWS, LANES), bf16)]
    quarters = run(functools.partial(peers_kernel, dp), packets * dp, slots_own, slots_other)
    held = run(fetch_kernel, shaped(hidden.shape, bf16), hidden, hbm=1, scratch=[pltpu.SemaphoreType.DMA])
    quarters = [send_dp(quarters[t], t) for t in reversed(range(dp))]
    quarters[-1], held = lax.optimization_barrier((quarters[-1], held))
    messages = run(functools.partial(owners_kernel, chips, cap, quarter), packets * chips, *quarters)
    columns = [logit_grad.T]
    for s in range(1, chips):
        columns.append(send(columns[s - 1], 1) if s % 2 else send(columns[0], s))
    head = run(
        functools.partial(head_kernel, chips, dp, shard),
        [shaped((chips * shard, cols), f32)] * dp,
        predict_mask[None, :],
        held,
        hidden_other,
        *columns,
    )
    embed = run(
        functools.partial(embed_kernel, dp, shard, quarter),
        [shaped((2 * shard, quarter // 2), f32)] * dp,
        *[send(messages[s], s) for s in reversed(range(chips))],
    )
    sums = run(
        functools.partial(sum_kernel, chips, shard),
        [shaped((2 * shard, cols // 2), f32)] * chips,
        *[send_dp(head[t], t) for t in reversed(range(dp))],
    )
    pieces = [send(sums[s], s) for s in reversed(range(chips))]
    embed = run(gather_kernel, shaped((shard, width), f32), *[send_dp(embed[t], t) for t in range(dp)])
    state = (embed, master, first_moment, second_moment)
    table = run(rows_kernel, shaped((chips * shard, cols), bf16), *state, *pieces)
    master_new, first_new, second_new, order = run(
        functools.partial(adam_kernel, chips, dp, shard),
        [shaped(master.shape, f32)] * 3 + [shaped((chips * rows, chips * rows), bf16)],
        *state,
        *pieces,
    )
    table = run(
        functools.partial(table_kernel, chips, dp, shard),
        shaped((rows, width), bf16),
        order,
        *[send_dp(table, t) for t in reversed(range(dp))],
        out_hbm=True,
        scratch=[pltpu.VMEM((chips, rows, cols), bf16), pltpu.SemaphoreType.DMA((chips,))],
    )
    return (master_new, first_new, second_new, table)


def plain(
    hidden,
    logit_grad,
    predict_mask,
    slot_grads,
    slot_rows,
    slot_counts,
    master,
    first_moment,
    second_moment,
):
    vocab = lax.axis_size("vocab")
    dp = lax.axis_size("dp")
    chips = vocab // CORES
    rows = logit_grad.shape[1]
    shard = master.shape[0]
    cols = hidden.shape[1] * CORES
    owners, cap, width = slot_grads.shape[1:]
    here = lax.axis_index("vocab")
    core = here % CORES
    z = here // CORES
    d = lax.axis_index("dp")

    def to_core(x):
        return lax.ppermute(x, "vocab", [(v, v ^ 1) for v in range(vocab)])

    def to_chip(x, s):
        return lax.ppermute(x, "vocab", [(v, v ^ (s * CORES)) for v in range(vocab)])

    def to_dp(x, t):
        return lax.ppermute(x, "dp", [(i, i ^ t) for i in range(dp)])

    label = jnp.arange(rows, dtype=jnp.int32)
    source = ((label // shard) ^ d) * shard + label % shard
    reorder = (source[:, None] == label[None, :]).astype(jnp.bfloat16)
    masked = logit_grad * predict_mask.astype(jnp.bfloat16)[:, None]
    masked = lax.dot_general(reorder, masked, (((1,), (1,)), ((), ())), preferred_element_type=jnp.bfloat16)

    slot_index = jnp.arange(cap, dtype=jnp.int32)[None, :]
    ids = ((slot_rows[0] // shard) ^ d) * shard + slot_rows[0] % shard
    ids = jnp.where(slot_index < slot_counts[0][:, None], ids, -1).astype(jnp.bfloat16)
    ids = jnp.broadcast_to(ids[:, :, None, None], (owners, cap, chips, LANES))
    slots = slot_grads[0].reshape(owners, cap, chips, cols)
    slots = jnp.concatenate([slots, ids], axis=3).reshape(chips, CORES, cap, chips, cols + LANES)
    mine = lax.dynamic_index_in_dim(slots, core, 1, keepdims=False)
    other = lax.dynamic_index_in_dim(slots, 1 - core, 1, keepdims=False)
    hidden_other = to_core(hidden)
    other = to_core(other)
    masked = [masked] + [to_chip(masked, s) for s in range(1, chips)]
    both = jnp.stack([mine, other]).reshape(CORES * chips * cap, chips, cols + LANES)
    slots = [lax.dynamic_index_in_dim(both, z ^ s, 1, keepdims=False) for s in range(chips)]
    slots = [slots[0]] + [to_chip(slots[s], s) for s in range(1, chips)]

    swap = core == 1
    low = jnp.where(swap, hidden_other, hidden)
    high = jnp.where(swap, hidden, hidden_other)
    wide = jnp.concatenate([low, high], axis=1)
    slots = jnp.concatenate(slots, axis=0)
    owner = (jnp.arange(slots.shape[0], dtype=jnp.int32) // cap) % chips
    ids = slots[:, cols].astype(jnp.int32)
    ids = jnp.where(ids < 0, -1, (owner ^ z) * rows + ids)
    picked = (jnp.arange(chips * rows, dtype=jnp.int32)[:, None] == ids[None, :]).astype(jnp.bfloat16)
    part = jnp.dot(jnp.concatenate(masked, axis=0), wide, preferred_element_type=jnp.float32)
    part = part + jnp.dot(picked, slots[:, :cols], preferred_element_type=jnp.float32)
    part = part.reshape(chips, dp, shard, cols)
    part = [part[:, t].reshape(chips * shard, cols) for t in range(dp)]
    total = part[0]
    for t in range(1, dp):
        total = total + to_dp(part[t], t)
    total = total.reshape(chips, shard, CORES, cols // CORES).transpose(0, 2, 1, 3)
    total = total.reshape(chips, CORES * shard, cols // CORES)
    pieces = [total[0]] + [to_chip(total[s], s) for s in range(1, chips)]
    pieces = jnp.stack(pieces).reshape(chips, CORES, shard, cols // CORES).transpose(0, 2, 1, 3)
    pieces = pieces.reshape(chips, shard, cols)
    gradient = jnp.concatenate([lax.dynamic_index_in_dim(pieces, z ^ s, 0, keepdims=False) for s in range(chips)], axis=1)
    first_new = 0.9 * first_moment + 0.1 * gradient
    second_new = 0.95 * second_moment + 0.05 * gradient * gradient
    first_hat = first_new / (1.0 - 0.9**STEP)
    second_hat = second_new / (1.0 - 0.95**STEP)
    master_new = master - 0.05 * (first_hat / (jnp.sqrt(second_hat) + 1e-08) + 0.1 * master)
    table = master_new.astype(jnp.bfloat16)
    table = table.reshape(shard, chips, cols).transpose(1, 0, 2).reshape(chips * shard, cols)
    table = jnp.stack([table] + [to_dp(table, t) for t in range(1, dp)])
    table = jnp.stack([lax.dynamic_index_in_dim(table, d ^ t, 0, keepdims=False) for t in range(dp)])
    table = table.reshape(dp, chips, shard, cols).transpose(0, 2, 1, 3).reshape(rows, width)
    return (master_new, first_new, second_new, table)


def local(hidden, logit_grad, predict_mask, slot_grads, *rest):
    vocab = lax.axis_size("vocab")
    fits = hidden.shape[1] % LANES == 0 and logit_grad.shape[1] % 16 == 0
    slots = vocab * slot_grads.shape[2]
    fits = fits and slots % 16 == 0 and slots <= LANES and lax.axis_size("dp") == vocab // CORES
    fits = fits and slot_grads.shape[3] // lax.axis_size("dp") % (2 * LANES) == 0
    step = aligned if fits else plain
    return step(hidden, logit_grad, predict_mask, slot_grads, *rest)


def solution(mesh):
    in_specs = (
        P("dp", "vocab"),
        P("dp", "vocab"),
        P("dp"),
        P(("dp", "vocab"), None, None, None),
        P(("dp", "vocab"), None, None),
        P(("dp", "vocab"), None),
        P(("vocab", "dp"), None),
        P(("vocab", "dp"), None),
        P(("vocab", "dp"), None),
    )
    out_specs = (
        P(("vocab", "dp"), None),
        P(("vocab", "dp"), None),
        P(("vocab", "dp"), None),
        P("vocab", None),
    )
    return jax.shard_map(local, mesh=mesh, in_specs=in_specs, out_specs=out_specs, check_vma=False)
```

```python
import functools

import jax
import jax.numpy as jnp
from jax import lax
from jax.experimental import pallas as pl
from jax.experimental.pallas import tpu as pltpu
from jax.sharding import PartitionSpec as P

STEP = 8
CORES = 2
LANES = 128
ID_ROWS = 16
VMEM_LIMIT = 24 * 1024 * 1024


def place():
    here = lax.axis_index("vocab")
    return lax.axis_index("dp"), lax.shift_right_logical(here, 1), here & 1


def iota(shape, axis):
    return lax.broadcasted_iota(jnp.int32, shape, axis)


def over(x, n):
    return ((x.astype(jnp.float32) + 0.5) * (1.0 / n)).astype(jnp.int32)


def one_hot(flag):
    return jnp.where(flag, 1.0, 0.0).astype(jnp.bfloat16)


def exact(left, right):
    return jnp.dot(left, right, preferred_element_type=jnp.float32)


def slots_kernel(chips, dp, slots_hbm, rows_hbm, counts_hbm, own_out, other_out, slots_ref, rows_ref, counts_ref, sems):
    d, z, core = place()
    copies = [
        pltpu.make_async_copy(rows_hbm, rows_ref, sems.at[0]),
        pltpu.make_async_copy(counts_hbm, counts_ref, sems.at[1]),
        pltpu.make_async_copy(slots_hbm, slots_ref, sems.at[2]),
    ]
    for copy in copies:
        copy.start()
    cap, owners = rows_ref.shape[0], rows_ref.shape[2]
    count = cap * owners
    group = cap * chips
    part = slots_ref.shape[1] // dp
    q = iota((count, count), 0)
    away = jnp.where(q >= group, 1, 0)
    q = q - away * group
    s = over(q, cap)
    wanted = (q - s * cap) * owners + (s ^ z) * CORES + (away ^ core)
    pick = one_hot(iota((count, count), 1) == wanted)
    own_lane = iota((count, owners), 1) == iota((count, owners), 0) % owners
    for copy in copies[:2]:
        copy.wait()
    rows = jnp.broadcast_to(rows_ref[...], (cap, owners, owners)).reshape(count, owners)
    rows = jnp.sum(jnp.where(own_lane, rows, 0), axis=1, keepdims=True)
    live = jnp.broadcast_to(counts_ref[...], (count, owners))
    live = jnp.sum(jnp.where(own_lane, live, 0), axis=1, keepdims=True)
    ids = jnp.where(over(iota((count, 1), 0), owners) < live, rows, -1)
    ids = jnp.broadcast_to(ids, (count, LANES)).astype(jnp.bfloat16)
    ids = exact(pick, ids)
    copies[2].wait()
    outs = ((own_out, slice(0, group)), (other_out, slice(group, count)))
    for t in range(dp):
        values = exact(pick, slots_ref[:, pl.ds(pl.multiple_of((d ^ t) * part, LANES), part)])
        for out_ref, spot in outs:
            out_ref[:, t * part : (t + 1) * part] = values[spot].astype(jnp.bfloat16)
    for out_ref, spot in outs:
        out_ref[:, dp * part :] = ids[spot].astype(jnp.bfloat16)


def diagonal(values, axis):
    return jnp.sum(jnp.where(iota(values.shape, 0) == iota(values.shape, 1), values, 0.0), axis=axis, keepdims=True)


def packed(values, ids):
    ids = jnp.broadcast_to(ids, (ids.shape[0], LANES))
    ids = jnp.broadcast_to(diagonal(ids, 0), (ID_ROWS, LANES))
    blocks = [values[:, c : c + LANES] for c in range(0, values.shape[1], LANES)]
    return jnp.concatenate([*blocks, ids], axis=0).astype(jnp.bfloat16)


def unpacked(ref, cols):
    group = (ref.shape[0] - ID_ROWS) // (cols // LANES)
    row = ref[cols // LANES * group :, :].astype(jnp.float32)[:1]
    ids = diagonal(jnp.broadcast_to(row, (group, LANES)), 1)
    values = [ref[c * group : (c + 1) * group, :] for c in range(cols // LANES)]
    return jnp.concatenate(values, axis=1).astype(jnp.float32), ids


def peers_kernel(dp, own_ref, other_ref, *out_refs):
    part = (own_ref.shape[1] - LANES) // dp
    ids = [ref[:, dp * part :].astype(jnp.float32) for ref in (own_ref, other_ref)]
    ids = jnp.concatenate(ids, axis=0)[:, :1]
    for t, out_ref in enumerate(out_refs):
        values = [ref[:, t * part : (t + 1) * part].astype(jnp.float32) for ref in (own_ref, other_ref)]
        out_ref[...] = packed(jnp.concatenate(values, axis=0), ids)


def owners_kernel(chips, cap, cols, *refs):
    in_refs, out_refs = refs[:-chips], refs[-chips:]
    held = [unpacked(ref, cols) for ref in in_refs]
    group = cap * chips
    for s, out_ref in enumerate(out_refs):
        spots = [slice(core * group + s * cap, core * group + (s + 1) * cap) for core in range(CORES)]
        rows = [[block[spot] for block in both for spot in spots] for both in zip(*held)]
        values, ids = [jnp.concatenate(blocks, axis=0) for blocks in rows]
        out_ref[...] = packed(values, ids)


def fetch_kernel(hidden_hbm, hidden_ref, sem):
    copy = pltpu.make_async_copy(hidden_hbm, hidden_ref, sem)
    copy.start()
    copy.wait()


def head_kernel(chips, dp, shard, mask_ref, own_ref, other_ref, *refs):
    d, z, core = place()
    parts, outs = refs[:chips], refs[chips:]
    rows = dp * shard
    total = chips * rows
    cols = own_ref.shape[1]
    half = chips // 2
    size = half * shard
    r = iota((total, total), 0)
    near = jnp.where(r >= total // 2, 1, 0)
    r = r - near * (total // 2)
    t = over(r, size)
    s = over(r - t * size, shard)
    i = r - t * size - s * shard
    s = s + (1 - near) * half
    order = one_hot(iota((total, total), 1) == s * rows + (t ^ d) * shard + i)
    mask = mask_ref[...].astype(jnp.float32).astype(jnp.bfloat16)
    columns = jnp.concatenate([part[...] for part in parts], axis=0) * mask
    columns = exact(order, columns).astype(jnp.bfloat16)
    for at, ref in ((core, own_ref), (1 - core, other_ref)):
        head = exact(columns, ref[...])
        spot = pl.ds(pl.multiple_of(at * cols, LANES), cols)
        for n, out_ref in enumerate(outs):
            out_ref[:, spot] = head[n * size : (n + 1) * size]


def stacked(rows):
    cut = rows.shape[1] // 2
    return jnp.concatenate([rows[:, :cut], rows[:, cut:]], axis=0)


def unstacked(rows):
    cut = rows.shape[0] // 2
    return jnp.concatenate([rows[:cut], rows[cut:]], axis=1)


def embed_kernel(dp, shard, cols, *refs):
    d, z, core = place()
    slot_refs, out_refs = refs[:-dp], refs[-dp:]
    held = [unpacked(ref, cols) for ref in slot_refs]
    values, ids = [jnp.concatenate(blocks, axis=0) for blocks in zip(*held)]
    values, ids = values.astype(jnp.bfloat16), ids.astype(jnp.int32)
    count = values.shape[0]
    block = over(jnp.maximum(ids, 0), shard)
    target = jnp.where(ids < 0, -1, (block ^ d) * shard + ids - block * shard)
    picked = one_hot(iota((count, dp * shard), 1) == target)
    embed = lax.dot_general(picked, values, (((0,), (0,)), ((), ())), preferred_element_type=jnp.float32)
    for t, out_ref in enumerate(out_refs):
        out_ref[...] = stacked(embed[t * shard : (t + 1) * shard])


def gather_kernel(*refs):
    d, z, core = place()
    parts, out_ref = refs[:-1], refs[-1]
    cols = out_ref.shape[1] // len(parts)
    for t, part in enumerate(parts):
        out_ref[:, pl.ds(pl.multiple_of((d ^ t) * cols, LANES), cols)] = unstacked(part[...])


def sum_kernel(half, shard, *refs):
    dp = len(refs) - half
    total = refs[0][...]
    for t in range(1, dp):
        total = total + refs[t][...]
    for s, out_ref in enumerate(refs[dp:]):
        out_ref[...] = stacked(total[s * shard : (s + 1) * shard])


def step(spot, piece_ref, embed_ref, master_ref, first_ref, second_ref):
    gradient = unstacked(piece_ref[...]) + embed_ref[:, spot]
    master = master_ref[:, spot]
    first_new = 0.9 * first_ref[:, spot] + 0.1 * gradient
    second_new = 0.95 * second_ref[:, spot] + 0.05 * gradient * gradient
    first_hat = first_new / (1.0 - 0.9**STEP)
    second_hat = second_new / (1.0 - 0.95**STEP)
    master_new = master - 0.05 * (first_hat / (jnp.sqrt(second_hat) + 1e-08) + 0.1 * master)
    return master_new, first_new, second_new


def chip_spot(z, s, piece_ref):
    cols = piece_ref.shape[1] * 2
    return pl.ds(pl.multiple_of((z ^ s) * cols, LANES), cols)


def rows_kernel(*refs):
    d, z, core = place()
    state, pieces, out_ref = refs[:4], refs[4:-1], refs[-1]
    table = [step(chip_spot(z, s, piece), piece, *state)[0] for s, piece in enumerate(reversed(pieces))]
    out_ref[...] = jnp.concatenate(table, axis=0).astype(jnp.bfloat16)


def adam_kernel(chips, dp, shard, *refs):
    d, z, core = place()
    state, pieces, outs, order_ref = refs[:4], refs[4:-4], refs[-4:-1], refs[-1]
    rows = dp * shard
    total = chips * rows
    r = iota((total, total), 0)
    s = over(r, rows)
    e = over(r - s * rows, shard)
    i = r - s * rows - e * shard
    order_ref[...] = one_hot(iota((total, total), 1) == ((e ^ d) * chips + s) * shard + i)
    for s, piece in enumerate(reversed(pieces)):
        spot = chip_spot(z, s, piece)
        for out_ref, value in zip(outs, step(spot, piece, *state)):
            out_ref[:, spot] = value


def table_kernel(chips, dp, shard, order_ref, *refs):
    d, z, core = place()
    parts, (out_hbm, out_ref, sems) = refs[-4::-1], refs[-3:]
    cols = parts[0].shape[1]
    rows = dp * shard
    values = jnp.concatenate([part[...] for part in parts], axis=0)
    values = exact(order_ref[...], values).astype(jnp.bfloat16)
    copies = []
    for s in range(chips):
        out_ref[s] = values[s * rows : (s + 1) * rows]
        spot = pl.ds(pl.multiple_of((z ^ s) * cols, LANES), cols)
        copies.append(pltpu.make_async_copy(out_ref.at[s], out_hbm.at[:, spot], sems.at[s]))
        copies[-1].start()
    for copy in copies:
        copy.wait()


def shaped(shape, kind):
    return jax.ShapeDtypeStruct(shape, kind)


def run(kernel, outs, *args, cost=1, hbm=0, out_hbm=False, scratch=()):
    moved = sum(x.size * x.dtype.itemsize for x in (*args, *jax.tree.leaves(outs)))
    vmem = pl.BlockSpec(memory_space=pltpu.VMEM)
    args = [pltpu.with_memory_space_constraint(x, pltpu.HBM) if n < hbm else x for n, x in enumerate(args)]
    return pl.pallas_call(
        kernel,
        out_shape=outs,
        in_specs=[pl.BlockSpec(memory_space=pltpu.HBM)] * hbm + [vmem] * (len(args) - hbm),
        out_specs=jax.tree.map(lambda _: pl.BlockSpec(memory_space=pltpu.HBM) if out_hbm else vmem, outs),
        scratch_shapes=list(scratch),
        cost_estimate=pl.CostEstimate(flops=0, bytes_accessed=moved * cost, transcendentals=0),
        compiler_params=pltpu.CompilerParams(vmem_limit_bytes=VMEM_LIMIT),
    )(*args)


def local_copies(*args):
    return [pltpu.VMEM(x.shape, x.dtype) for x in args] + [pltpu.SemaphoreType.DMA((len(args),))]


def aligned(
    hidden,
    logit_grad,
    predict_mask,
    slot_grads,
    slot_rows,
    slot_counts,
    master,
    first_moment,
    second_moment,
):
    vocab = lax.axis_size("vocab")
    dp = lax.axis_size("dp")
    chips = vocab // CORES
    rows = logit_grad.shape[1]
    shard = master.shape[0]
    cols = hidden.shape[1] * CORES
    owners, cap, width = slot_grads.shape[1:]
    group = cap * chips
    half = chips // 2
    bf16, f32 = jnp.bfloat16, jnp.float32

    def send(x, s, away=0):
        move = s * CORES + away
        return lax.ppermute(x, "vocab", [(v, v ^ move) for v in range(vocab)]) if move else x

    def send_dp(x, t):
        return lax.ppermute(x, "dp", [(i, i ^ t) for i in range(dp)]) if t else x

    hidden_other = send(hidden, 0, 1)
    slots_in = (
        slot_grads[0].transpose(1, 0, 2).reshape(cap * owners, width),
        slot_rows.transpose(2, 0, 1),
        slot_counts,
    )
    slots_own, slots_other = run(
        functools.partial(slots_kernel, chips, dp),
        [shaped((group, width + LANES), bf16)] * CORES,
        *slots_in,
        hbm=3,
        scratch=local_copies(*slots_in),
    )
    slots_other = send(slots_other, 0, 1)
    slots_other, hidden_other = lax.optimization_barrier((slots_other, hidden_other))
    quarter = width // dp
    packets = [shaped((vocab * cap * quarter // LANES + ID_ROWS, LANES), bf16)]
    quarters = run(functools.partial(peers_kernel, dp), packets * dp, slots_own, slots_other)
    held = run(fetch_kernel, shaped(hidden.shape, bf16), hidden, hbm=1, scratch=[pltpu.SemaphoreType.DMA])
    quarters = [send_dp(quarters[t], t) for t in reversed(range(dp))]
    quarters[-1], held = lax.optimization_barrier((quarters[-1], held))
    messages = run(functools.partial(owners_kernel, chips, cap, quarter), packets * chips, *quarters)
    columns = [logit_grad.T]
    for s in range(1, chips):
        columns.append(send(columns[s - 1], 1) if s % 2 else send(columns[0], s))
    head = run(
        functools.partial(head_kernel, chips, dp, shard),
        [shaped((half * shard, cols), f32)] * (2 * dp),
        predict_mask[None, :],
        held,
        hidden_other,
        *columns,
    )
    embed = run(
        functools.partial(embed_kernel, dp, shard, quarter),
        [shaped((2 * shard, quarter // 2), f32)] * dp,
        *[send(messages[s], s) for s in reversed(range(chips))],
    )
    pieces = {}
    for h, members in enumerate((range(half, chips), range(half))):
        heard = [send_dp(head[h * dp + t], t) for t in reversed(range(dp))]
        if h:
            heard[-1], _ = lax.optimization_barrier((heard[-1], sums[0]))
        sums = run(
            functools.partial(sum_kernel, half, shard),
            [shaped((2 * shard, cols // 2), f32)] * half,
            *heard,
        )
        for s, total in zip(members, sums):
            pieces[s] = send(total, s)
    pieces = [pieces[s] for s in reversed(range(chips))]
    embed = run(gather_kernel, shaped((shard, width), f32), *[send_dp(embed[t], t) for t in range(dp)])
    state = (embed, master, first_moment, second_moment)
    table = run(rows_kernel, shaped((chips * shard, cols), bf16), *state, *pieces)
    master_new, first_new, second_new, order = run(
        functools.partial(adam_kernel, chips, dp, shard),
        [shaped(master.shape, f32)] * 3 + [shaped((chips * rows, chips * rows), bf16)],
        *state,
        *pieces,
    )
    table = run(
        functools.partial(table_kernel, chips, dp, shard),
        shaped((rows, width), bf16),
        order,
        *[send_dp(table, t) for t in reversed(range(dp))],
        out_hbm=True,
        scratch=[pltpu.VMEM((chips, rows, cols), bf16), pltpu.SemaphoreType.DMA((chips,))],
    )
    return (master_new, first_new, second_new, table)


def plain(
    hidden,
    logit_grad,
    predict_mask,
    slot_grads,
    slot_rows,
    slot_counts,
    master,
    first_moment,
    second_moment,
):
    vocab = lax.axis_size("vocab")
    dp = lax.axis_size("dp")
    chips = vocab // CORES
    rows = logit_grad.shape[1]
    shard = master.shape[0]
    cols = hidden.shape[1] * CORES
    owners, cap, width = slot_grads.shape[1:]
    here = lax.axis_index("vocab")
    core = here % CORES
    z = here // CORES
    d = lax.axis_index("dp")

    def to_core(x):
        return lax.ppermute(x, "vocab", [(v, v ^ 1) for v in range(vocab)])

    def to_chip(x, s):
        return lax.ppermute(x, "vocab", [(v, v ^ (s * CORES)) for v in range(vocab)])

    def to_dp(x, t):
        return lax.ppermute(x, "dp", [(i, i ^ t) for i in range(dp)])

    label = jnp.arange(rows, dtype=jnp.int32)
    source = ((label // shard) ^ d) * shard + label % shard
    reorder = (source[:, None] == label[None, :]).astype(jnp.bfloat16)
    masked = logit_grad * predict_mask.astype(jnp.bfloat16)[:, None]
    masked = lax.dot_general(reorder, masked, (((1,), (1,)), ((), ())), preferred_element_type=jnp.bfloat16)

    slot_index = jnp.arange(cap, dtype=jnp.int32)[None, :]
    ids = ((slot_rows[0] // shard) ^ d) * shard + slot_rows[0] % shard
    ids = jnp.where(slot_index < slot_counts[0][:, None], ids, -1).astype(jnp.bfloat16)
    ids = jnp.broadcast_to(ids[:, :, None, None], (owners, cap, chips, LANES))
    slots = slot_grads[0].reshape(owners, cap, chips, cols)
    slots = jnp.concatenate([slots, ids], axis=3).reshape(chips, CORES, cap, chips, cols + LANES)
    mine = lax.dynamic_index_in_dim(slots, core, 1, keepdims=False)
    other = lax.dynamic_index_in_dim(slots, 1 - core, 1, keepdims=False)
    hidden_other = to_core(hidden)
    other = to_core(other)
    masked = [masked] + [to_chip(masked, s) for s in range(1, chips)]
    both = jnp.stack([mine, other]).reshape(CORES * chips * cap, chips, cols + LANES)
    slots = [lax.dynamic_index_in_dim(both, z ^ s, 1, keepdims=False) for s in range(chips)]
    slots = [slots[0]] + [to_chip(slots[s], s) for s in range(1, chips)]

    swap = core == 1
    low = jnp.where(swap, hidden_other, hidden)
    high = jnp.where(swap, hidden, hidden_other)
    wide = jnp.concatenate([low, high], axis=1)
    slots = jnp.concatenate(slots, axis=0)
    owner = (jnp.arange(slots.shape[0], dtype=jnp.int32) // cap) % chips
    ids = slots[:, cols].astype(jnp.int32)
    ids = jnp.where(ids < 0, -1, (owner ^ z) * rows + ids)
    picked = (jnp.arange(chips * rows, dtype=jnp.int32)[:, None] == ids[None, :]).astype(jnp.bfloat16)
    part = jnp.dot(jnp.concatenate(masked, axis=0), wide, preferred_element_type=jnp.float32)
    part = part + jnp.dot(picked, slots[:, :cols], preferred_element_type=jnp.float32)
    part = part.reshape(chips, dp, shard, cols)
    part = [part[:, t].reshape(chips * shard, cols) for t in range(dp)]
    total = part[0]
    for t in range(1, dp):
        total = total + to_dp(part[t], t)
    total = total.reshape(chips, shard, CORES, cols // CORES).transpose(0, 2, 1, 3)
    total = total.reshape(chips, CORES * shard, cols // CORES)
    pieces = [total[0]] + [to_chip(total[s], s) for s in range(1, chips)]
    pieces = jnp.stack(pieces).reshape(chips, CORES, shard, cols // CORES).transpose(0, 2, 1, 3)
    pieces = pieces.reshape(chips, shard, cols)
    gradient = jnp.concatenate([lax.dynamic_index_in_dim(pieces, z ^ s, 0, keepdims=False) for s in range(chips)], axis=1)
    first_new = 0.9 * first_moment + 0.1 * gradient
    second_new = 0.95 * second_moment + 0.05 * gradient * gradient
    first_hat = first_new / (1.0 - 0.9**STEP)
    second_hat = second_new / (1.0 - 0.95**STEP)
    master_new = master - 0.05 * (first_hat / (jnp.sqrt(second_hat) + 1e-08) + 0.1 * master)
    table = master_new.astype(jnp.bfloat16)
    table = table.reshape(shard, chips, cols).transpose(1, 0, 2).reshape(chips * shard, cols)
    table = jnp.stack([table] + [to_dp(table, t) for t in range(1, dp)])
    table = jnp.stack([lax.dynamic_index_in_dim(table, d ^ t, 0, keepdims=False) for t in range(dp)])
    table = table.reshape(dp, chips, shard, cols).transpose(0, 2, 1, 3).reshape(rows, width)
    return (master_new, first_new, second_new, table)


def local(hidden, logit_grad, predict_mask, slot_grads, *rest):
    vocab = lax.axis_size("vocab")
    fits = hidden.shape[1] % LANES == 0 and logit_grad.shape[1] % 16 == 0
    slots = vocab * slot_grads.shape[2]
    fits = fits and slots % 16 == 0 and slots <= LANES and lax.axis_size("dp") == vocab // CORES
    fits = fits and slot_grads.shape[3] // lax.axis_size("dp") % (2 * LANES) == 0
    step = aligned if fits else plain
    return step(hidden, logit_grad, predict_mask, slot_grads, *rest)


def solution(mesh):
    in_specs = (
        P("dp", "vocab"),
        P("dp", "vocab"),
        P("dp"),
        P(("dp", "vocab"), None, None, None),
        P(("dp", "vocab"), None, None),
        P(("dp", "vocab"), None),
        P(("vocab", "dp"), None),
        P(("vocab", "dp"), None),
        P(("vocab", "dp"), None),
    )
    out_specs = (
        P(("vocab", "dp"), None),
        P(("vocab", "dp"), None),
        P(("vocab", "dp"), None),
        P("vocab", None),
    )
    return jax.shard_map(local, mesh=mesh, in_specs=in_specs, out_specs=out_specs, check_vma=False)
```

```python
import functools

import jax
import jax.numpy as jnp
from jax import lax
from jax.experimental import pallas as pl
from jax.experimental.pallas import tpu as pltpu
from jax.sharding import PartitionSpec as P

STEP = 8
CORES = 2
LANES = 128
ID_ROWS = 16
VMEM_LIMIT = 24 * 1024 * 1024


def place():
    here = lax.axis_index("vocab")
    return lax.axis_index("dp"), lax.shift_right_logical(here, 1), here & 1


def iota(shape, axis):
    return lax.broadcasted_iota(jnp.int32, shape, axis)


def over(x, n):
    return ((x.astype(jnp.float32) + 0.5) * (1.0 / n)).astype(jnp.int32)


def one_hot(flag):
    return jnp.where(flag, 1.0, 0.0).astype(jnp.bfloat16)


def exact(left, right):
    return jnp.dot(left, right, preferred_element_type=jnp.float32)


def slots_kernel(chips, dp, slots_hbm, rows_hbm, counts_hbm, own_out, other_out, slots_ref, rows_ref, counts_ref, sems):
    d, z, core = place()
    copies = [
        pltpu.make_async_copy(rows_hbm, rows_ref, sems.at[0]),
        pltpu.make_async_copy(counts_hbm, counts_ref, sems.at[1]),
        pltpu.make_async_copy(slots_hbm, slots_ref, sems.at[2]),
    ]
    for copy in copies:
        copy.start()
    cap, owners = rows_ref.shape[0], rows_ref.shape[2]
    count = cap * owners
    group = cap * chips
    part = slots_ref.shape[1] // dp
    q = iota((count, count), 0)
    away = jnp.where(q >= group, 1, 0)
    q = q - away * group
    s = over(q, cap)
    wanted = (q - s * cap) * owners + (s ^ z) * CORES + (away ^ core)
    pick = one_hot(iota((count, count), 1) == wanted)
    own_lane = iota((count, owners), 1) == iota((count, owners), 0) % owners
    for copy in copies[:2]:
        copy.wait()
    rows = jnp.broadcast_to(rows_ref[...], (cap, owners, owners)).reshape(count, owners)
    rows = jnp.sum(jnp.where(own_lane, rows, 0), axis=1, keepdims=True)
    live = jnp.broadcast_to(counts_ref[...], (count, owners))
    live = jnp.sum(jnp.where(own_lane, live, 0), axis=1, keepdims=True)
    ids = jnp.where(over(iota((count, 1), 0), owners) < live, rows, -1)
    ids = jnp.broadcast_to(ids, (count, LANES)).astype(jnp.bfloat16)
    ids = exact(pick, ids)
    copies[2].wait()
    outs = ((own_out, slice(0, group)), (other_out, slice(group, count)))
    for t in range(dp):
        values = exact(pick, slots_ref[:, pl.ds(pl.multiple_of((d ^ t) * part, LANES), part)])
        for out_ref, spot in outs:
            out_ref[:, t * part : (t + 1) * part] = values[spot].astype(jnp.bfloat16)
    for out_ref, spot in outs:
        out_ref[:, dp * part :] = ids[spot].astype(jnp.bfloat16)


def diagonal(values, axis):
    return jnp.sum(jnp.where(iota(values.shape, 0) == iota(values.shape, 1), values, 0.0), axis=axis, keepdims=True)


def packed(values, ids):
    ids = jnp.broadcast_to(ids, (ids.shape[0], LANES))
    ids = jnp.broadcast_to(diagonal(ids, 0), (ID_ROWS, LANES))
    blocks = [values[:, c : c + LANES] for c in range(0, values.shape[1], LANES)]
    return jnp.concatenate([*blocks, ids], axis=0).astype(jnp.bfloat16)


def unpacked(ref, cols):
    group = (ref.shape[0] - ID_ROWS) // (cols // LANES)
    row = ref[cols // LANES * group :, :].astype(jnp.float32)[:1]
    ids = diagonal(jnp.broadcast_to(row, (group, LANES)), 1)
    values = [ref[c * group : (c + 1) * group, :] for c in range(cols // LANES)]
    return jnp.concatenate(values, axis=1).astype(jnp.float32), ids


def peers_kernel(dp, own_ref, other_ref, *out_refs):
    part = (own_ref.shape[1] - LANES) // dp
    ids = [ref[:, dp * part :].astype(jnp.float32) for ref in (own_ref, other_ref)]
    ids = jnp.concatenate(ids, axis=0)[:, :1]
    for t, out_ref in enumerate(out_refs):
        values = [ref[:, t * part : (t + 1) * part].astype(jnp.float32) for ref in (own_ref, other_ref)]
        out_ref[...] = packed(jnp.concatenate(values, axis=0), ids)


def owners_kernel(chips, cap, cols, *refs):
    in_refs, out_refs = refs[:-chips], refs[-chips:]
    held = [unpacked(ref, cols) for ref in in_refs]
    group = cap * chips
    for s, out_ref in enumerate(out_refs):
        spots = [slice(core * group + s * cap, core * group + (s + 1) * cap) for core in range(CORES)]
        rows = [[block[spot] for block in both for spot in spots] for both in zip(*held)]
        values, ids = [jnp.concatenate(blocks, axis=0) for blocks in rows]
        out_ref[...] = packed(values, ids)


def fetch_kernel(hidden_hbm, hidden_ref, sem):
    copy = pltpu.make_async_copy(hidden_hbm, hidden_ref, sem)
    copy.start()
    copy.wait()


def head_kernel(chips, dp, shard, mask_ref, own_ref, other_ref, *refs):
    d, z, core = place()
    parts, outs = refs[:chips], refs[chips:]
    rows = dp * shard
    total = chips * rows
    cols = own_ref.shape[1]
    size = chips * shard
    r = iota((total, total), 0)
    t = over(r, size)
    s = over(r - t * size, shard)
    i = r - t * size - s * shard
    order = one_hot(iota((total, total), 1) == s * rows + (t ^ d) * shard + i)
    mask = mask_ref[...].astype(jnp.float32).astype(jnp.bfloat16)
    columns = jnp.concatenate([part[...] for part in parts], axis=0) * mask
    columns = exact(order, columns).astype(jnp.bfloat16)
    for at, ref in ((core, own_ref), (1 - core, other_ref)):
        head = exact(columns, ref[...])
        spot = pl.ds(pl.multiple_of(at * cols, LANES), cols)
        for t, out_ref in enumerate(outs):
            out_ref[:, spot] = head[t * size : (t + 1) * size]


def stacked(rows):
    cut = rows.shape[1] // 2
    return jnp.concatenate([rows[:, :cut], rows[:, cut:]], axis=0)


def unstacked(rows):
    cut = rows.shape[0] // 2
    return jnp.concatenate([rows[:cut], rows[cut:]], axis=1)


def embed_kernel(dp, shard, cols, *refs):
    d, z, core = place()
    slot_refs, out_refs = refs[:-dp], refs[-dp:]
    held = [unpacked(ref, cols) for ref in slot_refs]
    values, ids = [jnp.concatenate(blocks, axis=0) for blocks in zip(*held)]
    values, ids = values.astype(jnp.bfloat16), ids.astype(jnp.int32)
    count = values.shape[0]
    block = over(jnp.maximum(ids, 0), shard)
    target = jnp.where(ids < 0, -1, (block ^ d) * shard + ids - block * shard)
    picked = one_hot(iota((count, dp * shard), 1) == target)
    embed = lax.dot_general(picked, values, (((0,), (0,)), ((), ())), preferred_element_type=jnp.float32)
    for t, out_ref in enumerate(out_refs):
        out_ref[...] = stacked(embed[t * shard : (t + 1) * shard])


def gather_kernel(*refs):
    d, z, core = place()
    parts, out_ref = refs[:-1], refs[-1]
    cols = out_ref.shape[1] // len(parts)
    for t, part in enumerate(parts):
        out_ref[:, pl.ds(pl.multiple_of((d ^ t) * cols, LANES), cols)] = unstacked(part[...])


def sum_kernel(chips, shard, *refs):
    dp = len(refs) - chips
    total = refs[0][...]
    for t in range(1, dp):
        total = total + refs[t][...]
    for s, out_ref in enumerate(refs[dp:]):
        out_ref[...] = stacked(total[s * shard : (s + 1) * shard])


def step(spot, piece_ref, embed_ref, master_ref, first_ref, second_ref):
    gradient = unstacked(piece_ref[...]) + embed_ref[:, spot]
    master = master_ref[:, spot]
    first_new = 0.9 * first_ref[:, spot] + 0.1 * gradient
    second_new = 0.95 * second_ref[:, spot] + 0.05 * gradient * gradient
    first_hat = first_new / (1.0 - 0.9**STEP)
    second_hat = second_new / (1.0 - 0.95**STEP)
    master_new = master - 0.05 * (first_hat / (jnp.sqrt(second_hat) + 1e-08) + 0.1 * master)
    return master_new, first_new, second_new


def chip_spot(z, s, piece_ref):
    cols = piece_ref.shape[1] * 2
    return pl.ds(pl.multiple_of((z ^ s) * cols, LANES), cols)


def rows_kernel(members, *refs):
    d, z, core = place()
    state, pieces, out_ref = refs[:4], refs[4:-1], refs[-1]
    table = [step(chip_spot(z, s, piece), piece, *state)[0] for s, piece in zip(members, pieces)]
    table = [table[members.index(s)] for s in range(len(members))]
    out_ref[...] = jnp.concatenate(table, axis=0).astype(jnp.bfloat16)


def adam_kernel(members, dp, shard, *refs):
    d, z, core = place()
    state, pieces, outs, order_ref = refs[:4], refs[4:-4], refs[-4:-1], refs[-1]
    rows = dp * shard
    total = len(members) * rows
    r = iota((total, total), 0)
    s = over(r, rows)
    e = over(r - s * rows, shard)
    i = r - s * rows - e * shard
    order_ref[...] = one_hot(iota((total, total), 1) == ((e ^ d) * len(members) + s) * shard + i)
    for s, piece in zip(members, pieces):
        spot = chip_spot(z, s, piece)
        for out_ref, value in zip(outs, step(spot, piece, *state)):
            out_ref[:, spot] = value


def table_kernel(chips, dp, shard, order_ref, *refs):
    d, z, core = place()
    parts, (out_hbm, out_ref, sems) = refs[-4::-1], refs[-3:]
    cols = parts[0].shape[1]
    rows = dp * shard
    values = jnp.concatenate([part[...] for part in parts], axis=0)
    values = exact(order_ref[...], values).astype(jnp.bfloat16)
    copies = []
    for s in range(chips):
        out_ref[s] = values[s * rows : (s + 1) * rows]
        spot = pl.ds(pl.multiple_of((z ^ s) * cols, LANES), cols)
        copies.append(pltpu.make_async_copy(out_ref.at[s], out_hbm.at[:, spot], sems.at[s]))
        copies[-1].start()
    for copy in copies:
        copy.wait()


def shaped(shape, kind):
    return jax.ShapeDtypeStruct(shape, kind)


def run(kernel, outs, *args, cost=1, hbm=0, out_hbm=False, scratch=()):
    moved = sum(x.size * x.dtype.itemsize for x in (*args, *jax.tree.leaves(outs)))
    vmem = pl.BlockSpec(memory_space=pltpu.VMEM)
    args = [pltpu.with_memory_space_constraint(x, pltpu.HBM) if n < hbm else x for n, x in enumerate(args)]
    return pl.pallas_call(
        kernel,
        out_shape=outs,
        in_specs=[pl.BlockSpec(memory_space=pltpu.HBM)] * hbm + [vmem] * (len(args) - hbm),
        out_specs=jax.tree.map(lambda _: pl.BlockSpec(memory_space=pltpu.HBM) if out_hbm else vmem, outs),
        scratch_shapes=list(scratch),
        cost_estimate=pl.CostEstimate(flops=0, bytes_accessed=moved * cost, transcendentals=0),
        compiler_params=pltpu.CompilerParams(vmem_limit_bytes=VMEM_LIMIT),
    )(*args)


def local_copies(*args):
    return [pltpu.VMEM(x.shape, x.dtype) for x in args] + [pltpu.SemaphoreType.DMA((len(args),))]


def aligned(
    hidden,
    logit_grad,
    predict_mask,
    slot_grads,
    slot_rows,
    slot_counts,
    master,
    first_moment,
    second_moment,
):
    vocab = lax.axis_size("vocab")
    dp = lax.axis_size("dp")
    chips = vocab // CORES
    rows = logit_grad.shape[1]
    shard = master.shape[0]
    cols = hidden.shape[1] * CORES
    owners, cap, width = slot_grads.shape[1:]
    group = cap * chips
    far_first = (*range(chips // 2, chips), *reversed(range(chips // 2)))
    bf16, f32 = jnp.bfloat16, jnp.float32

    def send(x, s, away=0):
        move = s * CORES + away
        return lax.ppermute(x, "vocab", [(v, v ^ move) for v in range(vocab)]) if move else x

    def send_dp(x, t):
        return lax.ppermute(x, "dp", [(i, i ^ t) for i in range(dp)]) if t else x

    hidden_other = send(hidden, 0, 1)
    slots_in = (
        slot_grads[0].transpose(1, 0, 2).reshape(cap * owners, width),
        slot_rows.transpose(2, 0, 1),
        slot_counts,
    )
    slots_own, slots_other = run(
        functools.partial(slots_kernel, chips, dp),
        [shaped((group, width + LANES), bf16)] * CORES,
        *slots_in,
        hbm=3,
        scratch=local_copies(*slots_in),
    )
    slots_other = send(slots_other, 0, 1)
    slots_other, hidden_other = lax.optimization_barrier((slots_other, hidden_other))
    quarter = width // dp
    packets = [shaped((vocab * cap * quarter // LANES + ID_ROWS, LANES), bf16)]
    quarters = run(functools.partial(peers_kernel, dp), packets * dp, slots_own, slots_other)
    held = run(fetch_kernel, shaped(hidden.shape, bf16), hidden, hbm=1, scratch=[pltpu.SemaphoreType.DMA])
    quarters = [send_dp(quarters[t], t) for t in reversed(range(dp))]
    quarters[-1], held = lax.optimization_barrier((quarters[-1], held))
    messages = run(functools.partial(owners_kernel, chips, cap, quarter), packets * chips, *quarters)
    columns = [logit_grad.T]
    for s in range(1, chips):
        columns.append(send(columns[s - 1], 1) if s % 2 else send(columns[0], s))
    head = run(
        functools.partial(head_kernel, chips, dp, shard),
        [shaped((chips * shard, cols), f32)] * dp,
        predict_mask[None, :],
        held,
        hidden_other,
        *columns,
    )
    embed = run(
        functools.partial(embed_kernel, dp, shard, quarter),
        [shaped((2 * shard, quarter // 2), f32)] * dp,
        *[send(messages[s], s) for s in far_first],
    )
    sums = run(
        functools.partial(sum_kernel, chips, shard),
        [shaped((2 * shard, cols // 2), f32)] * chips,
        *[send_dp(head[t], t) for t in reversed(range(dp))],
    )
    pieces = [send(sums[s], s) for s in far_first]
    embed = run(gather_kernel, shaped((shard, width), f32), *[send_dp(embed[t], t) for t in range(dp)])
    state = (embed, master, first_moment, second_moment)
    table = run(functools.partial(rows_kernel, far_first), shaped((chips * shard, cols), bf16), *state, *pieces)
    master_new, first_new, second_new, order = run(
        functools.partial(adam_kernel, far_first, dp, shard),
        [shaped(master.shape, f32)] * 3 + [shaped((chips * rows, chips * rows), bf16)],
        *state,
        *pieces,
    )
    table = run(
        functools.partial(table_kernel, chips, dp, shard),
        shaped((rows, width), bf16),
        order,
        *[send_dp(table, t) for t in reversed(range(dp))],
        out_hbm=True,
        scratch=[pltpu.VMEM((chips, rows, cols), bf16), pltpu.SemaphoreType.DMA((chips,))],
    )
    return (master_new, first_new, second_new, table)


def plain(
    hidden,
    logit_grad,
    predict_mask,
    slot_grads,
    slot_rows,
    slot_counts,
    master,
    first_moment,
    second_moment,
):
    vocab = lax.axis_size("vocab")
    dp = lax.axis_size("dp")
    chips = vocab // CORES
    rows = logit_grad.shape[1]
    shard = master.shape[0]
    cols = hidden.shape[1] * CORES
    owners, cap, width = slot_grads.shape[1:]
    here = lax.axis_index("vocab")
    core = here % CORES
    z = here // CORES
    d = lax.axis_index("dp")

    def to_core(x):
        return lax.ppermute(x, "vocab", [(v, v ^ 1) for v in range(vocab)])

    def to_chip(x, s):
        return lax.ppermute(x, "vocab", [(v, v ^ (s * CORES)) for v in range(vocab)])

    def to_dp(x, t):
        return lax.ppermute(x, "dp", [(i, i ^ t) for i in range(dp)])

    label = jnp.arange(rows, dtype=jnp.int32)
    source = ((label // shard) ^ d) * shard + label % shard
    reorder = (source[:, None] == label[None, :]).astype(jnp.bfloat16)
    masked = logit_grad * predict_mask.astype(jnp.bfloat16)[:, None]
    masked = lax.dot_general(reorder, masked, (((1,), (1,)), ((), ())), preferred_element_type=jnp.bfloat16)

    slot_index = jnp.arange(cap, dtype=jnp.int32)[None, :]
    ids = ((slot_rows[0] // shard) ^ d) * shard + slot_rows[0] % shard
    ids = jnp.where(slot_index < slot_counts[0][:, None], ids, -1).astype(jnp.bfloat16)
    ids = jnp.broadcast_to(ids[:, :, None, None], (owners, cap, chips, LANES))
    slots = slot_grads[0].reshape(owners, cap, chips, cols)
    slots = jnp.concatenate([slots, ids], axis=3).reshape(chips, CORES, cap, chips, cols + LANES)
    mine = lax.dynamic_index_in_dim(slots, core, 1, keepdims=False)
    other = lax.dynamic_index_in_dim(slots, 1 - core, 1, keepdims=False)
    hidden_other = to_core(hidden)
    other = to_core(other)
    masked = [masked] + [to_chip(masked, s) for s in range(1, chips)]
    both = jnp.stack([mine, other]).reshape(CORES * chips * cap, chips, cols + LANES)
    slots = [lax.dynamic_index_in_dim(both, z ^ s, 1, keepdims=False) for s in range(chips)]
    slots = [slots[0]] + [to_chip(slots[s], s) for s in range(1, chips)]

    swap = core == 1
    low = jnp.where(swap, hidden_other, hidden)
    high = jnp.where(swap, hidden, hidden_other)
    wide = jnp.concatenate([low, high], axis=1)
    slots = jnp.concatenate(slots, axis=0)
    owner = (jnp.arange(slots.shape[0], dtype=jnp.int32) // cap) % chips
    ids = slots[:, cols].astype(jnp.int32)
    ids = jnp.where(ids < 0, -1, (owner ^ z) * rows + ids)
    picked = (jnp.arange(chips * rows, dtype=jnp.int32)[:, None] == ids[None, :]).astype(jnp.bfloat16)
    part = jnp.dot(jnp.concatenate(masked, axis=0), wide, preferred_element_type=jnp.float32)
    part = part + jnp.dot(picked, slots[:, :cols], preferred_element_type=jnp.float32)
    part = part.reshape(chips, dp, shard, cols)
    part = [part[:, t].reshape(chips * shard, cols) for t in range(dp)]
    total = part[0]
    for t in range(1, dp):
        total = total + to_dp(part[t], t)
    total = total.reshape(chips, shard, CORES, cols // CORES).transpose(0, 2, 1, 3)
    total = total.reshape(chips, CORES * shard, cols // CORES)
    pieces = [total[0]] + [to_chip(total[s], s) for s in range(1, chips)]
    pieces = jnp.stack(pieces).reshape(chips, CORES, shard, cols // CORES).transpose(0, 2, 1, 3)
    pieces = pieces.reshape(chips, shard, cols)
    gradient = jnp.concatenate([lax.dynamic_index_in_dim(pieces, z ^ s, 0, keepdims=False) for s in range(chips)], axis=1)
    first_new = 0.9 * first_moment + 0.1 * gradient
    second_new = 0.95 * second_moment + 0.05 * gradient * gradient
    first_hat = first_new / (1.0 - 0.9**STEP)
    second_hat = second_new / (1.0 - 0.95**STEP)
    master_new = master - 0.05 * (first_hat / (jnp.sqrt(second_hat) + 1e-08) + 0.1 * master)
    table = master_new.astype(jnp.bfloat16)
    table = table.reshape(shard, chips, cols).transpose(1, 0, 2).reshape(chips * shard, cols)
    table = jnp.stack([table] + [to_dp(table, t) for t in range(1, dp)])
    table = jnp.stack([lax.dynamic_index_in_dim(table, d ^ t, 0, keepdims=False) for t in range(dp)])
    table = table.reshape(dp, chips, shard, cols).transpose(0, 2, 1, 3).reshape(rows, width)
    return (master_new, first_new, second_new, table)


def local(hidden, logit_grad, predict_mask, slot_grads, *rest):
    vocab = lax.axis_size("vocab")
    fits = hidden.shape[1] % LANES == 0 and logit_grad.shape[1] % 16 == 0
    slots = vocab * slot_grads.shape[2]
    fits = fits and slots % 16 == 0 and slots <= LANES and lax.axis_size("dp") == vocab // CORES
    fits = fits and slot_grads.shape[3] // lax.axis_size("dp") % (2 * LANES) == 0
    step = aligned if fits else plain
    return step(hidden, logit_grad, predict_mask, slot_grads, *rest)


def solution(mesh):
    in_specs = (
        P("dp", "vocab"),
        P("dp", "vocab"),
        P("dp"),
        P(("dp", "vocab"), None, None, None),
        P(("dp", "vocab"), None, None),
        P(("dp", "vocab"), None),
        P(("vocab", "dp"), None),
        P(("vocab", "dp"), None),
        P(("vocab", "dp"), None),
    )
    out_specs = (
        P(("vocab", "dp"), None),
        P(("vocab", "dp"), None),
        P(("vocab", "dp"), None),
        P("vocab", None),
    )
    return jax.shard_map(local, mesh=mesh, in_specs=in_specs, out_specs=out_specs, check_vma=False)
```

```python
import functools

import jax
import jax.numpy as jnp
from jax import lax
from jax.experimental import pallas as pl
from jax.experimental.pallas import tpu as pltpu
from jax.sharding import PartitionSpec as P

STEP = 8
CORES = 2
LANES = 128
ID_ROWS = 16
VMEM_LIMIT = 24 * 1024 * 1024


def place():
    here = lax.axis_index("vocab")
    return lax.axis_index("dp"), lax.shift_right_logical(here, 1), here & 1


def iota(shape, axis):
    return lax.broadcasted_iota(jnp.int32, shape, axis)


def over(x, n):
    return ((x.astype(jnp.float32) + 0.5) * (1.0 / n)).astype(jnp.int32)


def one_hot(flag):
    return jnp.where(flag, 1.0, 0.0).astype(jnp.bfloat16)


def exact(left, right):
    return jnp.dot(left, right, preferred_element_type=jnp.float32)


def slots_kernel(chips, dp, slots_hbm, rows_hbm, counts_hbm, own_out, other_out, slots_ref, rows_ref, counts_ref, sems):
    d, z, core = place()
    copies = [
        pltpu.make_async_copy(rows_hbm, rows_ref, sems.at[0]),
        pltpu.make_async_copy(counts_hbm, counts_ref, sems.at[1]),
        pltpu.make_async_copy(slots_hbm, slots_ref, sems.at[2]),
    ]
    for copy in copies:
        copy.start()
    cap, owners = rows_ref.shape[0], rows_ref.shape[2]
    count = cap * owners
    group = cap * chips
    part = slots_ref.shape[1] // dp
    q = iota((count, count), 0)
    away = jnp.where(q >= group, 1, 0)
    q = q - away * group
    s = over(q, cap)
    wanted = (q - s * cap) * owners + (s ^ z) * CORES + (away ^ core)
    pick = one_hot(iota((count, count), 1) == wanted)
    own_lane = iota((count, owners), 1) == iota((count, owners), 0) % owners
    for copy in copies[:2]:
        copy.wait()
    rows = jnp.broadcast_to(rows_ref[...], (cap, owners, owners)).reshape(count, owners)
    rows = jnp.sum(jnp.where(own_lane, rows, 0), axis=1, keepdims=True)
    live = jnp.broadcast_to(counts_ref[...], (count, owners))
    live = jnp.sum(jnp.where(own_lane, live, 0), axis=1, keepdims=True)
    ids = jnp.where(over(iota((count, 1), 0), owners) < live, rows, -1)
    ids = jnp.broadcast_to(ids, (count, LANES)).astype(jnp.bfloat16)
    ids = exact(pick, ids)
    copies[2].wait()
    outs = ((own_out, slice(0, group)), (other_out, slice(group, count)))
    for t in range(dp):
        values = exact(pick, slots_ref[:, pl.ds(pl.multiple_of((d ^ t) * part, LANES), part)])
        for out_ref, spot in outs:
            out_ref[:, t * part : (t + 1) * part] = values[spot].astype(jnp.bfloat16)
    for out_ref, spot in outs:
        out_ref[:, dp * part :] = ids[spot].astype(jnp.bfloat16)


def diagonal(values, axis):
    return jnp.sum(jnp.where(iota(values.shape, 0) == iota(values.shape, 1), values, 0.0), axis=axis, keepdims=True)


def packed(values, ids):
    ids = jnp.broadcast_to(ids, (ids.shape[0], LANES))
    ids = jnp.broadcast_to(diagonal(ids, 0), (ID_ROWS, LANES))
    blocks = [values[:, c : c + LANES] for c in range(0, values.shape[1], LANES)]
    return jnp.concatenate([*blocks, ids], axis=0).astype(jnp.bfloat16)


def unpacked(ref, cols):
    group = (ref.shape[0] - ID_ROWS) // (cols // LANES)
    row = ref[cols // LANES * group :, :].astype(jnp.float32)[:1]
    ids = diagonal(jnp.broadcast_to(row, (group, LANES)), 1)
    values = [ref[c * group : (c + 1) * group, :] for c in range(cols // LANES)]
    return jnp.concatenate(values, axis=1).astype(jnp.float32), ids


def peers_kernel(dp, own_ref, other_ref, *out_refs):
    part = (own_ref.shape[1] - LANES) // dp
    ids = [ref[:, dp * part :].astype(jnp.float32) for ref in (own_ref, other_ref)]
    ids = jnp.concatenate(ids, axis=0)[:, :1]
    for t, out_ref in enumerate(out_refs):
        values = [ref[:, t * part : (t + 1) * part].astype(jnp.float32) for ref in (own_ref, other_ref)]
        out_ref[...] = packed(jnp.concatenate(values, axis=0), ids)


def owners_kernel(chips, cap, cols, *refs):
    in_refs, out_refs = refs[:-chips], refs[-chips:]
    held = [unpacked(ref, cols) for ref in in_refs]
    group = cap * chips
    for s, out_ref in enumerate(out_refs):
        spots = [slice(core * group + s * cap, core * group + (s + 1) * cap) for core in range(CORES)]
        rows = [[block[spot] for block in both for spot in spots] for both in zip(*held)]
        values, ids = [jnp.concatenate(blocks, axis=0) for blocks in rows]
        out_ref[...] = packed(values, ids)


def fetch_kernel(hidden_hbm, hidden_ref, sem):
    copy = pltpu.make_async_copy(hidden_hbm, hidden_ref, sem)
    copy.start()
    copy.wait()


def head_kernel(chips, dp, shard, mask_ref, own_ref, other_ref, *refs):
    d, z, core = place()
    parts, outs = refs[:chips], refs[chips:]
    rows = dp * shard
    total = chips * rows
    cols = own_ref.shape[1]
    size = chips * shard
    r = iota((total, total), 0)
    t = over(r, size)
    s = over(r - t * size, shard)
    i = r - t * size - s * shard
    order = one_hot(iota((total, total), 1) == s * rows + (t ^ d) * shard + i)
    mask = mask_ref[...].astype(jnp.float32).astype(jnp.bfloat16)
    columns = jnp.concatenate([part[...] for part in parts], axis=0) * mask
    columns = exact(order, columns).astype(jnp.bfloat16)
    for at, ref in ((core, own_ref), (1 - core, other_ref)):
        head = exact(columns, ref[...])
        spot = pl.ds(pl.multiple_of(at * cols, LANES), cols)
        for t, out_ref in enumerate(outs):
            out_ref[:, spot] = head[t * size : (t + 1) * size]


def stacked(rows):
    cut = rows.shape[1] // 2
    return jnp.concatenate([rows[:, :cut], rows[:, cut:]], axis=0)


def unstacked(rows):
    cut = rows.shape[0] // 2
    return jnp.concatenate([rows[:cut], rows[cut:]], axis=1)


def embed_kernel(dp, shard, cols, *refs):
    d, z, core = place()
    slot_refs, out_refs = refs[:-dp], refs[-dp:]
    held = [unpacked(ref, cols) for ref in slot_refs]
    values, ids = [jnp.concatenate(blocks, axis=0) for blocks in zip(*held)]
    values, ids = values.astype(jnp.bfloat16), ids.astype(jnp.int32)
    count = values.shape[0]
    block = over(jnp.maximum(ids, 0), shard)
    target = jnp.where(ids < 0, -1, (block ^ d) * shard + ids - block * shard)
    picked = one_hot(iota((count, dp * shard), 1) == target)
    embed = lax.dot_general(picked, values, (((0,), (0,)), ((), ())), preferred_element_type=jnp.float32)
    for t, out_ref in enumerate(out_refs):
        out_ref[...] = stacked(embed[t * shard : (t + 1) * shard])


def gather_kernel(*refs):
    d, z, core = place()
    parts, out_ref = refs[:-1], refs[-1]
    cols = out_ref.shape[1] // len(parts)
    for t, part in enumerate(parts):
        out_ref[:, pl.ds(pl.multiple_of((d ^ t) * cols, LANES), cols)] = unstacked(part[...])


def sum_kernel(chips, shard, *refs):
    dp = len(refs) - chips
    total = refs[0][...]
    for t in range(1, dp):
        total = total + refs[t][...]
    for s, out_ref in enumerate(refs[dp:]):
        out_ref[...] = stacked(total[s * shard : (s + 1) * shard])


def step(spot, piece_ref, embed_ref, master_ref, first_ref, second_ref):
    gradient = unstacked(piece_ref[...]) + embed_ref[:, spot]
    master = master_ref[:, spot]
    first_new = 0.9 * first_ref[:, spot] + 0.1 * gradient
    second_new = 0.95 * second_ref[:, spot] + 0.05 * gradient * gradient
    first_hat = first_new / (1.0 - 0.9**STEP)
    second_hat = second_new / (1.0 - 0.95**STEP)
    master_new = master - 0.05 * (first_hat / (jnp.sqrt(second_hat) + 1e-08) + 0.1 * master)
    return master_new, first_new, second_new


def chip_spot(z, s, piece_ref):
    cols = piece_ref.shape[1] * 2
    return pl.ds(pl.multiple_of((z ^ s) * cols, LANES), cols)


def rows_kernel(members, *refs):
    d, z, core = place()
    state, pieces, out_ref = refs[:4], refs[4:-1], refs[-1]
    table = [step(chip_spot(z, s, piece), piece, *state)[0] for s, piece in zip(members, pieces)]
    table = [table[members.index(s)] for s in range(len(members))]
    out_ref[...] = jnp.concatenate(table, axis=0).astype(jnp.bfloat16)


def adam_kernel(members, dp, shard, *refs):
    d, z, core = place()
    state, pieces, outs, order_ref = refs[:4], refs[4:-4], refs[-4:-1], refs[-1]
    rows = dp * shard
    total = len(members) * rows
    r = iota((total, total), 0)
    s = over(r, rows)
    e = over(r - s * rows, shard)
    i = r - s * rows - e * shard
    order_ref[...] = one_hot(iota((total, total), 1) == ((e ^ d) * len(members) + s) * shard + i)
    for s, piece in zip(members, pieces):
        spot = chip_spot(z, s, piece)
        for out_ref, value in zip(outs, step(spot, piece, *state)):
            out_ref[:, spot] = value


def table_kernel(chips, dp, shard, order_ref, *refs):
    d, z, core = place()
    parts, (out_hbm, out_ref, sems) = refs[-4::-1], refs[-3:]
    cols = parts[0].shape[1]
    rows = dp * shard
    values = jnp.concatenate([part[...] for part in parts], axis=0)
    values = exact(order_ref[...], values).astype(jnp.bfloat16)
    copies = []
    for s in range(chips):
        out_ref[s] = values[s * rows : (s + 1) * rows]
        spot = pl.ds(pl.multiple_of((z ^ s) * cols, LANES), cols)
        copies.append(pltpu.make_async_copy(out_ref.at[s], out_hbm.at[:, spot], sems.at[s]))
        copies[-1].start()
    for copy in copies:
        copy.wait()


def shaped(shape, kind):
    return jax.ShapeDtypeStruct(shape, kind)


def run(kernel, outs, *args, cost=1, hbm=0, out_hbm=False, scratch=()):
    moved = sum(x.size * x.dtype.itemsize for x in (*args, *jax.tree.leaves(outs)))
    vmem = pl.BlockSpec(memory_space=pltpu.VMEM)
    args = [pltpu.with_memory_space_constraint(x, pltpu.HBM) if n < hbm else x for n, x in enumerate(args)]
    return pl.pallas_call(
        kernel,
        out_shape=outs,
        in_specs=[pl.BlockSpec(memory_space=pltpu.HBM)] * hbm + [vmem] * (len(args) - hbm),
        out_specs=jax.tree.map(lambda _: pl.BlockSpec(memory_space=pltpu.HBM) if out_hbm else vmem, outs),
        scratch_shapes=list(scratch),
        cost_estimate=pl.CostEstimate(flops=0, bytes_accessed=moved * cost, transcendentals=0),
        compiler_params=pltpu.CompilerParams(vmem_limit_bytes=VMEM_LIMIT),
    )(*args)


def local_copies(*args):
    return [pltpu.VMEM(x.shape, x.dtype) for x in args] + [pltpu.SemaphoreType.DMA((len(args),))]


def aligned(
    hidden,
    logit_grad,
    predict_mask,
    slot_grads,
    slot_rows,
    slot_counts,
    master,
    first_moment,
    second_moment,
):
    vocab = lax.axis_size("vocab")
    dp = lax.axis_size("dp")
    chips = vocab // CORES
    rows = logit_grad.shape[1]
    shard = master.shape[0]
    cols = hidden.shape[1] * CORES
    owners, cap, width = slot_grads.shape[1:]
    group = cap * chips
    far_first = (*range(chips // 2, chips), *reversed(range(chips // 2)))
    bf16, f32 = jnp.bfloat16, jnp.float32

    def send(x, s, away=0):
        move = s * CORES + away
        return lax.ppermute(x, "vocab", [(v, v ^ move) for v in range(vocab)]) if move else x

    def send_dp(x, t):
        return lax.ppermute(x, "dp", [(i, i ^ t) for i in range(dp)]) if t else x

    hidden_other = send(hidden, 0, 1)
    slots_in = (
        slot_grads[0].transpose(1, 0, 2).reshape(cap * owners, width),
        slot_rows.transpose(2, 0, 1),
        slot_counts,
    )
    slots_own, slots_other = run(
        functools.partial(slots_kernel, chips, dp),
        [shaped((group, width + LANES), bf16)] * CORES,
        *slots_in,
        hbm=3,
        scratch=local_copies(*slots_in),
    )
    slots_other = send(slots_other, 0, 1)
    slots_other, hidden_other = lax.optimization_barrier((slots_other, hidden_other))
    quarter = width // dp
    packets = [shaped((vocab * cap * quarter // LANES + ID_ROWS, LANES), bf16)]
    quarters = run(functools.partial(peers_kernel, dp), packets * dp, slots_own, slots_other)
    held = run(fetch_kernel, shaped(hidden.shape, bf16), hidden, hbm=1, scratch=[pltpu.SemaphoreType.DMA])
    quarters = [send_dp(quarters[t], t) for t in reversed(range(dp))]
    quarters[-1], held = lax.optimization_barrier((quarters[-1], held))
    messages = run(functools.partial(owners_kernel, chips, cap, quarter), packets * chips, *quarters)
    columns = [logit_grad.T]
    for s in range(1, chips):
        columns.append(send(columns[s - 1], 1) if s % 2 else send(columns[0], s))
    head = run(
        functools.partial(head_kernel, chips, dp, shard),
        [shaped((chips * shard, cols), f32)] * dp,
        predict_mask[None, :],
        held,
        hidden_other,
        *columns,
    )
    embed = run(
        functools.partial(embed_kernel, dp, shard, quarter),
        [shaped((2 * shard, quarter // 2), f32)] * dp,
        *[send(messages[s], s) for s in far_first],
    )
    sums = run(
        functools.partial(sum_kernel, chips, shard),
        [shaped((2 * shard, cols // 2), f32)] * chips,
        *[send_dp(head[t], t) for t in reversed(range(dp))],
    )
    half = chips // 2
    pieces = [send(sums[s], s) for s in far_first[:half]]
    sums, _ = lax.optimization_barrier((list(sums), pieces[0]))
    pieces += [send(sums[s], s) for s in far_first[half:]]
    last = send_dp(embed[dp - 1], dp - 1)
    rest, last = lax.optimization_barrier((list(embed[: dp - 1]), last))
    embed = run(gather_kernel, shaped((shard, width), f32), *[send_dp(rest[t], t) for t in range(dp - 1)], last)
    state = (embed, master, first_moment, second_moment)
    table = run(functools.partial(rows_kernel, far_first), shaped((chips * shard, cols), bf16), *state, *pieces)
    master_new, first_new, second_new, order = run(
        functools.partial(adam_kernel, far_first, dp, shard),
        [shaped(master.shape, f32)] * 3 + [shaped((chips * rows, chips * rows), bf16)],
        *state,
        *pieces,
    )
    table = run(
        functools.partial(table_kernel, chips, dp, shard),
        shaped((rows, width), bf16),
        order,
        *[send_dp(table, t) for t in reversed(range(dp))],
        out_hbm=True,
        scratch=[pltpu.VMEM((chips, rows, cols), bf16), pltpu.SemaphoreType.DMA((chips,))],
    )
    return (master_new, first_new, second_new, table)


def plain(
    hidden,
    logit_grad,
    predict_mask,
    slot_grads,
    slot_rows,
    slot_counts,
    master,
    first_moment,
    second_moment,
):
    vocab = lax.axis_size("vocab")
    dp = lax.axis_size("dp")
    chips = vocab // CORES
    rows = logit_grad.shape[1]
    shard = master.shape[0]
    cols = hidden.shape[1] * CORES
    owners, cap, width = slot_grads.shape[1:]
    here = lax.axis_index("vocab")
    core = here % CORES
    z = here // CORES
    d = lax.axis_index("dp")

    def to_core(x):
        return lax.ppermute(x, "vocab", [(v, v ^ 1) for v in range(vocab)])

    def to_chip(x, s):
        return lax.ppermute(x, "vocab", [(v, v ^ (s * CORES)) for v in range(vocab)])

    def to_dp(x, t):
        return lax.ppermute(x, "dp", [(i, i ^ t) for i in range(dp)])

    label = jnp.arange(rows, dtype=jnp.int32)
    source = ((label // shard) ^ d) * shard + label % shard
    reorder = (source[:, None] == label[None, :]).astype(jnp.bfloat16)
    masked = logit_grad * predict_mask.astype(jnp.bfloat16)[:, None]
    masked = lax.dot_general(reorder, masked, (((1,), (1,)), ((), ())), preferred_element_type=jnp.bfloat16)

    slot_index = jnp.arange(cap, dtype=jnp.int32)[None, :]
    ids = ((slot_rows[0] // shard) ^ d) * shard + slot_rows[0] % shard
    ids = jnp.where(slot_index < slot_counts[0][:, None], ids, -1).astype(jnp.bfloat16)
    ids = jnp.broadcast_to(ids[:, :, None, None], (owners, cap, chips, LANES))
    slots = slot_grads[0].reshape(owners, cap, chips, cols)
    slots = jnp.concatenate([slots, ids], axis=3).reshape(chips, CORES, cap, chips, cols + LANES)
    mine = lax.dynamic_index_in_dim(slots, core, 1, keepdims=False)
    other = lax.dynamic_index_in_dim(slots, 1 - core, 1, keepdims=False)
    hidden_other = to_core(hidden)
    other = to_core(other)
    masked = [masked] + [to_chip(masked, s) for s in range(1, chips)]
    both = jnp.stack([mine, other]).reshape(CORES * chips * cap, chips, cols + LANES)
    slots = [lax.dynamic_index_in_dim(both, z ^ s, 1, keepdims=False) for s in range(chips)]
    slots = [slots[0]] + [to_chip(slots[s], s) for s in range(1, chips)]

    swap = core == 1
    low = jnp.where(swap, hidden_other, hidden)
    high = jnp.where(swap, hidden, hidden_other)
    wide = jnp.concatenate([low, high], axis=1)
    slots = jnp.concatenate(slots, axis=0)
    owner = (jnp.arange(slots.shape[0], dtype=jnp.int32) // cap) % chips
    ids = slots[:, cols].astype(jnp.int32)
    ids = jnp.where(ids < 0, -1, (owner ^ z) * rows + ids)
    picked = (jnp.arange(chips * rows, dtype=jnp.int32)[:, None] == ids[None, :]).astype(jnp.bfloat16)
    part = jnp.dot(jnp.concatenate(masked, axis=0), wide, preferred_element_type=jnp.float32)
    part = part + jnp.dot(picked, slots[:, :cols], preferred_element_type=jnp.float32)
    part = part.reshape(chips, dp, shard, cols)
    part = [part[:, t].reshape(chips * shard, cols) for t in range(dp)]
    total = part[0]
    for t in range(1, dp):
        total = total + to_dp(part[t], t)
    total = total.reshape(chips, shard, CORES, cols // CORES).transpose(0, 2, 1, 3)
    total = total.reshape(chips, CORES * shard, cols // CORES)
    pieces = [total[0]] + [to_chip(total[s], s) for s in range(1, chips)]
    pieces = jnp.stack(pieces).reshape(chips, CORES, shard, cols // CORES).transpose(0, 2, 1, 3)
    pieces = pieces.reshape(chips, shard, cols)
    gradient = jnp.concatenate([lax.dynamic_index_in_dim(pieces, z ^ s, 0, keepdims=False) for s in range(chips)], axis=1)
    first_new = 0.9 * first_moment + 0.1 * gradient
    second_new = 0.95 * second_moment + 0.05 * gradient * gradient
    first_hat = first_new / (1.0 - 0.9**STEP)
    second_hat = second_new / (1.0 - 0.95**STEP)
    master_new = master - 0.05 * (first_hat / (jnp.sqrt(second_hat) + 1e-08) + 0.1 * master)
    table = master_new.astype(jnp.bfloat16)
    table = table.reshape(shard, chips, cols).transpose(1, 0, 2).reshape(chips * shard, cols)
    table = jnp.stack([table] + [to_dp(table, t) for t in range(1, dp)])
    table = jnp.stack([lax.dynamic_index_in_dim(table, d ^ t, 0, keepdims=False) for t in range(dp)])
    table = table.reshape(dp, chips, shard, cols).transpose(0, 2, 1, 3).reshape(rows, width)
    return (master_new, first_new, second_new, table)


def local(hidden, logit_grad, predict_mask, slot_grads, *rest):
    vocab = lax.axis_size("vocab")
    fits = hidden.shape[1] % LANES == 0 and logit_grad.shape[1] % 16 == 0
    slots = vocab * slot_grads.shape[2]
    fits = fits and slots % 16 == 0 and slots <= LANES and lax.axis_size("dp") == vocab // CORES
    fits = fits and slot_grads.shape[3] // lax.axis_size("dp") % (2 * LANES) == 0
    step = aligned if fits else plain
    return step(hidden, logit_grad, predict_mask, slot_grads, *rest)


def solution(mesh):
    in_specs = (
        P("dp", "vocab"),
        P("dp", "vocab"),
        P("dp"),
        P(("dp", "vocab"), None, None, None),
        P(("dp", "vocab"), None, None),
        P(("dp", "vocab"), None),
        P(("vocab", "dp"), None),
        P(("vocab", "dp"), None),
        P(("vocab", "dp"), None),
    )
    out_specs = (
        P(("vocab", "dp"), None),
        P(("vocab", "dp"), None),
        P(("vocab", "dp"), None),
        P("vocab", None),
    )
    return jax.shard_map(local, mesh=mesh, in_specs=in_specs, out_specs=out_specs, check_vma=False)
```

```python
import functools

import jax
import jax.numpy as jnp
from jax import lax
from jax.experimental import pallas as pl
from jax.experimental.pallas import tpu as pltpu
from jax.sharding import PartitionSpec as P

STEP = 8
CORES = 2
LANES = 128
ID_ROWS = 16
VMEM_LIMIT = 24 * 1024 * 1024


def place():
    here = lax.axis_index("vocab")
    return lax.axis_index("dp"), lax.shift_right_logical(here, 1), here & 1


def iota(shape, axis):
    return lax.broadcasted_iota(jnp.int32, shape, axis)


def over(x, n):
    return ((x.astype(jnp.float32) + 0.5) * (1.0 / n)).astype(jnp.int32)


def one_hot(flag):
    return jnp.where(flag, 1.0, 0.0).astype(jnp.bfloat16)


def exact(left, right):
    return jnp.dot(left, right, preferred_element_type=jnp.float32)


def slots_kernel(chips, dp, slots_hbm, rows_hbm, counts_hbm, own_out, other_out, slots_ref, rows_ref, counts_ref, sems):
    d, z, core = place()
    part = slots_ref.shape[2]
    copies = [
        pltpu.make_async_copy(rows_hbm, rows_ref, sems.at[0]),
        pltpu.make_async_copy(counts_hbm, counts_ref, sems.at[1]),
    ]
    for t in range(dp):
        spot = pl.ds(pl.multiple_of((d ^ t) * part, LANES), part)
        copies.append(pltpu.make_async_copy(slots_hbm.at[:, spot], slots_ref.at[t], sems.at[2 + t]))
    for copy in copies:
        copy.start()
    cap, owners = rows_ref.shape[0], rows_ref.shape[2]
    count = cap * owners
    group = cap * chips
    q = iota((count, count), 0)
    away = jnp.where(q >= group, 1, 0)
    q = q - away * group
    s = over(q, cap)
    wanted = (q - s * cap) * owners + (s ^ z) * CORES + (away ^ core)
    pick = one_hot(iota((count, count), 1) == wanted)
    own_lane = iota((count, owners), 1) == iota((count, owners), 0) % owners
    for copy in copies[:2]:
        copy.wait()
    rows = jnp.broadcast_to(rows_ref[...], (cap, owners, owners)).reshape(count, owners)
    rows = jnp.sum(jnp.where(own_lane, rows, 0), axis=1, keepdims=True)
    live = jnp.broadcast_to(counts_ref[...], (count, owners))
    live = jnp.sum(jnp.where(own_lane, live, 0), axis=1, keepdims=True)
    ids = jnp.where(over(iota((count, 1), 0), owners) < live, rows, -1)
    ids = jnp.broadcast_to(ids, (count, LANES)).astype(jnp.bfloat16)
    ids = exact(pick, ids)
    outs = ((own_out, slice(0, group)), (other_out, slice(group, count)))
    for t in range(dp):
        copies[2 + t].wait()
        values = exact(pick, slots_ref[t])
        for out_ref, spot in outs:
            out_ref[:, t * part : (t + 1) * part] = values[spot].astype(jnp.bfloat16)
    for out_ref, spot in outs:
        out_ref[:, dp * part :] = ids[spot].astype(jnp.bfloat16)


def diagonal(values, axis):
    return jnp.sum(jnp.where(iota(values.shape, 0) == iota(values.shape, 1), values, 0.0), axis=axis, keepdims=True)


def packed(values, ids):
    ids = jnp.broadcast_to(ids, (ids.shape[0], LANES))
    ids = jnp.broadcast_to(diagonal(ids, 0), (ID_ROWS, LANES))
    blocks = [values[:, c : c + LANES] for c in range(0, values.shape[1], LANES)]
    return jnp.concatenate([*blocks, ids], axis=0).astype(jnp.bfloat16)


def unpacked(ref, cols):
    group = (ref.shape[0] - ID_ROWS) // (cols // LANES)
    row = ref[cols // LANES * group :, :].astype(jnp.float32)[:1]
    ids = diagonal(jnp.broadcast_to(row, (group, LANES)), 1)
    values = [ref[c * group : (c + 1) * group, :] for c in range(cols // LANES)]
    return jnp.concatenate(values, axis=1).astype(jnp.float32), ids


def peers_kernel(dp, own_ref, other_ref, *out_refs):
    part = (own_ref.shape[1] - LANES) // dp
    ids = [ref[:, dp * part :].astype(jnp.float32) for ref in (own_ref, other_ref)]
    ids = jnp.concatenate(ids, axis=0)[:, :1]
    for t, out_ref in enumerate(out_refs):
        values = [ref[:, t * part : (t + 1) * part].astype(jnp.float32) for ref in (own_ref, other_ref)]
        out_ref[...] = packed(jnp.concatenate(values, axis=0), ids)


def owners_kernel(chips, cap, cols, *refs):
    in_refs, out_refs = refs[:-chips], refs[-chips:]
    held = [unpacked(ref, cols) for ref in in_refs]
    group = cap * chips
    for s, out_ref in enumerate(out_refs):
        spots = [slice(core * group + s * cap, core * group + (s + 1) * cap) for core in range(CORES)]
        rows = [[block[spot] for block in both for spot in spots] for both in zip(*held)]
        values, ids = [jnp.concatenate(blocks, axis=0) for blocks in rows]
        out_ref[...] = packed(values, ids)


def fetch_kernel(chips, dp, shard, hidden_hbm, hidden_ref, order_ref, sem):
    copy = pltpu.make_async_copy(hidden_hbm, hidden_ref, sem)
    copy.start()
    d, z, core = place()
    rows = dp * shard
    total = chips * rows
    size = chips * shard
    r = iota((total, total), 0)
    t = over(r, size)
    s = over(r - t * size, shard)
    i = r - t * size - s * shard
    order_ref[...] = one_hot(iota((total, total), 1) == s * rows + (t ^ d) * shard + i)
    copy.wait()


def head_kernel(size, mask_ref, order_ref, own_ref, other_ref, *refs):
    d, z, core = place()
    cols = own_ref.shape[1]
    chips = len(refs) - order_ref.shape[0] // size
    parts, outs = refs[:chips], refs[chips:]
    mask = mask_ref[...].astype(jnp.float32).astype(jnp.bfloat16)
    columns = jnp.concatenate([part[...] for part in parts], axis=0) * mask
    columns = exact(order_ref[...], columns).astype(jnp.bfloat16)
    for at, ref in ((core, own_ref), (1 - core, other_ref)):
        head = exact(columns, ref[...])
        spot = pl.ds(pl.multiple_of(at * cols, LANES), cols)
        for t, out_ref in enumerate(outs):
            out_ref[:, spot] = head[t * size : (t + 1) * size]


def stacked(rows):
    cut = rows.shape[1] // 2
    return jnp.concatenate([rows[:, :cut], rows[:, cut:]], axis=0)


def unstacked(rows):
    cut = rows.shape[0] // 2
    return jnp.concatenate([rows[:cut], rows[cut:]], axis=1)


def embed_kernel(dp, shard, cols, *refs):
    d, z, core = place()
    slot_refs, out_refs = refs[:-dp], refs[-dp:]
    held = [unpacked(ref, cols) for ref in slot_refs]
    values, ids = [jnp.concatenate(blocks, axis=0) for blocks in zip(*held)]
    values, ids = values.astype(jnp.bfloat16), ids.astype(jnp.int32)
    count = values.shape[0]
    block = over(jnp.maximum(ids, 0), shard)
    target = jnp.where(ids < 0, -1, (block ^ d) * shard + ids - block * shard)
    picked = one_hot(iota((count, dp * shard), 1) == target)
    embed = lax.dot_general(picked, values, (((0,), (0,)), ((), ())), preferred_element_type=jnp.float32)
    for t, out_ref in enumerate(out_refs):
        out_ref[...] = stacked(embed[t * shard : (t + 1) * shard])


def gather_kernel(*refs):
    d, z, core = place()
    parts, out_ref = refs[:-1], refs[-1]
    cols = out_ref.shape[1] // len(parts)
    for t, part in enumerate(parts):
        out_ref[:, pl.ds(pl.multiple_of((d ^ t) * cols, LANES), cols)] = unstacked(part[...])


def sum_kernel(chips, shard, *refs):
    dp = len(refs) - chips
    total = refs[0][...]
    for t in range(1, dp):
        total = total + refs[t][...]
    for s, out_ref in enumerate(refs[dp:]):
        out_ref[...] = stacked(total[s * shard : (s + 1) * shard])


def step(spot, piece_ref, embed_ref, master_ref, first_ref, second_ref):
    gradient = unstacked(piece_ref[...]) + embed_ref[:, spot]
    master = master_ref[:, spot]
    first_new = 0.9 * first_ref[:, spot] + 0.1 * gradient
    second_new = 0.95 * second_ref[:, spot] + 0.05 * gradient * gradient
    first_hat = first_new / (1.0 - 0.9**STEP)
    second_hat = second_new / (1.0 - 0.95**STEP)
    master_new = master - 0.05 * (first_hat / (jnp.sqrt(second_hat) + 1e-08) + 0.1 * master)
    return master_new, first_new, second_new


def chip_spot(z, s, piece_ref):
    cols = piece_ref.shape[1] * 2
    return pl.ds(pl.multiple_of((z ^ s) * cols, LANES), cols)


def rows_kernel(*refs):
    d, z, core = place()
    state, pieces, out_ref = refs[:4], refs[4:-1], refs[-1]
    table = [step(chip_spot(z, s, piece), piece, *state)[0] for s, piece in enumerate(reversed(pieces))]
    out_ref[...] = jnp.concatenate(table, axis=0).astype(jnp.bfloat16)


def adam_kernel(chips, dp, shard, *refs):
    d, z, core = place()
    state, pieces, outs, order_ref = refs[:4], refs[4:-4], refs[-4:-1], refs[-1]
    rows = dp * shard
    total = chips * rows
    r = iota((total, total), 0)
    s = over(r, rows)
    e = over(r - s * rows, shard)
    i = r - s * rows - e * shard
    order_ref[...] = one_hot(iota((total, total), 1) == ((e ^ d) * chips + s) * shard + i)
    for s, piece in enumerate(reversed(pieces)):
        spot = chip_spot(z, s, piece)
        for out_ref, value in zip(outs, step(spot, piece, *state)):
            out_ref[:, spot] = value


def table_kernel(chips, dp, shard, order_ref, *refs):
    d, z, core = place()
    parts, (out_hbm, out_ref, sems) = refs[-4::-1], refs[-3:]
    cols = parts[0].shape[1]
    rows = dp * shard
    values = jnp.concatenate([part[...] for part in parts], axis=0)
    values = exact(order_ref[...], values).astype(jnp.bfloat16)
    copies = []
    for s in range(chips):
        out_ref[s] = values[s * rows : (s + 1) * rows]
        spot = pl.ds(pl.multiple_of((z ^ s) * cols, LANES), cols)
        copies.append(pltpu.make_async_copy(out_ref.at[s], out_hbm.at[:, spot], sems.at[s]))
        copies[-1].start()
    for copy in copies:
        copy.wait()


def shaped(shape, kind):
    return jax.ShapeDtypeStruct(shape, kind)


def run(kernel, outs, *args, cost=1, hbm=0, out_hbm=False, scratch=()):
    moved = sum(x.size * x.dtype.itemsize for x in (*args, *jax.tree.leaves(outs)))
    vmem = pl.BlockSpec(memory_space=pltpu.VMEM)
    args = [pltpu.with_memory_space_constraint(x, pltpu.HBM) if n < hbm else x for n, x in enumerate(args)]
    return pl.pallas_call(
        kernel,
        out_shape=outs,
        in_specs=[pl.BlockSpec(memory_space=pltpu.HBM)] * hbm + [vmem] * (len(args) - hbm),
        out_specs=jax.tree.map(lambda _: pl.BlockSpec(memory_space=pltpu.HBM) if out_hbm else vmem, outs),
        scratch_shapes=list(scratch),
        cost_estimate=pl.CostEstimate(flops=0, bytes_accessed=moved * cost, transcendentals=0),
        compiler_params=pltpu.CompilerParams(vmem_limit_bytes=VMEM_LIMIT),
    )(*args)


def aligned(
    hidden,
    logit_grad,
    predict_mask,
    slot_grads,
    slot_rows,
    slot_counts,
    master,
    first_moment,
    second_moment,
):
    vocab = lax.axis_size("vocab")
    dp = lax.axis_size("dp")
    chips = vocab // CORES
    rows = logit_grad.shape[1]
    shard = master.shape[0]
    cols = hidden.shape[1] * CORES
    owners, cap, width = slot_grads.shape[1:]
    group = cap * chips
    bf16, f32 = jnp.bfloat16, jnp.float32

    def send(x, s, away=0):
        move = s * CORES + away
        return lax.ppermute(x, "vocab", [(v, v ^ move) for v in range(vocab)]) if move else x

    def send_dp(x, t):
        return lax.ppermute(x, "dp", [(i, i ^ t) for i in range(dp)]) if t else x

    hidden_other = send(hidden, 0, 1)
    slots_in = (
        slot_grads[0].transpose(1, 0, 2).reshape(cap * owners, width),
        slot_rows.transpose(2, 0, 1),
        slot_counts,
    )
    slots_own, slots_other = run(
        functools.partial(slots_kernel, chips, dp),
        [shaped((group, width + LANES), bf16)] * CORES,
        *slots_in,
        hbm=3,
        scratch=[
            pltpu.VMEM((dp, cap * owners, width // dp), bf16),
            pltpu.VMEM(slots_in[1].shape, jnp.int32),
            pltpu.VMEM(slots_in[2].shape, jnp.int32),
            pltpu.SemaphoreType.DMA((2 + dp,)),
        ],
    )
    slots_other = send(slots_other, 0, 1)
    slots_other, hidden_other = lax.optimization_barrier((slots_other, hidden_other))
    quarter = width // dp
    packets = [shaped((vocab * cap * quarter // LANES + ID_ROWS, LANES), bf16)]
    quarters = run(functools.partial(peers_kernel, dp), packets * dp, slots_own, slots_other)
    held, head_order = run(
        functools.partial(fetch_kernel, chips, dp, shard),
        [shaped(hidden.shape, bf16), shaped((chips * rows, chips * rows), bf16)],
        hidden,
        hbm=1,
        scratch=[pltpu.SemaphoreType.DMA],
    )
    quarters = [send_dp(quarters[t], t) for t in reversed(range(dp))]
    quarters[-1], held = lax.optimization_barrier((quarters[-1], held))
    messages = run(functools.partial(owners_kernel, chips, cap, quarter), packets * chips, *quarters)
    columns = [logit_grad.T]
    for s in range(1, chips):
        columns.append(send(columns[s - 1], 1) if s % 2 else send(columns[0], s))
    head = run(
        functools.partial(head_kernel, chips * shard),
        [shaped((chips * shard, cols), f32)] * dp,
        predict_mask[None, :],
        head_order,
        held,
        hidden_other,
        *columns,
    )
    embed = run(
        functools.partial(embed_kernel, dp, shard, quarter),
        [shaped((2 * shard, quarter // 2), f32)] * dp,
        *[send(messages[s], s) for s in reversed(range(chips))],
    )
    sums = run(
        functools.partial(sum_kernel, chips, shard),
        [shaped((2 * shard, cols // 2), f32)] * chips,
        *[send_dp(head[t], t) for t in reversed(range(dp))],
    )
    pieces = [send(sums[s], s) for s in reversed(range(chips))]
    embed = run(gather_kernel, shaped((shard, width), f32), *[send_dp(embed[t], t) for t in range(dp)])
    state = (embed, master, first_moment, second_moment)
    table = run(rows_kernel, shaped((chips * shard, cols), bf16), *state, *pieces)
    master_new, first_new, second_new, order = run(
        functools.partial(adam_kernel, chips, dp, shard),
        [shaped(master.shape, f32)] * 3 + [shaped((chips * rows, chips * rows), bf16)],
        *state,
        *pieces,
    )
    table = run(
        functools.partial(table_kernel, chips, dp, shard),
        shaped((rows, width), bf16),
        order,
        *[send_dp(table, t) for t in reversed(range(dp))],
        out_hbm=True,
        scratch=[pltpu.VMEM((chips, rows, cols), bf16), pltpu.SemaphoreType.DMA((chips,))],
    )
    return (master_new, first_new, second_new, table)


def plain(
    hidden,
    logit_grad,
    predict_mask,
    slot_grads,
    slot_rows,
    slot_counts,
    master,
    first_moment,
    second_moment,
):
    vocab = lax.axis_size("vocab")
    dp = lax.axis_size("dp")
    chips = vocab // CORES
    rows = logit_grad.shape[1]
    shard = master.shape[0]
    cols = hidden.shape[1] * CORES
    owners, cap, width = slot_grads.shape[1:]
    here = lax.axis_index("vocab")
    core = here % CORES
    z = here // CORES
    d = lax.axis_index("dp")

    def to_core(x):
        return lax.ppermute(x, "vocab", [(v, v ^ 1) for v in range(vocab)])

    def to_chip(x, s):
        return lax.ppermute(x, "vocab", [(v, v ^ (s * CORES)) for v in range(vocab)])

    def to_dp(x, t):
        return lax.ppermute(x, "dp", [(i, i ^ t) for i in range(dp)])

    label = jnp.arange(rows, dtype=jnp.int32)
    source = ((label // shard) ^ d) * shard + label % shard
    reorder = (source[:, None] == label[None, :]).astype(jnp.bfloat16)
    masked = logit_grad * predict_mask.astype(jnp.bfloat16)[:, None]
    masked = lax.dot_general(reorder, masked, (((1,), (1,)), ((), ())), preferred_element_type=jnp.bfloat16)

    slot_index = jnp.arange(cap, dtype=jnp.int32)[None, :]
    ids = ((slot_rows[0] // shard) ^ d) * shard + slot_rows[0] % shard
    ids = jnp.where(slot_index < slot_counts[0][:, None], ids, -1).astype(jnp.bfloat16)
    ids = jnp.broadcast_to(ids[:, :, None, None], (owners, cap, chips, LANES))
    slots = slot_grads[0].reshape(owners, cap, chips, cols)
    slots = jnp.concatenate([slots, ids], axis=3).reshape(chips, CORES, cap, chips, cols + LANES)
    mine = lax.dynamic_index_in_dim(slots, core, 1, keepdims=False)
    other = lax.dynamic_index_in_dim(slots, 1 - core, 1, keepdims=False)
    hidden_other = to_core(hidden)
    other = to_core(other)
    masked = [masked] + [to_chip(masked, s) for s in range(1, chips)]
    both = jnp.stack([mine, other]).reshape(CORES * chips * cap, chips, cols + LANES)
    slots = [lax.dynamic_index_in_dim(both, z ^ s, 1, keepdims=False) for s in range(chips)]
    slots = [slots[0]] + [to_chip(slots[s], s) for s in range(1, chips)]

    swap = core == 1
    low = jnp.where(swap, hidden_other, hidden)
    high = jnp.where(swap, hidden, hidden_other)
    wide = jnp.concatenate([low, high], axis=1)
    slots = jnp.concatenate(slots, axis=0)
    owner = (jnp.arange(slots.shape[0], dtype=jnp.int32) // cap) % chips
    ids = slots[:, cols].astype(jnp.int32)
    ids = jnp.where(ids < 0, -1, (owner ^ z) * rows + ids)
    picked = (jnp.arange(chips * rows, dtype=jnp.int32)[:, None] == ids[None, :]).astype(jnp.bfloat16)
    part = jnp.dot(jnp.concatenate(masked, axis=0), wide, preferred_element_type=jnp.float32)
    part = part + jnp.dot(picked, slots[:, :cols], preferred_element_type=jnp.float32)
    part = part.reshape(chips, dp, shard, cols)
    part = [part[:, t].reshape(chips * shard, cols) for t in range(dp)]
    total = part[0]
    for t in range(1, dp):
        total = total + to_dp(part[t], t)
    total = total.reshape(chips, shard, CORES, cols // CORES).transpose(0, 2, 1, 3)
    total = total.reshape(chips, CORES * shard, cols // CORES)
    pieces = [total[0]] + [to_chip(total[s], s) for s in range(1, chips)]
    pieces = jnp.stack(pieces).reshape(chips, CORES, shard, cols // CORES).transpose(0, 2, 1, 3)
    pieces = pieces.reshape(chips, shard, cols)
    gradient = jnp.concatenate([lax.dynamic_index_in_dim(pieces, z ^ s, 0, keepdims=False) for s in range(chips)], axis=1)
    first_new = 0.9 * first_moment + 0.1 * gradient
    second_new = 0.95 * second_moment + 0.05 * gradient * gradient
    first_hat = first_new / (1.0 - 0.9**STEP)
    second_hat = second_new / (1.0 - 0.95**STEP)
    master_new = master - 0.05 * (first_hat / (jnp.sqrt(second_hat) + 1e-08) + 0.1 * master)
    table = master_new.astype(jnp.bfloat16)
    table = table.reshape(shard, chips, cols).transpose(1, 0, 2).reshape(chips * shard, cols)
    table = jnp.stack([table] + [to_dp(table, t) for t in range(1, dp)])
    table = jnp.stack([lax.dynamic_index_in_dim(table, d ^ t, 0, keepdims=False) for t in range(dp)])
    table = table.reshape(dp, chips, shard, cols).transpose(0, 2, 1, 3).reshape(rows, width)
    return (master_new, first_new, second_new, table)


def local(hidden, logit_grad, predict_mask, slot_grads, *rest):
    vocab = lax.axis_size("vocab")
    fits = hidden.shape[1] % LANES == 0 and logit_grad.shape[1] % 16 == 0
    slots = vocab * slot_grads.shape[2]
    fits = fits and slots % 16 == 0 and slots <= LANES and lax.axis_size("dp") == vocab // CORES
    fits = fits and slot_grads.shape[3] // lax.axis_size("dp") % (2 * LANES) == 0
    step = aligned if fits else plain
    return step(hidden, logit_grad, predict_mask, slot_grads, *rest)


def solution(mesh):
    in_specs = (
        P("dp", "vocab"),
        P("dp", "vocab"),
        P("dp"),
        P(("dp", "vocab"), None, None, None),
        P(("dp", "vocab"), None, None),
        P(("dp", "vocab"), None),
        P(("vocab", "dp"), None),
        P(("vocab", "dp"), None),
        P(("vocab", "dp"), None),
    )
    out_specs = (
        P(("vocab", "dp"), None),
        P(("vocab", "dp"), None),
        P(("vocab", "dp"), None),
        P("vocab", None),
    )
    return jax.shard_map(local, mesh=mesh, in_specs=in_specs, out_specs=out_specs, check_vma=False)
```

```python
import functools

import jax
import jax.numpy as jnp
from jax import lax
from jax.experimental import pallas as pl
from jax.experimental.pallas import tpu as pltpu
from jax.sharding import PartitionSpec as P

STEP = 8
CORES = 2
LANES = 128
ID_ROWS = 16
VMEM_LIMIT = 24 * 1024 * 1024


def place():
    here = lax.axis_index("vocab")
    return lax.axis_index("dp"), lax.shift_right_logical(here, 1), here & 1


def iota(shape, axis):
    return lax.broadcasted_iota(jnp.int32, shape, axis)


def over(x, n):
    return ((x.astype(jnp.float32) + 0.5) * (1.0 / n)).astype(jnp.int32)


def one_hot(flag):
    return jnp.where(flag, 1.0, 0.0).astype(jnp.bfloat16)


def exact(left, right):
    return jnp.dot(left, right, preferred_element_type=jnp.float32)


def slots_kernel(chips, dp, slots_hbm, rows_hbm, counts_hbm, own_out, other_out, slots_ref, rows_ref, counts_ref, sems):
    d, z, core = place()
    copies = [
        pltpu.make_async_copy(rows_hbm, rows_ref, sems.at[0]),
        pltpu.make_async_copy(counts_hbm, counts_ref, sems.at[1]),
        pltpu.make_async_copy(slots_hbm, slots_ref, sems.at[2]),
    ]
    for copy in copies:
        copy.start()
    cap, owners = rows_ref.shape[0], rows_ref.shape[2]
    count = cap * owners
    group = cap * chips
    part = slots_ref.shape[1] // dp
    q = iota((count, count), 0)
    away = jnp.where(q >= group, 1, 0)
    q = q - away * group
    s = over(q, cap)
    wanted = (q - s * cap) * owners + (s ^ z) * CORES + (away ^ core)
    pick = one_hot(iota((count, count), 1) == wanted)
    own_lane = iota((count, owners), 1) == iota((count, owners), 0) % owners
    for copy in copies[:2]:
        copy.wait()
    rows = jnp.broadcast_to(rows_ref[...], (cap, owners, owners)).reshape(count, owners)
    rows = jnp.sum(jnp.where(own_lane, rows, 0), axis=1, keepdims=True)
    live = jnp.broadcast_to(counts_ref[...], (count, owners))
    live = jnp.sum(jnp.where(own_lane, live, 0), axis=1, keepdims=True)
    ids = jnp.where(over(iota((count, 1), 0), owners) < live, rows, -1)
    ids = jnp.broadcast_to(ids, (count, LANES)).astype(jnp.bfloat16)
    ids = exact(pick, ids)
    copies[2].wait()
    outs = ((own_out, slice(0, group)), (other_out, slice(group, count)))
    for t in range(dp):
        values = exact(pick, slots_ref[:, pl.ds(pl.multiple_of((d ^ t) * part, LANES), part)])
        for out_ref, spot in outs:
            out_ref[:, t * part : (t + 1) * part] = values[spot].astype(jnp.bfloat16)
    for out_ref, spot in outs:
        out_ref[:, dp * part :] = ids[spot].astype(jnp.bfloat16)


def diagonal(values, axis):
    return jnp.sum(jnp.where(iota(values.shape, 0) == iota(values.shape, 1), values, 0.0), axis=axis, keepdims=True)


def packed(values, ids):
    ids = jnp.broadcast_to(ids, (ids.shape[0], LANES))
    ids = jnp.broadcast_to(diagonal(ids, 0), (ID_ROWS, LANES))
    blocks = [values[:, c : c + LANES] for c in range(0, values.shape[1], LANES)]
    return jnp.concatenate([*blocks, ids], axis=0).astype(jnp.bfloat16)


def unpacked(ref, cols):
    group = (ref.shape[0] - ID_ROWS) // (cols // LANES)
    row = ref[cols // LANES * group :, :].astype(jnp.float32)[:1]
    ids = diagonal(jnp.broadcast_to(row, (group, LANES)), 1)
    values = [ref[c * group : (c + 1) * group, :] for c in range(cols // LANES)]
    return jnp.concatenate(values, axis=1).astype(jnp.float32), ids


def peers_kernel(dp, own_ref, other_ref, *out_refs):
    part = (own_ref.shape[1] - LANES) // dp
    ids = [ref[:, dp * part :].astype(jnp.float32) for ref in (own_ref, other_ref)]
    ids = jnp.concatenate(ids, axis=0)[:, :1]
    for t, out_ref in enumerate(out_refs):
        values = [ref[:, t * part : (t + 1) * part].astype(jnp.float32) for ref in (own_ref, other_ref)]
        out_ref[...] = packed(jnp.concatenate(values, axis=0), ids)


def owners_kernel(chips, cap, cols, *refs):
    in_refs, out_refs = refs[:-chips], refs[-chips:]
    held = [unpacked(ref, cols) for ref in in_refs]
    group = cap * chips
    for s, out_ref in enumerate(out_refs):
        spots = [slice(core * group + s * cap, core * group + (s + 1) * cap) for core in range(CORES)]
        rows = [[block[spot] for block in both for spot in spots] for both in zip(*held)]
        values, ids = [jnp.concatenate(blocks, axis=0) for blocks in rows]
        out_ref[...] = packed(values, ids)


def fetch_kernel(hidden_hbm, hidden_ref, sem):
    copy = pltpu.make_async_copy(hidden_hbm, hidden_ref, sem)
    copy.start()
    copy.wait()


def head_kernel(chips, dp, shard, mask_ref, own_ref, other_ref, *refs):
    d, z, core = place()
    parts, outs = refs[:chips], refs[chips:]
    rows = dp * shard
    total = chips * rows
    cols = own_ref.shape[1]
    size = chips * shard
    r = iota((total, total), 0)
    t = over(r, size)
    s = over(r - t * size, shard)
    i = r - t * size - s * shard
    order = one_hot(iota((total, total), 1) == s * rows + (t ^ d) * shard + i)
    mask = mask_ref[...].astype(jnp.float32).astype(jnp.bfloat16)
    columns = jnp.concatenate([part[...] for part in parts], axis=0) * mask
    columns = exact(order, columns).astype(jnp.bfloat16)
    for at, ref in ((core, own_ref), (1 - core, other_ref)):
        head = exact(columns, ref[...])
        spot = pl.ds(pl.multiple_of(at * cols, LANES), cols)
        for t, out_ref in enumerate(outs):
            out_ref[:, spot] = head[t * size : (t + 1) * size]


def stacked(rows):
    cut = rows.shape[1] // 2
    return jnp.concatenate([rows[:, :cut], rows[:, cut:]], axis=0)


def unstacked(rows):
    cut = rows.shape[0] // 2
    return jnp.concatenate([rows[:cut], rows[cut:]], axis=1)


def embed_kernel(dp, shard, cols, *refs):
    d, z, core = place()
    slot_refs, out_refs = refs[:-dp], refs[-dp:]
    held = [unpacked(ref, cols) for ref in slot_refs]
    values, ids = [jnp.concatenate(blocks, axis=0) for blocks in zip(*held)]
    values, ids = values.astype(jnp.bfloat16), ids.astype(jnp.int32)
    count = values.shape[0]
    block = over(jnp.maximum(ids, 0), shard)
    target = jnp.where(ids < 0, -1, (block ^ d) * shard + ids - block * shard)
    picked = one_hot(iota((count, dp * shard), 1) == target)
    embed = lax.dot_general(picked, values, (((0,), (0,)), ((), ())), preferred_element_type=jnp.float32)
    for t, out_ref in enumerate(out_refs):
        out_ref[...] = stacked(embed[t * shard : (t + 1) * shard])


def gather_kernel(dp, members, *refs):
    d, z, core = place()
    parts, pieces, out_ref = refs[:dp], refs[dp:-1], refs[-1]
    cols = out_ref.shape[1] // dp
    for t, part in enumerate(parts):
        out_ref[:, pl.ds(pl.multiple_of((d ^ t) * cols, LANES), cols)] = unstacked(part[...])
    for s, piece in zip(members, pieces):
        spot = chip_spot(z, s, piece)
        out_ref[:, spot] += unstacked(piece[...])


def sum_kernel(chips, shard, *refs):
    dp = len(refs) - chips
    total = refs[0][...]
    for t in range(1, dp):
        total = total + refs[t][...]
    for s, out_ref in enumerate(refs[dp:]):
        out_ref[...] = stacked(total[s * shard : (s + 1) * shard])


def step(spot, gradient, master_ref, first_ref, second_ref):
    master = master_ref[:, spot]
    first_new = 0.9 * first_ref[:, spot] + 0.1 * gradient
    second_new = 0.95 * second_ref[:, spot] + 0.05 * gradient * gradient
    first_hat = first_new / (1.0 - 0.9**STEP)
    second_hat = second_new / (1.0 - 0.95**STEP)
    master_new = master - 0.05 * (first_hat / (jnp.sqrt(second_hat) + 1e-08) + 0.1 * master)
    return master_new, first_new, second_new


def chip_spot(z, s, piece_ref):
    cols = piece_ref.shape[1] * 2
    return pl.ds(pl.multiple_of((z ^ s) * cols, LANES), cols)


def gradients(chips, cols, gradient_ref, pieces):
    d, z, core = place()
    for s in range(chips):
        spot = pl.ds(pl.multiple_of((z ^ s) * cols, LANES), cols)
        gradient = gradient_ref[:, spot]
        yield spot, gradient + unstacked(pieces[s][...]) if s < len(pieces) else gradient


def rows_kernel(chips, *refs):
    (gradient_ref, *state), pieces, out_ref = refs[:4], refs[4:-1], refs[-1]
    cols = out_ref.shape[1]
    table = [step(spot, gradient, *state)[0] for spot, gradient in gradients(chips, cols, gradient_ref, pieces)]
    out_ref[...] = jnp.concatenate(table, axis=0).astype(jnp.bfloat16)


def adam_kernel(chips, dp, shard, *refs):
    d, z, core = place()
    (gradient_ref, *state), pieces, outs, order_ref = refs[:4], refs[4:-4], refs[-4:-1], refs[-1]
    rows = dp * shard
    total = chips * rows
    r = iota((total, total), 0)
    s = over(r, rows)
    e = over(r - s * rows, shard)
    i = r - s * rows - e * shard
    order_ref[...] = one_hot(iota((total, total), 1) == ((e ^ d) * chips + s) * shard + i)
    cols = gradient_ref.shape[1] // chips
    for spot, gradient in gradients(chips, cols, gradient_ref, pieces):
        for out_ref, value in zip(outs, step(spot, gradient, *state)):
            out_ref[:, spot] = value


def table_kernel(chips, dp, shard, order_ref, *refs):
    d, z, core = place()
    parts, (out_hbm, out_ref, sems) = refs[-4::-1], refs[-3:]
    cols = parts[0].shape[1]
    rows = dp * shard
    values = jnp.concatenate([part[...] for part in parts], axis=0)
    values = exact(order_ref[...], values).astype(jnp.bfloat16)
    copies = []
    for s in range(chips):
        out_ref[s] = values[s * rows : (s + 1) * rows]
        spot = pl.ds(pl.multiple_of((z ^ s) * cols, LANES), cols)
        copies.append(pltpu.make_async_copy(out_ref.at[s], out_hbm.at[:, spot], sems.at[s]))
        copies[-1].start()
    for copy in copies:
        copy.wait()


def shaped(shape, kind):
    return jax.ShapeDtypeStruct(shape, kind)


def run(kernel, outs, *args, cost=1, hbm=0, out_hbm=False, scratch=()):
    moved = sum(x.size * x.dtype.itemsize for x in (*args, *jax.tree.leaves(outs)))
    vmem = pl.BlockSpec(memory_space=pltpu.VMEM)
    args = [pltpu.with_memory_space_constraint(x, pltpu.HBM) if n < hbm else x for n, x in enumerate(args)]
    return pl.pallas_call(
        kernel,
        out_shape=outs,
        in_specs=[pl.BlockSpec(memory_space=pltpu.HBM)] * hbm + [vmem] * (len(args) - hbm),
        out_specs=jax.tree.map(lambda _: pl.BlockSpec(memory_space=pltpu.HBM) if out_hbm else vmem, outs),
        scratch_shapes=list(scratch),
        cost_estimate=pl.CostEstimate(flops=0, bytes_accessed=moved * cost, transcendentals=0),
        compiler_params=pltpu.CompilerParams(vmem_limit_bytes=VMEM_LIMIT),
    )(*args)


def local_copies(*args):
    return [pltpu.VMEM(x.shape, x.dtype) for x in args] + [pltpu.SemaphoreType.DMA((len(args),))]


def aligned(
    hidden,
    logit_grad,
    predict_mask,
    slot_grads,
    slot_rows,
    slot_counts,
    master,
    first_moment,
    second_moment,
):
    vocab = lax.axis_size("vocab")
    dp = lax.axis_size("dp")
    chips = vocab // CORES
    rows = logit_grad.shape[1]
    shard = master.shape[0]
    cols = hidden.shape[1] * CORES
    owners, cap, width = slot_grads.shape[1:]
    group = cap * chips
    bf16, f32 = jnp.bfloat16, jnp.float32

    def send(x, s, away=0):
        move = s * CORES + away
        return lax.ppermute(x, "vocab", [(v, v ^ move) for v in range(vocab)]) if move else x

    def send_dp(x, t):
        return lax.ppermute(x, "dp", [(i, i ^ t) for i in range(dp)]) if t else x

    hidden_other = send(hidden, 0, 1)
    slots_in = (
        slot_grads[0].transpose(1, 0, 2).reshape(cap * owners, width),
        slot_rows.transpose(2, 0, 1),
        slot_counts,
    )
    slots_own, slots_other = run(
        functools.partial(slots_kernel, chips, dp),
        [shaped((group, width + LANES), bf16)] * CORES,
        *slots_in,
        hbm=3,
        scratch=local_copies(*slots_in),
    )
    slots_other = send(slots_other, 0, 1)
    slots_other, hidden_other = lax.optimization_barrier((slots_other, hidden_other))
    quarter = width // dp
    packets = [shaped((vocab * cap * quarter // LANES + ID_ROWS, LANES), bf16)]
    quarters = run(functools.partial(peers_kernel, dp), packets * dp, slots_own, slots_other)
    held = run(fetch_kernel, shaped(hidden.shape, bf16), hidden, hbm=1, scratch=[pltpu.SemaphoreType.DMA])
    quarters = [send_dp(quarters[t], t) for t in reversed(range(dp))]
    quarters[-1], held = lax.optimization_barrier((quarters[-1], held))
    messages = run(functools.partial(owners_kernel, chips, cap, quarter), packets * chips, *quarters)
    columns = [logit_grad.T]
    for s in range(1, chips):
        columns.append(send(columns[s - 1], 1) if s % 2 else send(columns[0], s))
    held, _ = lax.optimization_barrier((held, messages[0]))
    head = run(
        functools.partial(head_kernel, chips, dp, shard),
        [shaped((chips * shard, cols), f32)] * dp,
        predict_mask[None, :],
        held,
        hidden_other,
        *columns,
    )
    embed = run(
        functools.partial(embed_kernel, dp, shard, quarter),
        [shaped((2 * shard, quarter // 2), f32)] * dp,
        *[send(messages[s], s) for s in reversed(range(chips))],
    )
    sums = run(
        functools.partial(sum_kernel, chips, shard),
        [shaped((2 * shard, cols // 2), f32)] * chips,
        *[send_dp(head[t], t) for t in reversed(range(dp))],
    )
    half = chips // 2
    pieces = [send(sums[s], s) for s in reversed(range(chips))][::-1]
    embed = [send_dp(embed[t], t) for t in range(dp)]
    gradient = run(
        functools.partial(gather_kernel, dp, reversed(range(half, chips))),
        shaped((shard, width), f32),
        *embed,
        *pieces[:half - 1 : -1],
    )
    state = (gradient, master, first_moment, second_moment)
    pieces = pieces[:half]
    table = run(functools.partial(rows_kernel, chips), shaped((chips * shard, cols), bf16), *state, *pieces)
    master_new, first_new, second_new, order = run(
        functools.partial(adam_kernel, chips, dp, shard),
        [shaped(master.shape, f32)] * 3 + [shaped((chips * rows, chips * rows), bf16)],
        *state,
        *pieces,
    )
    table = run(
        functools.partial(table_kernel, chips, dp, shard),
        shaped((rows, width), bf16),
        order,
        *[send_dp(table, t) for t in reversed(range(dp))],
        out_hbm=True,
        scratch=[pltpu.VMEM((chips, rows, cols), bf16), pltpu.SemaphoreType.DMA((chips,))],
    )
    return (master_new, first_new, second_new, table)


def plain(
    hidden,
    logit_grad,
    predict_mask,
    slot_grads,
    slot_rows,
    slot_counts,
    master,
    first_moment,
    second_moment,
):
    vocab = lax.axis_size("vocab")
    dp = lax.axis_size("dp")
    chips = vocab // CORES
    rows = logit_grad.shape[1]
    shard = master.shape[0]
    cols = hidden.shape[1] * CORES
    owners, cap, width = slot_grads.shape[1:]
    here = lax.axis_index("vocab")
    core = here % CORES
    z = here // CORES
    d = lax.axis_index("dp")

    def to_core(x):
        return lax.ppermute(x, "vocab", [(v, v ^ 1) for v in range(vocab)])

    def to_chip(x, s):
        return lax.ppermute(x, "vocab", [(v, v ^ (s * CORES)) for v in range(vocab)])

    def to_dp(x, t):
        return lax.ppermute(x, "dp", [(i, i ^ t) for i in range(dp)])

    label = jnp.arange(rows, dtype=jnp.int32)
    source = ((label // shard) ^ d) * shard + label % shard
    reorder = (source[:, None] == label[None, :]).astype(jnp.bfloat16)
    masked = logit_grad * predict_mask.astype(jnp.bfloat16)[:, None]
    masked = lax.dot_general(reorder, masked, (((1,), (1,)), ((), ())), preferred_element_type=jnp.bfloat16)

    slot_index = jnp.arange(cap, dtype=jnp.int32)[None, :]
    ids = ((slot_rows[0] // shard) ^ d) * shard + slot_rows[0] % shard
    ids = jnp.where(slot_index < slot_counts[0][:, None], ids, -1).astype(jnp.bfloat16)
    ids = jnp.broadcast_to(ids[:, :, None, None], (owners, cap, chips, LANES))
    slots = slot_grads[0].reshape(owners, cap, chips, cols)
    slots = jnp.concatenate([slots, ids], axis=3).reshape(chips, CORES, cap, chips, cols + LANES)
    mine = lax.dynamic_index_in_dim(slots, core, 1, keepdims=False)
    other = lax.dynamic_index_in_dim(slots, 1 - core, 1, keepdims=False)
    hidden_other = to_core(hidden)
    other = to_core(other)
    masked = [masked] + [to_chip(masked, s) for s in range(1, chips)]
    both = jnp.stack([mine, other]).reshape(CORES * chips * cap, chips, cols + LANES)
    slots = [lax.dynamic_index_in_dim(both, z ^ s, 1, keepdims=False) for s in range(chips)]
    slots = [slots[0]] + [to_chip(slots[s], s) for s in range(1, chips)]

    swap = core == 1
    low = jnp.where(swap, hidden_other, hidden)
    high = jnp.where(swap, hidden, hidden_other)
    wide = jnp.concatenate([low, high], axis=1)
    slots = jnp.concatenate(slots, axis=0)
    owner = (jnp.arange(slots.shape[0], dtype=jnp.int32) // cap) % chips
    ids = slots[:, cols].astype(jnp.int32)
    ids = jnp.where(ids < 0, -1, (owner ^ z) * rows + ids)
    picked = (jnp.arange(chips * rows, dtype=jnp.int32)[:, None] == ids[None, :]).astype(jnp.bfloat16)
    part = jnp.dot(jnp.concatenate(masked, axis=0), wide, preferred_element_type=jnp.float32)
    part = part + jnp.dot(picked, slots[:, :cols], preferred_element_type=jnp.float32)
    part = part.reshape(chips, dp, shard, cols)
    part = [part[:, t].reshape(chips * shard, cols) for t in range(dp)]
    total = part[0]
    for t in range(1, dp):
        total = total + to_dp(part[t], t)
    total = total.reshape(chips, shard, CORES, cols // CORES).transpose(0, 2, 1, 3)
    total = total.reshape(chips, CORES * shard, cols // CORES)
    pieces = [total[0]] + [to_chip(total[s], s) for s in range(1, chips)]
    pieces = jnp.stack(pieces).reshape(chips, CORES, shard, cols // CORES).transpose(0, 2, 1, 3)
    pieces = pieces.reshape(chips, shard, cols)
    gradient = jnp.concatenate([lax.dynamic_index_in_dim(pieces, z ^ s, 0, keepdims=False) for s in range(chips)], axis=1)
    first_new = 0.9 * first_moment + 0.1 * gradient
    second_new = 0.95 * second_moment + 0.05 * gradient * gradient
    first_hat = first_new / (1.0 - 0.9**STEP)
    second_hat = second_new / (1.0 - 0.95**STEP)
    master_new = master - 0.05 * (first_hat / (jnp.sqrt(second_hat) + 1e-08) + 0.1 * master)
    table = master_new.astype(jnp.bfloat16)
    table = table.reshape(shard, chips, cols).transpose(1, 0, 2).reshape(chips * shard, cols)
    table = jnp.stack([table] + [to_dp(table, t) for t in range(1, dp)])
    table = jnp.stack([lax.dynamic_index_in_dim(table, d ^ t, 0, keepdims=False) for t in range(dp)])
    table = table.reshape(dp, chips, shard, cols).transpose(0, 2, 1, 3).reshape(rows, width)
    return (master_new, first_new, second_new, table)


def local(hidden, logit_grad, predict_mask, slot_grads, *rest):
    vocab = lax.axis_size("vocab")
    fits = hidden.shape[1] % LANES == 0 and logit_grad.shape[1] % 16 == 0
    slots = vocab * slot_grads.shape[2]
    fits = fits and slots % 16 == 0 and slots <= LANES and lax.axis_size("dp") == vocab // CORES
    fits = fits and slot_grads.shape[3] // lax.axis_size("dp") % (2 * LANES) == 0
    step = aligned if fits else plain
    return step(hidden, logit_grad, predict_mask, slot_grads, *rest)


def solution(mesh):
    in_specs = (
        P("dp", "vocab"),
        P("dp", "vocab"),
        P("dp"),
        P(("dp", "vocab"), None, None, None),
        P(("dp", "vocab"), None, None),
        P(("dp", "vocab"), None),
        P(("vocab", "dp"), None),
        P(("vocab", "dp"), None),
        P(("vocab", "dp"), None),
    )
    out_specs = (
        P(("vocab", "dp"), None),
        P(("vocab", "dp"), None),
        P(("vocab", "dp"), None),
        P("vocab", None),
    )
    return jax.shard_map(local, mesh=mesh, in_specs=in_specs, out_specs=out_specs, check_vma=False)
```
